32 devices in a mesh: groups: 2 (over y), pool: 4 (over z), tensor: 4 (over x, core).
Axes of the slice: x: 2, y: 2, z: 4, core: 2. Of those that a mesh axis runs over, the one named last changes fastest.
Arguments:
- hidden_in: bfloat16 [128, 16384], P('groups', 'pool'), parts along dimension 0, may hold values from -750 to 750
- norm_gain: bfloat16 [16384], P('pool'), may hold values from 0.099609375 to 1.8984375
- w_query: bfloat16 [16384, 16384], P('pool', 'tensor'), may hold values from -0.046875 to 0.046875
- w_key: bfloat16 [16384, 1024], P('pool', 'tensor'), may hold values from -0.046875 to 0.046875
- w_value: bfloat16 [16384, 1024], P('pool', 'tensor'), may hold values from -0.046875 to 0.046875
- cache_keys: bfloat16 [8192, 1024], P(('groups', 'pool'), 'tensor'), parts along dimension 0, may hold values from -110 to 110
- cache_values: bfloat16 [8192, 1024], P(('groups', 'pool'), 'tensor'), parts along dimension 0, may hold values from -6 to 6
- send_row: int32 [8, 4, 4], P('groups'), parts along dimension 0, may hold values from -1 to 15, as said below
- piece_len: int32 [8, 4, 4], P(('groups', 'pool')), parts along dimension 0, may hold values from 0 to 64, as said below
- row_len: int32 [128], P('groups'), parts along dimension 0, may hold values from 1 to 64, as said below
Outputs:
- attention: bfloat16 [128, 16384], P(('groups', 'pool'), 'tensor'), parts along dimension 0
The draws below stay inside these ranges and needn't reach their ends.
There are 2 independent parts, one for each index of `groups`. The reference program is written for one: setup_inputs(seed, part) draws one part's arguments, and reference() takes and returns one part's arrays. A program takes and returns all parts, laid end to end along the dimension named above; an argument that names none is the same for every part. Nothing has to cross between parts.
Inputs may be any that keep to these rules, and one draw needn't show every extreme that they name: `send_row`: each entry is -1 or a row of 0 to 15; every row of every home is named at least once; entry [h, p, c] is live exactly when piece_len[p, h, c] > 0. `piece_len`: 0 exactly at empty slots. `row_len`: the sum of piece_len over the slots that name the row.
All inputs are finite; a program needn't handle non-finite values.
Results may differ from the reference program's by a relative error of at most 0.012.
Values may be sent and summed in bfloat16 or wider, within the bound.
No kernel may reach another device: no remote copies, remote signals or barrier semaphores. Data moves between devices by JAX's collectives and lax.ppermute only.
A program may use at most 128 MiB of HBM per device.

```python
import jax
import jax.numpy as jnp
from jax import lax

D = 16384
QH = 128
KVH = 8
HD = 128
ROWS_DEV = 16
SEG = 64
SLOTS = 4
ROWS = 64
CACHE = 4096
N_POOL = 4


def route_plan(key):
    live_key, row_key, length_key = jax.random.split(key, 3)
    array_shape = (N_POOL, N_POOL, SLOTS)
    home_index = lax.broadcasted_iota(jnp.int32, array_shape, 0)
    owner_index = lax.broadcasted_iota(jnp.int32, array_shape, 1)
    slot_index = lax.broadcasted_iota(jnp.int32, array_shape, 2)
    forced_row = (owner_index - home_index) % N_POOL + slot_index * N_POOL
    forced = forced_row < ROWS_DEV
    heavy_home = home_index == 0
    is_live = (jax.random.randint(live_key, array_shape, 0, 2) == 1) | forced | heavy_home
    free_row = jnp.where(heavy_home, 0, jax.random.randint(row_key, array_shape, 0, ROWS_DEV))
    chosen = jnp.where(forced, forced_row, free_row)
    lengths = jax.random.randint(length_key, array_shape, 1, SEG + 1)
    lengths = jnp.where((home_index == owner_index) & (slot_index == 0), SEG, lengths)
    lengths = jnp.where(heavy_home & (chosen == 0), SEG, lengths)
    lengths = jnp.where(is_live, lengths, 0)
    sends = jnp.where(is_live, chosen, -1)
    return (sends.astype(jnp.int32), lengths.astype(jnp.int32))


def draw_send_row(key, part):
    sends, lengths = route_plan(key)
    return sends


def draw_piece_len(key, part):
    sends, lengths = route_plan(key)
    return jnp.transpose(lengths, (1, 0, 2))


def draw_row_len(key, part):
    sends, lengths = route_plan(key)
    matches = sends[..., None] == jnp.arange(ROWS_DEV, dtype=jnp.int32)
    counted = jnp.sum(jnp.where(matches, lengths[..., None], 0), axis=(1, 2))
    return counted.reshape(ROWS).astype(jnp.int32)


def draw_hidden_in(key, part):
    key = jax.random.fold_in(key, 11)
    sample_key, column_key, row_key = jax.random.split(key, 3)
    position = jnp.arange(D, dtype=jnp.float32) / D
    rough = jnp.exp(jax.random.uniform(column_key, (D,), jnp.float32, 0.0, jnp.log(4.0)))
    sample = jnp.clip(jax.random.normal(sample_key, (ROWS, D), jnp.float32), -6.0, 6.0)
    column = jnp.exp(position * jnp.log(3.0)) * rough
    row_scale = jnp.exp(jax.random.uniform(row_key, (ROWS, 1), jnp.float32, 0.0, jnp.log(10.0)))
    return (sample * column[None, :] * row_scale).astype(jnp.bfloat16)


def draw_cache_keys(key, part):
    key = jax.random.fold_in(key, 23)
    sample_key = jax.random.fold_in(key, 0)
    array_shape = (CACHE, KVH * HD)
    result = jnp.clip(jax.random.normal(sample_key, array_shape, jnp.float32), -6.0, 6.0)
    return result.astype(jnp.bfloat16)


def block_levels(stream_key, extent, shards, smallest, high):
    def one(axis_at, shards_of):
        steps = jax.random.uniform(jax.random.fold_in(jax.random.fold_in(stream_key, 6), axis_at), (shards_of,), jnp.float32, smallest / len(shards), high / len(shards))
        return jnp.repeat(jnp.exp(steps), extent[axis_at] // shards_of).reshape((-1,) + (1,) * (len(extent) - axis_at - 1))

    factor_of = one(*shards[0])
    for cut in shards[1:]:
        factor_of = factor_of * one(*cut)
    return factor_of


def noise(own_key, shape, spread, limit, pieces=(), kind=jnp.bfloat16):
    entries = spread * jax.random.normal(own_key, shape, jnp.float32)
    if pieces:
        entries = entries * block_levels(own_key, shape, pieces, -0.22, 0.18)
    return jnp.clip(entries, -limit, limit).astype(kind)


def setup_inputs(seed: int = 0, part: int = 0) -> dict:
    seeds = jax.random.split(jax.random.key(seed), 11)
    own_keys = jax.random.split(jax.random.fold_in(seeds[10], part), 11)
    return {
        "hidden_in": draw_hidden_in(jax.random.fold_in(jax.random.fold_in(seeds[10], part), 71), part),
        "norm_gain": jnp.clip(1.0 + 0.18 * jax.random.normal(seeds[1], (D,), jnp.float32), 0.099609375, 1.8984375).astype(jnp.bfloat16),
        "w_query": noise(seeds[2], (D, QH * HD), D ** -0.5, 0.046875, ((0, 4), (1, 4))),
        "w_key": noise(seeds[3], (D, KVH * HD), D ** -0.5, 0.046875, ((0, 4), (1, 4))),
        "w_value": noise(seeds[4], (D, KVH * HD), D ** -0.5, 0.046875, ((0, 4), (1, 4))),
        "cache_keys": draw_cache_keys(jax.random.fold_in(jax.random.fold_in(seeds[10], part), 71), part),
        "cache_values": noise(own_keys[6], (CACHE, KVH * HD), 1.0, 6.0, ((0, 4), (1, 4))),
        "send_row": draw_send_row(jax.random.fold_in(jax.random.fold_in(seeds[10], part), 71), part),
        "piece_len": draw_piece_len(jax.random.fold_in(jax.random.fold_in(seeds[10], part), 71), part),
        "row_len": draw_row_len(jax.random.fold_in(jax.random.fold_in(seeds[10], part), 71), part),
    }


EPS = 1e-05
THETA = 500000.0

def rotate(vectors, positions):
    head_size = vectors.shape[-1]
    half_dim = head_size // 2
    inverse_freq = THETA ** (-(jnp.arange(half_dim, dtype=jnp.float32) * 2.0) / head_size)
    angles = positions.astype(jnp.float32)[:, None] * inverse_freq[None, :]
    cosines = jnp.cos(angles)[:, None, :]
    sines = jnp.sin(angles)[:, None, :]
    front_half = vectors[..., :half_dim]
    back_half = vectors[..., half_dim:]
    return jnp.concatenate([front_half * cosines - back_half * sines, back_half * cosines + front_half * sines], -1)

def partial_attention(queries, key_block, value_block, lengths):
    score = jnp.einsum('rkgd,rtkd->rkgt', queries.astype(jnp.float32), key_block.astype(jnp.float32)) * HD ** (-0.5)
    usable = (jnp.arange(key_block.shape[1], dtype=jnp.int32)[None, :] < lengths[:, None])[:, None, None, :]
    peak_score = lax.optimization_barrier(jnp.max(jnp.where(usable, score, -1e+30), axis=-1))
    weight = jnp.where(usable, jnp.exp(score - peak_score[..., None]), 0.0)
    totals = lax.optimization_barrier(jnp.sum(weight, axis=-1))
    blended = jnp.einsum('rkgt,rtkd->rkgd', weight.astype(jnp.bfloat16).astype(jnp.float32), value_block.astype(jnp.float32))
    slot_total = queries.shape[0]
    return (blended.reshape(slot_total, -1), peak_score.reshape(slot_total, -1), totals.reshape(slot_total, -1))

def combine(slot_rows, blended, peaks, totals, self_peak, self_value):
    row_local = self_peak.shape[0]
    matches = slot_rows[None, :] == jnp.arange(row_local, dtype=jnp.int32)[:, None]
    highest = jnp.maximum(self_peak, lax.optimization_barrier(jnp.max(jnp.where(matches[:, :, None], peaks[None], -1e+30), axis=1)))
    factor = jnp.where(matches[:, :, None], jnp.exp(peaks[None] - highest[:, None, :]), 0.0)
    self_weight = jnp.exp(self_peak - highest)
    denominator = self_weight + lax.optimization_barrier(jnp.sum(factor * totals[None], axis=1))
    numerator = self_weight[..., None] * self_value + jnp.einsum('jsh,shd->jhd', factor, blended)
    return (numerator / denominator[..., None]).astype(jnp.bfloat16).reshape(row_local, -1)

def reference(hidden_in, norm_gain, w_query, w_key, w_value, cache_keys, cache_values, send_row, piece_len, row_len):
    row_count = hidden_in.shape[0]
    pool_size = send_row.shape[0]
    slot_count = send_row.shape[2]
    group = QH // KVH
    x_float = hidden_in.astype(jnp.float32)
    power = lax.optimization_barrier(jnp.mean(x_float * x_float, axis=1, keepdims=True))
    factor_row = lax.rsqrt(power + EPS)
    scaled = (x_float * norm_gain.astype(jnp.float32)).astype(jnp.bfloat16)
    query = (jnp.dot(scaled, w_query, preferred_element_type=jnp.float32) * factor_row).reshape(row_count, QH, HD)
    key_new = (jnp.dot(scaled, w_key, preferred_element_type=jnp.float32) * factor_row).reshape(row_count, KVH, HD)
    value_b = (jnp.dot(scaled, w_value, preferred_element_type=jnp.float32) * factor_row).astype(jnp.bfloat16).reshape(row_count, KVH, HD)
    query_b = rotate(query, row_len).astype(jnp.bfloat16)
    key_b = rotate(key_new, row_len).astype(jnp.bfloat16)
    grouped = query_b.reshape(row_count, KVH, group, HD).astype(jnp.float32)
    self_peak = (jnp.einsum('rkgd,rkd->rkg', grouped, key_b.astype(jnp.float32)) * HD ** (-0.5)).reshape(row_count, QH)
    self_value = jnp.repeat(value_b.astype(jnp.float32), group, axis=1)
    key_pages = cache_keys.reshape(pool_size, pool_size * slot_count, SEG, KVH, HD)
    value_pages = cache_values.reshape(pool_size, pool_size * slot_count, SEG, KVH, HD)
    lengths = piece_len.reshape(pool_size, pool_size * slot_count)
    global_rows = jnp.arange(pool_size, dtype=jnp.int32)[:, None, None] * ROWS_DEV + jnp.maximum(send_row, 0)
    owner_rows = jnp.transpose(global_rows, (1, 0, 2)).reshape(pool_size, pool_size * slot_count)

    def owner_part(inputs):
        key_block, value_block, owner_lengths, row_index = inputs
        chosen = query_b[row_index].reshape(-1, KVH, group, HD)
        return partial_attention(chosen, key_block, value_block, owner_lengths)
    blended, peaks, totals = lax.map(owner_part, (key_pages, value_pages, lengths, owner_rows))
    blended = jnp.transpose(blended.reshape(pool_size, pool_size, slot_count, QH * HD), (1, 0, 2, 3)).reshape(pool_size, pool_size * slot_count, QH, HD)
    peaks = jnp.transpose(peaks.reshape(pool_size, pool_size, slot_count, QH), (1, 0, 2, 3)).reshape(pool_size, pool_size * slot_count, QH)
    totals = jnp.transpose(totals.reshape(pool_size, pool_size, slot_count, QH), (1, 0, 2, 3)).reshape(pool_size, pool_size * slot_count, QH)
    slot_rows = send_row.reshape(pool_size, pool_size * slot_count)
    merged = jax.vmap(combine)(slot_rows, blended, peaks, totals, self_peak.reshape(pool_size, ROWS_DEV, QH), self_value.reshape(pool_size, ROWS_DEV, QH, HD))
    return merged.reshape(row_count, QH * HD)
```

```python
import functools

import jax
import jax.numpy as jnp
import numpy as np
from jax import lax
from jax.experimental import pallas as pl
from jax.experimental.pallas import tpu as pltpu
from jax.sharding import PartitionSpec as P

HD = 128
EPS = 1e-05
THETA = 500000.0
LOW = -1e30
WINDOW = 6


def divides(width, limit):
    while width % limit:
        limit //= 2
    return limit


def split3(x):
    a = x.astype(jnp.bfloat16).astype(jnp.float32)
    r = x - a
    b = r.astype(jnp.bfloat16).astype(jnp.float32)
    return a, b, (r - b).astype(jnp.bfloat16).astype(jnp.float32)


def project_kernel(pool, slots, rows_local, meta, row_len, hidden, gain, *rest):
    n_w = 3
    weights, rest = rest[:n_w], rest[n_w:]
    outs, rest = rest[:pool], rest[pool:]
    pos_out, x_buf, g_buf, pick, lhs, *bufs, in_sem, sems = rest
    per = pool * slots
    n_slots = pool * per
    tiles = []
    for n, (w, buf) in enumerate(zip(weights, bufs)):
        width = buf.shape[2]
        for t in range(buf.shape[0]):
            tiles.append((n, t, width))

    def copy(i):
        n, t, width = tiles[i]
        return pltpu.make_async_copy(
            weights[n].at[:, t * width : (t + 1) * width], bufs[n].at[t], sems.at[i]
        )

    x_copy = pltpu.make_async_copy(hidden, x_buf, in_sem.at[0])
    g_copy = pltpu.make_async_copy(gain, g_buf, in_sem.at[1])
    x_copy.start()
    g_copy.start()
    for i in range(min(WINDOW, len(tiles))):
        copy(i).start()

    me = meta[0]
    n_rows = x_buf.shape[0]
    lane = lax.broadcasted_iota(jnp.int32, (1, n_rows), 1)

    def slot_row(k, j, c):
        owner = lax.rem(me + k, pool)
        home = lax.rem(owner + j, pool)
        r = meta[1 + home * per + owner * slots + c]
        return jnp.where(r >= 0, home * rows_local + r, -1)

    def fill(i, carry):
        k, s = i // per, lax.rem(i, per)
        row = slot_row(k, s // slots, lax.rem(s, slots))
        pick[pl.ds(i, 1), :] = (lane == row).astype(jnp.float32)
        return carry

    lax.fori_loop(0, n_slots, fill, 0)

    def fill_pos(s, carry):
        row = slot_row(0, s // slots, lax.rem(s, slots))
        at = row_len[jnp.maximum(row, 0)].astype(jnp.float32)
        pos_out[pl.ds(s, 1), :] = jnp.full((1, HD), at, jnp.float32)
        return carry

    lax.fori_loop(0, per, fill_pos, 0)

    x_copy.wait()
    g_copy.wait()
    x = x_buf[...].astype(jnp.float32)
    power = jnp.sum(x * x, axis=1, keepdims=True)
    scaled = (x * g_buf[...].astype(jnp.float32)).astype(jnp.bfloat16)
    chosen = pick[...].astype(jnp.bfloat16)
    lhs[...] = jnp.dot(chosen, scaled, preferred_element_type=jnp.float32).astype(jnp.bfloat16)
    at = lax.broadcasted_iota(jnp.int32, (n_rows, HD), 1)
    a, b, c = split3(power)
    aux = jnp.where(at == 0, a, jnp.where(at == 1, b, jnp.where(at == 2, c, 0.0)))
    aux = jnp.dot(chosen, aux.astype(jnp.bfloat16), preferred_element_type=jnp.float32)
    tail = outs[0].shape[1] - HD
    for k in range(pool):
        outs[k][:, tail:] = aux[k * per : (k + 1) * per].astype(outs[k].dtype)

    start = 0
    first = 0
    for n in range(n_w):
        count, width = bufs[n].shape[0], bufs[n].shape[2]

        def column(t, carry, n=n, first=first, start=start, width=width):
            i = first + t
            pltpu.make_async_copy(
                weights[n].at[:, pl.ds(pl.multiple_of(t * width, width), width)],
                bufs[n].at[t],
                sems.at[i],
            ).wait()
            part = jnp.dot(lhs[...], bufs[n][t], preferred_element_type=jnp.float32)
            for k in range(pool):
                outs[k][:, pl.ds(pl.multiple_of(start + t * width, width), width)] = part[
                    k * per : (k + 1) * per
                ].astype(outs[k].dtype)
            return carry

        t = 0
        while t < count:
            ahead = first + t + WINDOW
            if ahead < len(tiles):
                m, u, w_ahead = tiles[ahead]
                run = 1
                while (
                    t + run < count
                    and ahead + run < len(tiles)
                    and tiles[ahead + run][0] == m
                ):
                    run += 1

                def step(q, carry, m=m, u=u, w=w_ahead, t=t, ahead=ahead):
                    pltpu.make_async_copy(
                        weights[m].at[:, pl.ds(pl.multiple_of((u + q) * w, w), w)],
                        bufs[m].at[u + q],
                        sems.at[ahead + q],
                    ).start()
                    return column(t + q, carry)

                lax.fori_loop(0, run, step, 0)
            else:
                run = count - t
                lax.fori_loop(t, count, column, 0)
            t += run
        start += count * width
        first += count


def attend_kernel(pool, slots, seg, width_d, q_heads, kv_heads, meta, first, lens, *rest):
    parts, rest = rest[:pool], rest[pool:]
    cos, sin, keys, values = rest[:4]
    outs, rest = rest[4 : 4 + pool], rest[4 + pool :]
    q_buf, k_buf, v_buf = rest
    per = pool * slots
    group = q_heads // kv_heads
    scale = HD ** (-0.5)

    def total(at):
        got = parts[0][:, at : at + HD].astype(jnp.float32)
        for part in parts[1:]:
            got = got + part[:, at : at + HD].astype(jnp.float32)
        return got

    power = jnp.sum(total((q_heads + 2 * kv_heads) * HD), axis=1, keepdims=True)
    factor = lax.rsqrt(power * (1.0 / width_d) + EPS)
    cosines, sines = cos[...], sin[...]

    def rounded(x):
        return x.astype(jnp.bfloat16).astype(jnp.float32)

    def rotated(x):
        return rounded(x * cosines + pltpu.roll(x, HD // 2, axis=1) * sines)

    for i in range(q_heads):
        q_buf[i * per : (i + 1) * per, :] = rotated(total(i * HD) * factor)
    for g in range(kv_heads):
        k_buf[g * per : (g + 1) * per, :] = rotated(total((q_heads + g) * HD) * factor)
        v_buf[g * per : (g + 1) * per, :] = rounded(
            total((q_heads + kv_heads + g) * HD) * factor
        )

    me = meta[0]
    lane = lax.broadcasted_iota(jnp.int32, (group, HD), 1)
    at = lax.broadcasted_iota(jnp.int32, (group, seg), 1)
    for j in range(pool):
        home = lax.rem(me + j, pool)
        marks = [jnp.zeros((group, HD), jnp.float32) for _ in range(kv_heads)]
        for c in range(slots):
            s = j * slots + c
            cell = home * slots + c
            base = pl.multiple_of(cell * seg, seg)
            length = lens[cell]
            own = first[cell]
            usable = at < length
            for g in range(kv_heads):
                query = q_buf[pl.ds(g * group * per + s, group, stride=per), :]
                key_block = keys[pl.ds(base, seg), g * HD : (g + 1) * HD]
                value_block = values[pl.ds(base, seg), g * HD : (g + 1) * HD]
                score = (
                    lax.dot_general(
                        query.astype(jnp.bfloat16),
                        key_block,
                        (((1,), (1,)), ((), ())),
                        preferred_element_type=jnp.float32,
                    )
                    * scale
                )
                key_own = k_buf[g * per + s : g * per + s + 1, :]
                value_own = v_buf[g * per + s : g * per + s + 1, :]
                score_own = jnp.sum(query * key_own, axis=1, keepdims=True) * scale
                score_own = jnp.where(own > 0, score_own, LOW)
                top = jnp.maximum(
                    jnp.max(jnp.where(usable, score, LOW), axis=1, keepdims=True), score_own
                )
                weight = jnp.where(usable, jnp.exp(score - top), 0.0)
                weight_own = jnp.where(own > 0, jnp.exp(score_own - top), 0.0)
                sums = jnp.sum(weight, axis=1, keepdims=True) + weight_own
                sums = jnp.where(length > 0, sums, 1.0)
                mixed = (
                    jnp.dot(
                        weight.astype(jnp.bfloat16),
                        value_block,
                        preferred_element_type=jnp.float32,
                    )
                    + weight_own * value_own
                )
                to = c * q_heads + g * group
                outs[j][to : to + group, :] = (mixed / sums).astype(jnp.bfloat16)
                level = split3(top + jnp.log(sums))
                for piece in range(3):
                    marks[g] = jnp.where(lane == piece * slots + c, level[piece], marks[g])
        for g in range(kv_heads):
            to = slots * q_heads + g * group
            outs[j][to : to + group, :] = marks[g].astype(jnp.bfloat16)


def merge_kernel(pool, slots, rows_local, q_heads, meta, *rest):
    parts, (out, o_buf, f_buf) = rest[:pool], rest[pool:]
    per = pool * slots
    block = slots * q_heads
    me = meta[0]
    lane = lax.broadcasted_iota(jnp.int32, (q_heads, HD), 1)
    level = jnp.zeros((q_heads, HD), jnp.float32)
    slot_rows = jnp.full((1, HD), -1, jnp.int32)
    for k in range(pool):
        o_buf[k * block : (k + 1) * block, :] = parts[k][:block, :].astype(jnp.float32)
        marks = parts[k][block:, :].astype(jnp.float32)
        marks = (
            marks + pltpu.roll(marks, HD - slots, axis=1) + pltpu.roll(marks, HD - 2 * slots, axis=1)
        )
        if k:
            marks = pltpu.roll(marks, k * slots, axis=1)
        level = jnp.where((lane >= k * slots) & (lane < (k + 1) * slots), marks, level)
        owner = lax.rem(me + pool - k, pool)
        for c in range(slots):
            r = meta[1 + me * per + owner * slots + c]
            slot_rows = jnp.where(lane[:1] == k * slots + c, r, slot_rows)
    for r in range(rows_local):
        match = slot_rows == r
        top = jnp.max(jnp.where(match, level, LOW), axis=1, keepdims=True)
        factor = jnp.where(match, jnp.exp(level - top), 0.0)
        factor = factor / jnp.sum(factor, axis=1, keepdims=True)
        high = factor.astype(jnp.bfloat16).astype(jnp.float32)
        low = pltpu.roll(factor - high, per, axis=1)
        f_buf[pl.ds(r, q_heads, stride=rows_local), :] = high + low
    for i in range(q_heads):
        o = o_buf[pl.ds(i, per, stride=q_heads), :].astype(jnp.bfloat16)
        f = f_buf[i * rows_local : (i + 1) * rows_local, : 2 * per].astype(jnp.bfloat16)
        out[:, i * HD : (i + 1) * HD] = jnp.dot(
            f, jnp.concatenate([o, o], axis=0), preferred_element_type=jnp.float32
        ).astype(jnp.bfloat16)


def exchange(parts):
    pool = len(parts)
    return [parts[0]] + [
        lax.ppermute(parts[k], "pool", [(i, (i + k) % pool) for i in range(pool)])
        for k in range(1, pool)
    ]


SMEM = pl.BlockSpec(memory_space=pltpu.SMEM)
VMEM = pl.BlockSpec(memory_space=pltpu.VMEM)
ANY = pl.BlockSpec(memory_space=pl.ANY)


def body(
    hidden_in,
    norm_gain,
    w_query,
    w_key,
    w_value,
    cache_keys,
    cache_values,
    send_row,
    piece_len,
    row_len,
):
    pool = lax.axis_size("pool")
    me = lax.axis_index("pool")
    n_rows, depth = hidden_in.shape
    width_d = depth * pool
    rows_local = n_rows // pool
    slots = send_row.shape[2]
    per = pool * slots
    seg = cache_keys.shape[0] // per
    q_cols, kv_cols = w_query.shape[1], w_key.shape[1]
    q_heads, kv_heads = q_cols // HD, kv_cols // HD
    cols = q_cols + 2 * kv_cols + HD

    meta = jnp.concatenate([me[None].astype(jnp.int32), send_row.reshape(-1)])
    lens = piece_len.reshape(-1)

    weights = (w_query, w_key, w_value)
    bufs = []
    n_tiles = 0
    for w in weights:
        width = divides(w.shape[1], 256)
        bufs.append(pltpu.VMEM((w.shape[1] // width, depth, width), jnp.bfloat16))
        n_tiles += w.shape[1] // width
    *terms, positions = pl.pallas_call(
        functools.partial(project_kernel, pool, slots, rows_local),
        out_shape=[jax.ShapeDtypeStruct((per, cols), jnp.float32)]
        + [jax.ShapeDtypeStruct((per, cols), jnp.bfloat16)] * (pool - 1)
        + [jax.ShapeDtypeStruct((per, HD), jnp.float32)],
        in_specs=[SMEM, SMEM] + [ANY] * 5,
        out_specs=[VMEM] * (pool + 1),
        scratch_shapes=[
            pltpu.VMEM((n_rows, depth), jnp.bfloat16),
            pltpu.VMEM((1, depth), jnp.bfloat16),
            pltpu.VMEM((pool * per, n_rows), jnp.float32),
            pltpu.VMEM((pool * per, depth), jnp.bfloat16),
            *bufs,
            pltpu.SemaphoreType.DMA((2,)),
            pltpu.SemaphoreType.DMA((n_tiles,)),
        ],
        compiler_params=pltpu.CompilerParams(vmem_limit_bytes=50 * 2**20),
        name="project",
    )(meta, row_len, hidden_in, norm_gain.reshape(1, depth), *weights)

    terms = exchange(terms)

    named = send_row.reshape(pool, per)
    mine = lax.dynamic_slice_in_dim(send_row, me, 1, 1)[:, 0, :]
    order = me * slots + jnp.arange(slots, dtype=jnp.int32)
    earlier = (named[:, None, :] == mine[:, :, None]) & (
        jnp.arange(per, dtype=jnp.int32)[None, None, :] < order[None, :, None]
    )
    first = ((mine >= 0) & ~jnp.any(earlier, axis=2)).astype(jnp.int32).reshape(-1)

    half = HD // 2
    freq = THETA ** (-(np.arange(half) * 2.0) / HD)
    angles = positions * np.concatenate([freq, freq]).astype(np.float32)[None, :]
    sign = np.concatenate([-np.ones(half), np.ones(half)]).astype(np.float32)[None, :]
    cosines, sines = jnp.cos(angles), jnp.sin(angles) * sign

    found = pl.pallas_call(
        functools.partial(attend_kernel, pool, slots, seg, width_d, q_heads, kv_heads),
        out_shape=[jax.ShapeDtypeStruct(((slots + 1) * q_heads, HD), jnp.bfloat16)] * pool,
        in_specs=[SMEM] * 3 + [VMEM] * (pool + 4),
        out_specs=[VMEM] * pool,
        scratch_shapes=[
            pltpu.VMEM((q_heads * per, HD), jnp.float32),
            pltpu.VMEM((kv_heads * per, HD), jnp.float32),
            pltpu.VMEM((kv_heads * per, HD), jnp.float32),
        ],
        compiler_params=pltpu.CompilerParams(vmem_limit_bytes=24 * 2**20),
        name="attend",
    )(meta, first, lens, *terms, cosines, sines, cache_keys, cache_values)

    found = exchange(found)

    return pl.pallas_call(
        functools.partial(merge_kernel, pool, slots, rows_local, q_heads),
        out_shape=jax.ShapeDtypeStruct((rows_local, q_cols), jnp.bfloat16),
        in_specs=[SMEM] + [VMEM] * pool,
        out_specs=VMEM,
        scratch_shapes=[
            pltpu.VMEM((per * q_heads, HD), jnp.float32),
            pltpu.VMEM((rows_local * q_heads, HD), jnp.float32),
        ],
        compiler_params=pltpu.CompilerParams(vmem_limit_bytes=24 * 2**20),
        name="merge",
    )(meta, *found)


def solution(mesh):
    return jax.shard_map(
        body,
        mesh=mesh,
        in_specs=(
            P("groups", "pool"),
            P("pool"),
            P("pool", "tensor"),
            P("pool", "tensor"),
            P("pool", "tensor"),
            P(("groups", "pool"), "tensor"),
            P(("groups", "pool"), "tensor"),
            P("groups", None, None),
            P(("groups", "pool"), None, None),
            P("groups"),
        ),
        out_specs=P(("groups", "pool"), "tensor"),
        check_vma=False,
    )
```

```python
import functools

import jax
import jax.numpy as jnp
import numpy as np
from jax import lax
from jax.experimental import pallas as pl
from jax.experimental.pallas import tpu as pltpu
from jax.sharding import PartitionSpec as P

HD = 128
EPS = 1e-05
THETA = 500000.0
LOW = -1e30
WINDOW = 8
TILE = 256
MARKS = 72


def divides(width, limit):
    while width % limit:
        limit //= 2
    return limit


def split3(x):
    a = x.astype(jnp.bfloat16).astype(jnp.float32)
    r = x - a
    b = r.astype(jnp.bfloat16).astype(jnp.float32)
    return a, b, (r - b).astype(jnp.bfloat16).astype(jnp.float32)


def project_kernel(pool, slots, rows_local, me_ref, send, row_len, hidden, gain, *rest):
    n_w = 3
    weights, rest = rest[:n_w], rest[n_w:]
    out, pos_out, send_buf, len_buf, x_buf, g_buf, pick, lhs, *bufs, in_sem, sems = rest
    per = pool * slots
    n_slots = pool * per
    tiles = []
    for n, buf in enumerate(bufs):
        for t in range(buf.shape[0]):
            tiles.append((n, t))

    def copy(n, t, i):
        width = bufs[n].shape[2]
        at = t * width if isinstance(t, int) else pl.multiple_of(t * width, width)
        return pltpu.make_async_copy(
            weights[n].at[:, pl.ds(at, width)], bufs[n].at[t], sems.at[i]
        )

    inputs = [
        pltpu.make_async_copy(source, target, in_sem.at[i])
        for i, (source, target) in enumerate(
            ((send, send_buf), (row_len, len_buf), (hidden, x_buf), (gain, g_buf))
        )
    ]
    for one in inputs:
        one.start()
    for i in range(min(WINDOW, len(tiles))):
        copy(*tiles[i], i).start()

    n_rows = x_buf.shape[0]
    lane = lax.broadcasted_iota(jnp.int32, (1, n_rows), 1)
    inputs[0].wait()
    inputs[1].wait()

    def slot_row(owner, home, c):
        r = send_buf[home, owner, c] if len(send_buf.shape) == 3 else send_buf[
            home * per + owner * slots + c
        ]
        return jnp.where(r >= 0, home * rows_local + r, -1)

    def fill(i, carry):
        for c in range(slots):
            row = slot_row(i // pool, lax.rem(i, pool), c)
            pick[pl.ds(i * slots + c, 1), :] = (lane == row).astype(jnp.float32)
        return carry

    lax.fori_loop(0, pool * pool, fill, 0)
    me = me_ref[0]

    def fill_pos(home, carry):
        for c in range(slots):
            row = slot_row(me, home, c)
            at = len_buf[jnp.maximum(row, 0)].astype(jnp.float32)
            pos_out[pl.ds(home * slots + c, 1), :] = jnp.full((1, HD), at, jnp.float32)
        return carry

    lax.fori_loop(0, pool, fill_pos, 0)

    inputs[2].wait()
    inputs[3].wait()
    x = x_buf[...].astype(jnp.float32)
    power = jnp.sum(x * x, axis=1, keepdims=True)
    gains = g_buf[...].astype(jnp.float32).reshape(1, x.shape[1])
    scaled = (x * gains).astype(jnp.bfloat16)
    chosen = pick[...].astype(jnp.bfloat16)
    lhs[...] = jnp.dot(chosen, scaled, preferred_element_type=jnp.float32).astype(jnp.bfloat16)
    at = lax.broadcasted_iota(jnp.int32, (n_rows, HD), 1)
    a, b, c = split3(power)
    aux = jnp.where(at == 0, a, jnp.where(at == 1, b, jnp.where(at == 2, c, 0.0)))
    aux = jnp.dot(chosen, aux.astype(jnp.bfloat16), preferred_element_type=jnp.float32)
    tail = out.shape[1] - HD
    out[:, tail:] = aux.astype(jnp.bfloat16)

    start = 0
    first = 0
    for n in range(n_w):
        count, width = bufs[n].shape[0], bufs[n].shape[2]

        def column(t, carry, n=n, first=first, start=start, width=width):
            copy(n, t, first + t).wait()
            part = jnp.dot(lhs[...], bufs[n][t], preferred_element_type=jnp.float32)
            out[:, pl.ds(pl.multiple_of(start + t * width, width), width)] = part.astype(
                jnp.bfloat16
            )
            return carry

        t = 0
        while t < count:
            ahead = first + t + WINDOW
            if ahead < len(tiles):
                m, u = tiles[ahead]
                run = 1
                while (
                    t + run < count
                    and ahead + run < len(tiles)
                    and tiles[ahead + run][0] == m
                ):
                    run += 1

                def step(q, carry, m=m, u=u, t=t, ahead=ahead):
                    copy(m, u + q, ahead + q).start()
                    return column(t + q, carry)

                lax.fori_loop(0, run, step, 0)
            else:
                run = count - t
                lax.fori_loop(t, count, column, 0)
            t += run
        start += count * width
        first += count


def attend_kernel(pool, slots, seg, width_d, q_heads, kv_heads, terms, cos, sin, marks, keys, values, out, q_buf):
    per = pool * slots
    group = q_heads // kv_heads
    step = HD // group
    scale = HD ** (-0.5)

    def total(at):
        got = terms[:per, at : at + HD].astype(jnp.float32)
        for p in range(1, pool):
            got = got + terms[p * per : (p + 1) * per, at : at + HD].astype(jnp.float32)
        return got

    power = jnp.sum(total((q_heads + 2 * kv_heads) * HD), axis=1, keepdims=True)
    factor = lax.rsqrt(power * (1.0 / width_d) + EPS)
    cosines, sines = cos[...], sin[...]

    def rounded(x):
        return x.astype(jnp.bfloat16).astype(jnp.float32)

    def rotated(x):
        return rounded(x * cosines + pltpu.roll(x, HD // 2, axis=1) * sines)

    for i in range(q_heads):
        q_buf[i * per : (i + 1) * per, :] = rotated(total((2 * kv_heads + i) * HD) * factor)
    keys_own = [rotated(total(g * HD) * factor) for g in range(kv_heads)]
    values_own = [
        rounded(total((kv_heads + g) * HD) * factor) for g in range(kv_heads)
    ]

    lane = lax.broadcasted_iota(jnp.int32, (1, HD), 1)
    slot_of = lane // group
    at = lax.broadcasted_iota(jnp.int32, (seg, HD), 0)
    at_own = lax.broadcasted_iota(jnp.int32, (step, HD), 0)
    blocks = [(g, s) for s in range(0, per, step) for g in range(kv_heads)]
    columns = []
    for g, s in blocks:
        query = jnp.concatenate(
            [q_buf[pl.ds(g * group * per + s + u, group, stride=per), :] for u in range(step)], 0
        )
        columns.append(query.T.astype(jnp.bfloat16))
    scores = []
    for (g, s), query in zip(blocks, columns):
        wide = jnp.dot(
            keys[s * seg : (s + step) * seg, g * HD : (g + 1) * HD],
            query,
            preferred_element_type=jnp.float32,
        )
        score = wide[:seg]
        for u in range(1, step):
            score = jnp.where(slot_of == u, wide[u * seg : (u + 1) * seg], score)
        own = jnp.dot(
            keys_own[g][s : s + step].astype(jnp.bfloat16),
            query,
            preferred_element_type=jnp.float32,
        )
        own = jnp.sum(jnp.where(at_own == slot_of, own, 0.0), axis=0, keepdims=True)
        scores.append((score * scale, own * scale))
    turned = []
    for (g, s), (score, own) in zip(blocks, scores):
        length = marks[0:1, s * group : s * group + HD]
        with_own = marks[1:2, s * group : s * group + HD] > 0
        usable = at < length
        own = jnp.where(with_own, own, LOW)
        top = jnp.maximum(jnp.max(jnp.where(usable, score, LOW), axis=0, keepdims=True), own)
        weight = jnp.where(usable, jnp.exp(score - top), 0.0)
        weight_own = jnp.where(with_own, jnp.exp(own - top), 0.0)
        sums = jnp.sum(weight, axis=0, keepdims=True) + weight_own
        sums = jnp.where(length > 0, sums, 1.0)
        level = split3(top + jnp.log(sums))
        rows = [weight_own, 1.0 / sums] + [jnp.zeros((1, HD), jnp.float32)] * (MARKS - seg - 2)
        for piece in range(3):
            for c in range(slots):
                rows.append(jnp.where(lax.rem(slot_of, slots) == c, level[piece], 0.0))
        rows.append(jnp.zeros((HD - MARKS - 3 * slots, HD), jnp.float32))
        turned.append(jnp.concatenate([weight] + rows, 0).T)
    place = lax.broadcasted_iota(jnp.int32, (group, HD), 1)
    kept = (place >= MARKS) & (place < MARKS + 3 * slots)
    levels = {}
    for (g, s), block in zip(blocks, turned):
        for u in range(step):
            home, c = (s + u) // slots, (s + u) % slots
            rows = block[u * group : (u + 1) * group]
            mixed = jnp.dot(
                rows[:, :seg].astype(jnp.bfloat16),
                values[(s + u) * seg : (s + u + 1) * seg, g * HD : (g + 1) * HD],
                preferred_element_type=jnp.float32,
            )
            mixed = mixed + rows[:, seg : seg + 1] * values_own[g][s + u : s + u + 1]
            to = (home * (slots + 1) + c) * q_heads + g * group
            out[to : to + group, :] = (mixed * rows[:, seg + 1 : seg + 2]).astype(jnp.bfloat16)
            levels[home, g] = levels.get((home, g), 0.0) + jnp.where(kept, rows, 0.0)
    for (home, g), level in levels.items():
        to = (home * (slots + 1) + slots) * q_heads + g * group
        out[to : to + group, :] = level.astype(jnp.bfloat16)


def merge_kernel(pool, slots, rows_local, q_heads, slot_row, found, out, o_buf, f_buf):
    per = pool * slots
    block = slots * q_heads
    lane = lax.broadcasted_iota(jnp.int32, (q_heads, HD), 1)
    level = jnp.zeros((q_heads, HD), jnp.float32)
    for p in range(pool):
        at = p * (block + q_heads)
        o_buf[p * block : (p + 1) * block, :] = found[at : at + block, :].astype(jnp.float32)
        got = found[at + block : at + block + q_heads, :].astype(jnp.float32)
        got = sum(
            pltpu.roll(got, (p * slots - MARKS - piece * slots) % HD, axis=1) for piece in range(3)
        )
        level = jnp.where((lane >= p * slots) & (lane < (p + 1) * slots), got, level)
    rows = slot_row[...]
    for r in range(rows_local):
        match = rows == r
        top = jnp.max(jnp.where(match, level, LOW), axis=1, keepdims=True)
        factor = jnp.where(match, jnp.exp(level - top), 0.0)
        factor = factor / jnp.sum(factor, axis=1, keepdims=True)
        high = factor.astype(jnp.bfloat16).astype(jnp.float32)
        low = pltpu.roll(factor - high, per, axis=1)
        f_buf[pl.ds(r, q_heads, stride=rows_local), :] = high + low
    for i in range(q_heads):
        o = o_buf[pl.ds(i, per, stride=q_heads), :].astype(jnp.bfloat16)
        f = f_buf[i * rows_local : (i + 1) * rows_local, : 2 * per].astype(jnp.bfloat16)
        out[:, i * HD : (i + 1) * HD] = jnp.dot(
            f, jnp.concatenate([o, o], axis=0), preferred_element_type=jnp.float32
        ).astype(jnp.bfloat16)


def exchange(x):
    return lax.all_to_all(x, "pool", split_axis=0, concat_axis=0, tiled=True)


def in_hbm(x):
    return pltpu.with_memory_space_constraint(x, pltpu.HBM)


SMEM = pl.BlockSpec(memory_space=pltpu.SMEM)
VMEM = pl.BlockSpec(memory_space=pltpu.VMEM)
HBM = pl.BlockSpec(memory_space=pltpu.HBM)


def body(
    hidden_in,
    norm_gain,
    w_query,
    w_key,
    w_value,
    cache_keys,
    cache_values,
    send_row,
    piece_len,
    row_len,
):
    pool = lax.axis_size("pool")
    me = lax.axis_index("pool").astype(jnp.int32)
    n_rows, depth = hidden_in.shape
    width_d = depth * pool
    rows_local = n_rows // pool
    slots = send_row.shape[2]
    per = pool * slots
    seg = cache_keys.shape[0] // per
    q_cols, kv_cols = w_query.shape[1], w_key.shape[1]
    q_heads, kv_heads = q_cols // HD, kv_cols // HD
    group = q_heads // kv_heads
    cols = q_cols + 2 * kv_cols + HD

    sends = send_row if pool <= 8 else send_row.reshape(-1)
    weights = (w_key, w_value, w_query)
    bufs = []
    n_tiles = 0
    for w in weights:
        width = divides(w.shape[1], TILE)
        bufs.append(pltpu.VMEM((w.shape[1] // width, depth, width), jnp.bfloat16))
        n_tiles += w.shape[1] // width
    operands = [in_hbm(x) for x in (sends, row_len, hidden_in, norm_gain, *weights)]
    terms, positions = pl.pallas_call(
        functools.partial(project_kernel, pool, slots, rows_local),
        out_shape=[
            jax.ShapeDtypeStruct((pool * per, cols), jnp.bfloat16),
            jax.ShapeDtypeStruct((per, HD), jnp.float32),
        ],
        in_specs=[SMEM] + [HBM] * 7,
        out_specs=[VMEM] * 2,
        scratch_shapes=[
            pltpu.SMEM(sends.shape, jnp.int32),
            pltpu.SMEM(row_len.shape, jnp.int32),
            pltpu.VMEM((n_rows, depth), jnp.bfloat16),
            pltpu.VMEM((depth,), jnp.bfloat16),
            pltpu.VMEM((pool * per, n_rows), jnp.float32),
            pltpu.VMEM((pool * per, depth), jnp.bfloat16),
            *bufs,
            pltpu.SemaphoreType.DMA((4,)),
            pltpu.SemaphoreType.DMA((n_tiles,)),
        ],
        compiler_params=pltpu.CompilerParams(vmem_limit_bytes=46 * 2**20),
        name="project",
    )(me[None], *operands)

    terms = exchange(terms)

    named = send_row.reshape(pool, per)
    mine = lax.dynamic_slice_in_dim(send_row, me, 1, 1)[:, 0, :]
    order = me * slots + jnp.arange(slots, dtype=jnp.int32)
    earlier = (named[:, None, :] == mine[:, :, None]) & (
        jnp.arange(per, dtype=jnp.int32)[None, None, :] < order[None, :, None]
    )
    first = ((mine >= 0) & ~jnp.any(earlier, axis=2)).astype(jnp.int32).reshape(-1)
    marks = jnp.stack([piece_len.reshape(-1), first])
    marks = jnp.broadcast_to(marks[:, :, None], (2, per, group)).reshape(2, per * group)
    slot_row = lax.dynamic_slice_in_dim(named, me, 1, 0)
    slot_row = jnp.concatenate([slot_row, jnp.full((1, HD - per), -1, jnp.int32)], 1)

    half = HD // 2
    freq = THETA ** (-(np.arange(half) * 2.0) / HD)
    angles = positions * np.concatenate([freq, freq]).astype(np.float32)[None, :]
    sign = np.concatenate([-np.ones(half), np.ones(half)]).astype(np.float32)[None, :]
    cosines, sines = jnp.cos(angles), jnp.sin(angles) * sign

    found = pl.pallas_call(
        functools.partial(attend_kernel, pool, slots, seg, width_d, q_heads, kv_heads),
        out_shape=jax.ShapeDtypeStruct((pool * (slots + 1) * q_heads, HD), jnp.bfloat16),
        in_specs=[VMEM] * 6,
        out_specs=VMEM,
        scratch_shapes=[pltpu.VMEM((q_heads * per, HD), jnp.float32)],
        compiler_params=pltpu.CompilerParams(vmem_limit_bytes=24 * 2**20),
        name="attend",
    )(terms, cosines, sines, marks, cache_keys, cache_values)

    found = exchange(found)

    return pl.pallas_call(
        functools.partial(merge_kernel, pool, slots, rows_local, q_heads),
        out_shape=jax.ShapeDtypeStruct((rows_local, q_cols), jnp.bfloat16),
        in_specs=[VMEM] * 2,
        out_specs=VMEM,
        scratch_shapes=[
            pltpu.VMEM((per * q_heads, HD), jnp.float32),
            pltpu.VMEM((rows_local * q_heads, HD), jnp.float32),
        ],
        compiler_params=pltpu.CompilerParams(vmem_limit_bytes=24 * 2**20),
        name="merge",
    )(slot_row, found)


def solution(mesh):
    return jax.shard_map(
        body,
        mesh=mesh,
        in_specs=(
            P("groups", "pool"),
            P("pool"),
            P("pool", "tensor"),
            P("pool", "tensor"),
            P("pool", "tensor"),
            P(("groups", "pool"), "tensor"),
            P(("groups", "pool"), "tensor"),
            P("groups", None, None),
            P(("groups", "pool"), None, None),
            P("groups"),
        ),
        out_specs=P(("groups", "pool"), "tensor"),
        check_vma=False,
    )
```

```python
import functools

import jax
import jax.numpy as jnp
import numpy as np
from jax import lax
from jax.experimental import pallas as pl
from jax.experimental.pallas import tpu as pltpu
from jax.sharding import PartitionSpec as P

HD = 128
EPS = 1e-05
THETA = 500000.0
LOW = -1e30
WINDOW = 6
DEEP = 512
MARKS = 72


def divides(width, limit):
    while width % limit:
        limit //= 2
    return limit


def split3(x):
    a = x.astype(jnp.bfloat16).astype(jnp.float32)
    r = x - a
    b = r.astype(jnp.bfloat16).astype(jnp.float32)
    return a, b, (r - b).astype(jnp.bfloat16).astype(jnp.float32)


def slot_row(send, per, slots, rows_local, owner, home, c):
    if len(send.shape) == 3:
        r = send[home, owner, c]
    else:
        r = send[home * per + owner * slots + c]
    return jnp.where(r >= 0, home * rows_local + r, -1)


def project_blocks(plan, lhs, sems):
    blocks = [(n, t) for n, entry in enumerate(plan) for t in range(entry[2].shape[0])]

    def copy(n, t, i):
        w, column, buf, _, _ = plan[n]
        _, deep, width = buf.shape
        at = t * deep if isinstance(t, int) else pl.multiple_of(t * deep, deep)
        return pltpu.make_async_copy(
            w.at[pl.ds(at, deep), column : column + width], buf.at[t], sems.at[i]
        )

    def begin():
        for i in range(min(WINDOW, len(blocks))):
            copy(*blocks[i], i).start()

    def finish():
        first = 0
        for n, (w, column, buf, sums, to) in enumerate(plan):
            count, deep, width = buf.shape
            tile = divides(width, 512)

            def work(t, carry, n=n, first=first, buf=buf, sums=sums, to=to, tile=tile, width=width):
                copy(n, t, first + t).wait()
                left = lhs[t] if count > 1 else None
                for at in range(0, width, tile):
                    if count > 1:
                        part = jnp.dot(
                            left, buf[t, :, at : at + tile], preferred_element_type=jnp.float32
                        )
                        sums[:, to + at : to + at + tile] += part
                    else:
                        part = 0.0
                        for k in range(lhs.shape[0]):
                            each = lhs.shape[2]
                            part = part + jnp.dot(
                                lhs[k],
                                buf[0, k * each : (k + 1) * each, at : at + tile],
                                preferred_element_type=jnp.float32,
                            )
                        sums[:, to + at : to + at + tile] = part
                return carry

            if count > 1:
                sums[:, to : to + width] = jnp.zeros((sums.shape[0], width), jnp.float32)
            t = 0
            while t < count:
                ahead = first + t + WINDOW
                if ahead < len(blocks):
                    m, u = blocks[ahead]
                    run = 1
                    while (
                        t + run < count
                        and ahead + run < len(blocks)
                        and blocks[ahead + run][0] == m
                    ):
                        run += 1

                    def step(q, carry, m=m, u=u, t=t, ahead=ahead, work=work):
                        copy(m, u + q, ahead + q).start()
                        return work(t + q, carry)

                    lax.fori_loop(0, run, step, 0)
                else:
                    run = count - t
                    lax.fori_loop(t, count, work, 0)
                t += run
            first += count

    return begin, finish


def project_kernel(pool, slots, rows_local, columns, me_ref, send, row_len, hidden, gain, *rest):
    w_key, w_value, w_query, *rest = rest
    outs, rest = rest[:pool], rest[pool:]
    lhs, pos_out, send_buf, len_buf, x_buf, g_buf, pick, *rest = rest
    key_buf, value_buf, query_buf, sums, in_sem, sems = rest
    per = pool * slots
    kv_cols = w_key.shape[1]
    begin, finish = project_blocks(
        [
            (w_key, 0, key_buf, sums, 0),
            (w_value, 0, value_buf, sums, kv_cols),
            (w_query, 0, query_buf, sums, 2 * kv_cols),
        ],
        lhs,
        sems,
    )
    inputs = [
        pltpu.make_async_copy(source, target, in_sem.at[i])
        for i, (source, target) in enumerate(
            ((send, send_buf), (row_len, len_buf), (hidden, x_buf), (gain, g_buf))
        )
    ]
    for one in inputs:
        one.start()
    begin()

    n_rows = x_buf.shape[0]
    lane = lax.broadcasted_iota(jnp.int32, (1, n_rows), 1)
    me = me_ref[0]
    row_of = functools.partial(slot_row, send_buf, per, slots, rows_local)
    inputs[0].wait()
    inputs[1].wait()

    def fill(i, carry):
        owner = lax.rem(me + i // pool, pool)
        home = lax.rem(owner + lax.rem(i, pool), pool)
        for c in range(slots):
            row = row_of(owner, home, c)
            pick[pl.ds(i * slots + c, 1), :] = (lane == row).astype(jnp.float32)
        return carry

    lax.fori_loop(0, pool * pool, fill, 0)

    def fill_pos(j, carry):
        for c in range(slots):
            row = row_of(me, lax.rem(me + j, pool), c)
            at = len_buf[jnp.maximum(row, 0)].astype(jnp.float32)
            pos_out[pl.ds(j * slots + c, 1), :] = jnp.full((1, HD), at, jnp.float32)
        return carry

    lax.fori_loop(0, pool, fill_pos, 0)

    inputs[2].wait()
    inputs[3].wait()
    x = x_buf[...].astype(jnp.float32)
    power = jnp.sum(x * x, axis=1, keepdims=True)
    gains = g_buf[...].astype(jnp.float32).reshape(1, x.shape[1])
    scaled = (x * gains).astype(jnp.bfloat16)
    chosen = pick[...].astype(jnp.bfloat16)
    each = lhs.shape[2]
    for k in range(lhs.shape[0]):
        lhs[k] = jnp.dot(
            chosen, scaled[:, k * each : (k + 1) * each], preferred_element_type=jnp.float32
        ).astype(jnp.bfloat16)
    at = lax.broadcasted_iota(jnp.int32, (n_rows, HD), 1)
    a, b, c = split3(power)
    aux = jnp.where(at == 0, a, jnp.where(at == 1, b, jnp.where(at == 2, c, 0.0)))
    aux = jnp.dot(chosen, aux.astype(jnp.bfloat16), preferred_element_type=jnp.float32)
    finish()
    cols = sums.shape[1]
    for k in range(pool):
        outs[k][:, :cols] = sums[k * per : (k + 1) * per, :].astype(jnp.bfloat16)
        outs[k][:, cols:] = aux[k * per : (k + 1) * per].astype(jnp.bfloat16)


def project_rest_kernel(pool, column, lhs, w_query, *rest):
    outs, (query_buf, sums, sems) = rest[:pool], rest[pool:]
    begin, finish = project_blocks([(w_query, column, query_buf, sums, 0)], lhs, sems)
    begin()
    finish()
    per = sums.shape[0] // pool
    for k in range(pool):
        outs[k][...] = sums[k * per : (k + 1) * per, :].astype(jnp.bfloat16)


def attend_kernel(pool, slots, seg, width_d, q_heads, kv_heads, batches, me_ref, *rest):
    terms, rest = rest[: pool * batches], rest[pool * batches :]
    cos, sin, marks, keys, values = rest[:5]
    outs, (q_buf,) = rest[5 : 5 + pool], rest[5 + pool :]
    per = pool * slots
    group = q_heads // kv_heads
    step = HD // group
    scale = HD ** (-0.5)

    def total(batch, at):
        got = terms[batch * pool][:, at : at + HD].astype(jnp.float32)
        for p in range(1, pool):
            got = got + terms[batch * pool + p][:, at : at + HD].astype(jnp.float32)
        return got

    heads = [(0, at) for at in range(2 * kv_heads * HD, terms[0].shape[1] - HD, HD)]
    for batch in range(1, batches):
        heads += [(batch, at) for at in range(0, terms[batch * pool].shape[1], HD)]
    power = jnp.sum(total(0, terms[0].shape[1] - HD), axis=1, keepdims=True)
    factor = lax.rsqrt(power * (1.0 / width_d) + EPS)
    cosines, sines = cos[...], sin[...]

    def rounded(x):
        return x.astype(jnp.bfloat16).astype(jnp.float32)

    def rotated(x):
        return rounded(x * cosines + pltpu.roll(x, HD // 2, axis=1) * sines)

    for i in range(q_heads):
        q_buf[i * per : (i + 1) * per, :] = rotated(total(*heads[i]) * factor)
    keys_own = [rotated(total(0, g * HD) * factor) for g in range(kv_heads)]
    values_own = [
        rounded(total(0, (kv_heads + g) * HD) * factor) for g in range(kv_heads)
    ]

    me = me_ref[0]

    def base(j):
        return pl.multiple_of(lax.rem(me + j, pool) * (slots * seg), slots * seg)

    lane = lax.broadcasted_iota(jnp.int32, (1, HD), 1)
    slot_of = lane // group
    at = lax.broadcasted_iota(jnp.int32, (seg, HD), 0)
    at_own = lax.broadcasted_iota(jnp.int32, (step, HD), 0)
    blocks = [(g, s) for s in range(0, per, step) for g in range(kv_heads)]
    columns = []
    for g, s in blocks:
        query = jnp.concatenate(
            [q_buf[pl.ds(g * group * per + s + u, group, stride=per), :] for u in range(step)], 0
        )
        columns.append(query.T.astype(jnp.bfloat16))
    scores = []
    for (g, s), query in zip(blocks, columns):
        score = None
        for u in range(0, step, slots):
            wide = jnp.dot(
                keys[pl.ds(base((s + u) // slots), slots * seg), g * HD : (g + 1) * HD],
                query,
                preferred_element_type=jnp.float32,
            )
            for c in range(slots):
                each = wide[c * seg : (c + 1) * seg]
                score = each if score is None else jnp.where(slot_of == u + c, each, score)
        own = jnp.dot(
            keys_own[g][s : s + step].astype(jnp.bfloat16),
            query,
            preferred_element_type=jnp.float32,
        )
        own = jnp.sum(jnp.where(at_own == slot_of, own, 0.0), axis=0, keepdims=True)
        scores.append((score * scale, own * scale))
    turned = []
    for (g, s), (score, own) in zip(blocks, scores):
        length = marks[0:1, s * group : s * group + HD]
        with_own = marks[1:2, s * group : s * group + HD] > 0
        usable = at < length
        own = jnp.where(with_own, own, LOW)
        top = jnp.maximum(jnp.max(jnp.where(usable, score, LOW), axis=0, keepdims=True), own)
        weight = jnp.where(usable, jnp.exp(score - top), 0.0)
        weight_own = jnp.where(with_own, jnp.exp(own - top), 0.0)
        sums = jnp.sum(weight, axis=0, keepdims=True) + weight_own
        sums = jnp.where(length > 0, sums, 1.0)
        level = split3(top + jnp.log(sums))
        rows = [weight_own, 1.0 / sums] + [jnp.zeros((1, HD), jnp.float32)] * (MARKS - seg - 2)
        for piece in range(3):
            for c in range(slots):
                rows.append(jnp.where(lax.rem(slot_of, slots) == c, level[piece], 0.0))
        rows.append(jnp.zeros((HD - MARKS - 3 * slots, HD), jnp.float32))
        turned.append(jnp.concatenate([weight] + rows, 0).T)
    place = lax.broadcasted_iota(jnp.int32, (group, HD), 1)
    kept = (place >= MARKS) & (place < MARKS + 3 * slots)
    levels = {}
    for (g, s), block in zip(blocks, turned):
        for u in range(step):
            home, c = (s + u) // slots, (s + u) % slots
            rows = block[u * group : (u + 1) * group]
            mixed = jnp.dot(
                rows[:, :seg].astype(jnp.bfloat16),
                values[pl.ds(base(home) + c * seg, seg), g * HD : (g + 1) * HD],
                preferred_element_type=jnp.float32,
            )
            mixed = mixed + rows[:, seg : seg + 1] * values_own[g][s + u : s + u + 1]
            to = c * q_heads + g * group
            outs[home][to : to + group, :] = (mixed * rows[:, seg + 1 : seg + 2]).astype(jnp.bfloat16)
            levels[home, g] = levels.get((home, g), 0.0) + jnp.where(kept, rows, 0.0)
    for (home, g), level in levels.items():
        to = slots * q_heads + g * group
        outs[home][to : to + group, :] = level.astype(jnp.bfloat16)


def merge_kernel(pool, slots, rows_local, q_heads, rows_ref, *rest):
    found, (out, o_buf, f_buf) = rest[:pool], rest[pool:]
    per = pool * slots
    block = slots * q_heads
    lane = lax.broadcasted_iota(jnp.int32, (q_heads, HD), 1)
    level = jnp.zeros((q_heads, HD), jnp.float32)
    for p in range(pool):
        o_buf[p * block : (p + 1) * block, :] = found[p][:block, :].astype(jnp.float32)
        got = found[p][block : block + q_heads, :].astype(jnp.float32)
        got = sum(
            pltpu.roll(got, (p * slots - MARKS - piece * slots) % HD, axis=1) for piece in range(3)
        )
        level = jnp.where((lane >= p * slots) & (lane < (p + 1) * slots), got, level)
    rows = rows_ref[...]
    for r in range(rows_local):
        match = rows == r
        top = jnp.max(jnp.where(match, level, LOW), axis=1, keepdims=True)
        factor = jnp.where(match, jnp.exp(level - top), 0.0)
        factor = factor / jnp.sum(factor, axis=1, keepdims=True)
        high = factor.astype(jnp.bfloat16).astype(jnp.float32)
        low = pltpu.roll(factor - high, per, axis=1)
        f_buf[pl.ds(r, q_heads, stride=rows_local), :] = high + low
    for i in range(q_heads):
        o = o_buf[pl.ds(i, per, stride=q_heads), :].astype(jnp.bfloat16)
        f = f_buf[i * rows_local : (i + 1) * rows_local, : 2 * per].astype(jnp.bfloat16)
        out[:, i * HD : (i + 1) * HD] = jnp.dot(
            f, jnp.concatenate([o, o], axis=0), preferred_element_type=jnp.float32
        ).astype(jnp.bfloat16)


def exchange(parts):
    pool = len(parts)
    return [parts[0]] + [
        lax.ppermute(parts[k], "pool", [(i, (i + k) % pool) for i in range(pool)])
        for k in range(1, pool)
    ]


def onwards(x, start):
    return lax.dynamic_slice_in_dim(jnp.concatenate([x, x], 0), start, x.shape[0], 0)


def in_hbm(x):
    return pltpu.with_memory_space_constraint(x, pltpu.HBM)


SMEM = pl.BlockSpec(memory_space=pltpu.SMEM)
VMEM = pl.BlockSpec(memory_space=pltpu.VMEM)
HBM = pl.BlockSpec(memory_space=pltpu.HBM)


def body(
    hidden_in,
    norm_gain,
    w_query,
    w_key,
    w_value,
    cache_keys,
    cache_values,
    send_row,
    piece_len,
    row_len,
):
    pool = lax.axis_size("pool")
    me = lax.axis_index("pool").astype(jnp.int32)
    n_rows, depth = hidden_in.shape
    width_d = depth * pool
    rows_local = n_rows // pool
    slots = send_row.shape[2]
    per = pool * slots
    seg = cache_keys.shape[0] // per
    q_cols, kv_cols = w_query.shape[1], w_key.shape[1]
    q_heads, kv_heads = q_cols // HD, kv_cols // HD
    group = q_heads // kv_heads
    cols = q_cols + 2 * kv_cols + HD

    sends = send_row if pool <= 8 else send_row.reshape(-1)
    deep = divides(depth, DEEP)
    batches = 2 if q_heads % 16 == 0 and kv_heads > 1 else 1
    width = q_cols // batches

    def parts(width):
        return [jax.ShapeDtypeStruct((per, width), jnp.bfloat16)] * pool

    operands = [in_hbm(x) for x in (sends, row_len, hidden_in, norm_gain, w_key, w_value, w_query)]
    *first_terms, lhs, positions = pl.pallas_call(
        functools.partial(project_kernel, pool, slots, rows_local, width),
        out_shape=[
            *parts(2 * kv_cols + width + HD),
            jax.ShapeDtypeStruct((depth // deep, pool * per, deep), jnp.bfloat16),
            jax.ShapeDtypeStruct((per, HD), jnp.float32),
        ],
        in_specs=[SMEM] + [HBM] * 7,
        out_specs=[VMEM] * (pool + 2),
        scratch_shapes=[
            pltpu.SMEM(sends.shape, jnp.int32),
            pltpu.SMEM(row_len.shape, jnp.int32),
            pltpu.VMEM((n_rows, depth), jnp.bfloat16),
            pltpu.VMEM((depth,), jnp.bfloat16),
            pltpu.VMEM((pool * per, n_rows), jnp.float32),
            pltpu.VMEM((1, depth, kv_cols), jnp.bfloat16),
            pltpu.VMEM((1, depth, kv_cols), jnp.bfloat16),
            pltpu.VMEM((depth // deep, deep, width), jnp.bfloat16),
            pltpu.VMEM((pool * per, 2 * kv_cols + width), jnp.float32),
            pltpu.SemaphoreType.DMA((4,)),
            pltpu.SemaphoreType.DMA((depth // deep + 2,)),
        ],
        compiler_params=pltpu.CompilerParams(vmem_limit_bytes=40 * 2**20),
        name="project",
    )(me[None], *operands)
    terms = exchange(first_terms)
    for batch in range(1, batches):
        terms += exchange(
            pl.pallas_call(
                functools.partial(project_rest_kernel, pool, batch * width),
                out_shape=parts(width),
                in_specs=[VMEM, HBM],
                out_specs=[VMEM] * pool,
                scratch_shapes=[
                    pltpu.VMEM((depth // deep, deep, width), jnp.bfloat16),
                    pltpu.VMEM((pool * per, width), jnp.float32),
                    pltpu.SemaphoreType.DMA((depth // deep,)),
                ],
                compiler_params=pltpu.CompilerParams(vmem_limit_bytes=40 * 2**20),
                name="project_rest",
            )(lhs, operands[-1])
        )

    named = send_row.reshape(pool, per)
    mine = lax.dynamic_slice_in_dim(send_row, me, 1, 1)[:, 0, :]
    order = me * slots + jnp.arange(slots, dtype=jnp.int32)
    earlier = (named[:, None, :] == mine[:, :, None]) & (
        jnp.arange(per, dtype=jnp.int32)[None, None, :] < order[None, :, None]
    )
    first = ((mine >= 0) & ~jnp.any(earlier, axis=2)).astype(jnp.int32).reshape(-1)
    marks = onwards(jnp.stack([piece_len.reshape(-1), first], 1), me * slots).T
    marks = jnp.broadcast_to(marks[:, :, None], (2, per, group)).reshape(2, per * group)
    owners = lax.dynamic_slice_in_dim(send_row, me, 1, 0)[0, ::-1]
    slot_rows = onwards(owners, pool - 1 - me).reshape(1, per)
    slot_rows = jnp.concatenate([slot_rows, jnp.full((1, HD - per), -1, jnp.int32)], 1)

    half = HD // 2
    freq = THETA ** (-(np.arange(half) * 2.0) / HD)
    angles = positions * np.concatenate([freq, freq]).astype(np.float32)[None, :]
    sign = np.concatenate([-np.ones(half), np.ones(half)]).astype(np.float32)[None, :]
    cosines, sines = jnp.cos(angles), jnp.sin(angles) * sign

    found = pl.pallas_call(
        functools.partial(attend_kernel, pool, slots, seg, width_d, q_heads, kv_heads, batches),
        out_shape=[jax.ShapeDtypeStruct(((slots + 1) * q_heads, HD), jnp.bfloat16)] * pool,
        in_specs=[SMEM] + [VMEM] * (pool * batches + 5),
        out_specs=[VMEM] * pool,
        scratch_shapes=[pltpu.VMEM((q_heads * per, HD), jnp.float32)],
        compiler_params=pltpu.CompilerParams(vmem_limit_bytes=24 * 2**20),
        name="attend",
    )(me[None], *terms, cosines, sines, marks, cache_keys, cache_values)

    found = exchange(found)

    return pl.pallas_call(
        functools.partial(merge_kernel, pool, slots, rows_local, q_heads),
        out_shape=jax.ShapeDtypeStruct((rows_local, q_cols), jnp.bfloat16),
        in_specs=[VMEM] * (1 + pool),
        out_specs=VMEM,
        scratch_shapes=[
            pltpu.VMEM((per * q_heads, HD), jnp.float32),
            pltpu.VMEM((rows_local * q_heads, HD), jnp.float32),
        ],
        compiler_params=pltpu.CompilerParams(vmem_limit_bytes=24 * 2**20),
        name="merge",
    )(slot_rows, *found)


def solution(mesh):
    return jax.shard_map(
        body,
        mesh=mesh,
        in_specs=(
            P("groups", "pool"),
            P("pool"),
            P("pool", "tensor"),
            P("pool", "tensor"),
            P("pool", "tensor"),
            P(("groups", "pool"), "tensor"),
            P(("groups", "pool"), "tensor"),
            P("groups", None, None),
            P(("groups", "pool"), None, None),
            P("groups"),
        ),
        out_specs=P(("groups", "pool"), "tensor"),
        check_vma=False,
    )
```

```python
import functools

import jax
import jax.numpy as jnp
import numpy as np
from jax import lax
from jax.experimental import pallas as pl
from jax.experimental.pallas import tpu as pltpu
from jax.sharding import PartitionSpec as P

HD = 128
EPS = 1e-05
THETA = 500000.0
LOW = -1e30
WINDOW = 8
DEEP = 512
LEVELS = 16


def divides(width, limit):
    while width % limit:
        limit //= 2
    return limit


def split3(x):
    a = x.astype(jnp.bfloat16).astype(jnp.float32)
    r = x - a
    b = r.astype(jnp.bfloat16).astype(jnp.float32)
    return a, b, (r - b).astype(jnp.bfloat16).astype(jnp.float32)


def partner(me, k):
    return lax.bitwise_xor(me, k)


def project_blocks(plan, sems):
    blocks = [(n, t) for n, entry in enumerate(plan) for t in range(entry[2].shape[0])]

    def copy(n, t, i):
        w, column, buf, _ = plan[n]
        _, deep, width = buf.shape
        at = t * deep if isinstance(t, int) else pl.multiple_of(t * deep, deep)
        return pltpu.make_async_copy(
            w.at[pl.ds(at, deep), column : column + width], buf.at[t], sems.at[i]
        )

    def begin():
        for i in range(min(WINDOW, len(blocks))):
            copy(*blocks[i], i).start()

    def finish(between=None):
        first = 0
        for n, (_, _, buf, use) in enumerate(plan):
            count = buf.shape[0]
            if n == len(plan) - 1 and between is not None:
                between()

            def work(t, carry, n=n, first=first, use=use):
                copy(n, t, first + t).wait()
                use(t)
                return carry

            t = 0
            while t < count:
                ahead = first + t + WINDOW
                if ahead < len(blocks):
                    m, u = blocks[ahead]
                    run = 1
                    while (
                        t + run < count
                        and ahead + run < len(blocks)
                        and blocks[ahead + run][0] == m
                    ):
                        run += 1

                    def step(q, carry, m=m, u=u, t=t, ahead=ahead, work=work):
                        copy(m, u + q, ahead + q).start()
                        return work(t + q, carry)

                    lax.fori_loop(0, run, step, 0)
                else:
                    run = count - t
                    lax.fori_loop(t, count, work, 0)
                t += run
            first += count

    return begin, finish


def add_products(left, buf, t, sums):
    width = buf.shape[2]
    tile = divides(width, 512)
    for at in range(0, width, tile):
        sums[:, at : at + tile] += jnp.dot(
            left, buf[t, :, at : at + tile], preferred_element_type=jnp.float32
        )


def spread(chosen, sums, outs, at):
    width = sums.shape[1]
    tile = divides(width, 512)
    per = chosen.shape[0] // len(outs)
    for column in range(0, width, tile):
        rows = jnp.dot(
            chosen,
            sums[:, column : column + tile].astype(jnp.bfloat16),
            preferred_element_type=jnp.float32,
        ).astype(jnp.bfloat16)
        for k, out in enumerate(outs):
            out[:, at + column : at + column + tile] = rows[k * per : (k + 1) * per]


def project_kernel(pool, slots, rows_local, me_ref, send, lens, row_len, hidden, gain, *rest):
    w_key, w_value, w_query, *rest = rest
    outs, rest = rest[:pool], rest[pool:]
    lhs, pick, positions, marks, home_rows, home_slots, *rest = rest
    send_buf, lens_buf, row_len_buf, x_buf, g_buf, *rest = rest
    query_buf, key_buf, value_buf, late_buf, sums, squares, in_sem, sems = rest
    per = pool * slots
    n_rows, depth = x_buf.shape
    count, deep, _ = query_buf.shape
    me = me_ref[0]

    def named(home, owner, c):
        if len(send_buf.shape) == 3:
            return send_buf[home, owner, c]
        return send_buf[home * per + owner * slots + c]

    lane = lax.broadcasted_iota(jnp.int32, (1, n_rows), 1)
    place = lax.broadcasted_iota(jnp.int32, (1, HD), 1)
    group = marks.shape[1] // per
    slot_of = lax.broadcasted_iota(jnp.int32, (1, marks.shape[1]), 1) // group

    def choose(i):
        owner = partner(me, i // per)
        s = lax.rem(i, per)
        home = partner(owner, s // slots)
        r = named(home, owner, lax.rem(s, slots))
        row = jnp.where(r >= 0, home * rows_local + r, -1)
        pick[pl.ds(i, 1), :] = (lane == row).astype(jnp.float32)

    def describe(s):
        k, c = s // slots, lax.rem(s, slots)
        home = partner(me, k)
        r = named(home, me, c)
        at = row_len_buf[home * rows_local + jnp.maximum(r, 0)].astype(jnp.float32)
        positions[pl.ds(s, 1), :] = jnp.full((1, HD), at, jnp.float32)
        length = lens_buf[0, home, c] if len(lens_buf.shape) == 3 else lens_buf[home * slots + c]
        earlier = jnp.int32(0)
        for e in range(per):
            same = (named(home, e // slots, e % slots) == r) & (e < me * slots + c)
            earlier = earlier | same.astype(jnp.int32)
        first = jnp.where((earlier == 0) & (r >= 0), 1, 0)
        marks[0:1, :] = jnp.where(slot_of == s, length, marks[0:1, :])
        marks[1:2, :] = jnp.where(slot_of == s, first, marks[1:2, :])
        mine = named(me, home, c)
        home_slots[...] = jnp.where(lax.rem(place, per) == s, mine, home_slots[...])
        home_rows[pl.ds(k, 1), :] = jnp.where(
            lax.rem(place // group, slots) == c, mine, home_rows[pl.ds(k, 1), :]
        )

    def each(do, total, t):
        share = -(-total // count)
        if share <= 16 and total % count == 0:
            for q in range(share):
                do(t * share + q)
        else:

            @pl.when(t == 0)
            def _():
                def one(i, carry):
                    do(i)
                    return carry

                lax.fori_loop(0, total, one, 0)

    def use_query(t):
        at = pl.multiple_of(t * deep, deep)
        x = x_buf[:, pl.ds(at, deep)].astype(jnp.float32)
        gains = g_buf[pl.ds(at, deep)].astype(jnp.float32).reshape(1, deep)
        left = (x * gains).astype(jnp.bfloat16)
        lhs[t] = left
        squared = x * x
        for column in range(0, deep, HD):
            squares[...] += squared[:, column : column + HD]
        add_products(left, query_buf, t, sums.at[:, 2 * kv_cols : late])
        each(choose, pool * per, t)
        each(describe, per, t)

    def use_late(t):
        add_products(lhs[t], late_buf, t, sums.at[:, late:])

    kv_cols = w_key.shape[1]
    late = 2 * kv_cols + query_buf.shape[2]

    def use_narrow(buf, at):
        halves, tall, _ = buf.shape

        def use(t):
            part = 0.0
            for k in range(tall // deep):
                part = part + jnp.dot(
                    lhs[t * (tall // deep) + k],
                    buf[t, k * deep : (k + 1) * deep, :],
                    preferred_element_type=jnp.float32,
                )
            sums[:, at : at + kv_cols] += part

        return use

    begin, finish = project_blocks(
        [
            (w_query, 0, query_buf, use_query),
            (w_key, 0, key_buf, use_narrow(key_buf, 0)),
            (w_value, 0, value_buf, use_narrow(value_buf, kv_cols)),
            (w_query, query_buf.shape[2], late_buf, use_late),
        ],
        sems,
    )
    inputs = [
        pltpu.make_async_copy(source, target, in_sem.at[i])
        for i, (source, target) in enumerate(
            (
                (gain, g_buf),
                (hidden, x_buf),
                (send, send_buf),
                (lens, lens_buf),
                (row_len, row_len_buf),
            )
        )
    ]
    for one in inputs:
        one.start()
    begin()
    sums[...] = jnp.zeros(sums.shape, jnp.float32)
    squares[...] = jnp.zeros((n_rows, HD), jnp.float32)
    marks[...] = jnp.zeros(marks.shape, jnp.int32)
    home_rows[...] = jnp.full(home_rows.shape, -1, jnp.int32)
    home_slots[...] = jnp.full(home_slots.shape, -1, jnp.int32)
    for one in inputs:
        one.wait()

    def between():
        power = jnp.sum(squares[...], axis=1, keepdims=True)
        at = lax.broadcasted_iota(jnp.int32, (n_rows, HD), 1)
        a, b, c = split3(power)
        squares[...] = jnp.where(at == 0, a, jnp.where(at == 1, b, jnp.where(at == 2, c, 0.0)))
        chosen = pick[...].astype(jnp.bfloat16)
        spread(chosen, squares, outs, sums.shape[1])
        spread(chosen, sums.at[:, :late], outs, 0)

    finish(between)
    spread(pick[...].astype(jnp.bfloat16), sums.at[:, late:], outs, late)


def project_rest_kernel(pool, column, lhs, pick, w_query, near, *rest):
    outs, (query_buf, sums, sems) = rest[:pool], rest[pool:]
    done = near.shape[1]

    def use(t):
        add_products(lhs[t], query_buf, t, sums)

    begin, finish = project_blocks([(w_query, column, query_buf, use)], sems)
    begin()
    sums[...] = jnp.zeros(sums.shape, jnp.float32)
    outs[1][:, :done] = near[...]
    finish()
    outs = [out.at[:, done:] if k == 1 else out for k, out in enumerate(outs)]
    spread(pick[...].astype(jnp.bfloat16), sums, outs, 0)


def attend_kernel(pool, slots, seg, width_d, q_heads, kv_heads, me_ref, *rest):
    terms, rest = rest[: 2 * pool - 1], rest[2 * pool - 1 :]
    cos, sin, marks, keys, values = rest[:5]
    outs, (q_buf,) = rest[5 : 5 + pool], rest[5 + pool :]
    per = pool * slots
    group = q_heads // kv_heads
    step = HD // group
    scale = HD ** (-0.5)

    own, own_rest, near = terms[:3]
    far, far_rest = terms[3 : 1 + pool], terms[1 + pool :]
    first_cols, cols = own.shape[1], near.shape[1]

    def total(at):
        if at < first_cols:
            got, others = own[:, at : at + HD], far
        else:
            got, others = own_rest[:, at - first_cols : at - first_cols + HD], far_rest
        got = got.astype(jnp.float32) + near[:, at : at + HD].astype(jnp.float32)
        at = at if at < first_cols else at - first_cols
        for part in others:
            got = got + part[:, at : at + HD].astype(jnp.float32)
        return got

    heads = [at for at in range(2 * kv_heads * HD, cols, HD) if at != first_cols - HD]
    power = jnp.sum(total(first_cols - HD), axis=1, keepdims=True)
    factor = lax.rsqrt(power * (1.0 / width_d) + EPS)
    cosines, sines = cos[...], sin[...]

    def rounded(x):
        return x.astype(jnp.bfloat16).astype(jnp.float32)

    def rotated(x):
        return rounded(x * cosines + pltpu.roll(x, HD // 2, axis=1) * sines)

    for i in range(q_heads):
        q_buf[i * per : (i + 1) * per, :] = rotated(total(heads[i]) * factor)
    keys_own = [rotated(total(g * HD) * factor) for g in range(kv_heads)]
    values_own = [
        rounded(total((kv_heads + g) * HD) * factor) for g in range(kv_heads)
    ]

    me = me_ref[0]

    def base(j):
        return pl.multiple_of(partner(me, j) * (slots * seg), slots * seg)

    lane = lax.broadcasted_iota(jnp.int32, (1, HD), 1)
    slot_of = lane // group
    at = lax.broadcasted_iota(jnp.int32, (seg, HD), 0)
    at_own = lax.broadcasted_iota(jnp.int32, (step, HD), 0)
    blocks = [(g, s) for s in range(0, per, step) for g in range(kv_heads)]
    columns = []
    for g, s in blocks:
        query = jnp.concatenate(
            [q_buf[pl.ds(g * group * per + s + u, group, stride=per), :] for u in range(step)], 0
        )
        columns.append(query.T.astype(jnp.bfloat16))
    scores = []
    for (g, s), query in zip(blocks, columns):
        score = None
        for u in range(0, step, slots):
            wide = jnp.dot(
                keys[pl.ds(base((s + u) // slots), slots * seg), g * HD : (g + 1) * HD],
                query,
                preferred_element_type=jnp.float32,
            )
            for c in range(slots):
                each = wide[c * seg : (c + 1) * seg]
                score = each if score is None else jnp.where(slot_of == u + c, each, score)
        own = jnp.dot(
            keys_own[g][s : s + step].astype(jnp.bfloat16),
            query,
            preferred_element_type=jnp.float32,
        )
        own = jnp.sum(jnp.where(at_own == slot_of, own, 0.0), axis=0, keepdims=True)
        scores.append((score * scale, own * scale))
    turned, levels = [], {}
    for (g, s), (score, own) in zip(blocks, scores):
        length = marks[0:1, s * group : s * group + HD]
        with_own = marks[1:2, s * group : s * group + HD] > 0
        usable = at < length
        own = jnp.where(with_own, own, LOW)
        top = jnp.maximum(jnp.max(jnp.where(usable, score, LOW), axis=0, keepdims=True), own)
        weight = jnp.where(usable, jnp.exp(score - top), 0.0)
        weight_own = jnp.where(with_own, jnp.exp(own - top), 0.0)
        sums = jnp.sum(weight, axis=0, keepdims=True) + weight_own
        sums = jnp.where(length > 0, sums, 1.0)
        level = top + jnp.log(sums)
        for u in range(0, step, slots):
            at_lane = g * slots * group
            moved = level if at_lane == u * group else pltpu.roll(level, (at_lane - u * group) % HD, axis=1)
            there = (lane >= at_lane) & (lane < at_lane + slots * group)
            home = (s + u) // slots
            levels[home] = jnp.where(there, moved, levels.get(home, 0.0))
        rows = [weight_own, 1.0 / sums, jnp.zeros((HD - seg - 2, HD), jnp.float32)]
        turned.append(jnp.concatenate([weight] + rows, 0).T)
    for (g, s), block in zip(blocks, turned):
        for u in range(step):
            home, c = (s + u) // slots, (s + u) % slots
            rows = block[u * group : (u + 1) * group]
            mixed = jnp.dot(
                rows[:, :seg].astype(jnp.bfloat16),
                values[pl.ds(base(home) + c * seg, seg), g * HD : (g + 1) * HD],
                preferred_element_type=jnp.float32,
            )
            mixed = mixed + rows[:, seg : seg + 1] * values_own[g][s + u : s + u + 1]
            to = c * q_heads + g * group
            outs[home][to : to + group, :] = (mixed * rows[:, seg + 1 : seg + 2]).astype(jnp.bfloat16)
    for home, level in levels.items():
        block = jnp.concatenate([*split3(level), jnp.zeros((LEVELS - 3, HD), jnp.float32)], 0)
        outs[home][slots * q_heads :, :] = block.astype(jnp.bfloat16)


def merge_kernel(pool, slots, rows_local, q_heads, kv_heads, slots_ref, rows_ref, *rest):
    found, (out, scaled) = rest[:pool], rest[pool:]
    per = pool * slots
    group = q_heads // kv_heads
    block = slots * q_heads
    span = slots * group
    level = jnp.concatenate(
        [jnp.sum(part[block : block + LEVELS, :].astype(jnp.float32), 0, keepdims=True) for part in found], 0
    )
    named = rows_ref[...]
    lane = lax.broadcasted_iota(jnp.int32, (pool, HD), 1)

    def turns(x):
        for c in range(slots):
            y = x
            if c:
                y = jnp.where(
                    lax.rem(lane, span) < span - c * group,
                    pltpu.roll(x, HD - c * group, axis=1),
                    pltpu.roll(x, span - c * group, axis=1),
                )
            for k in range(pool):
                yield jnp.concatenate([y[k:], y[:k]], 0) if k else y

    same = [other == named for other in turns(named)]
    top = level
    for match, other in zip(same, turns(level)):
        top = jnp.maximum(top, jnp.where(match, other, LOW))
    weight = jnp.exp(level - top)
    total = jnp.zeros_like(weight)
    for match, other in zip(same, turns(weight)):
        total = total + jnp.where(match, other, 0.0)
    share = jnp.where(named >= 0, weight / total, 0.0)
    share = jnp.concatenate([share, jnp.zeros((HD - pool, HD), jnp.float32)], 0).T
    for k in range(pool):
        for c in range(slots):
            for g in range(kv_heads):
                at = c * q_heads + g * group
                each = g * span + c * group
                scaled[k * block + at : k * block + at + group, :] = (
                    found[k][at : at + group, :].astype(jnp.float32)
                    * share[each : each + group, k : k + 1]
                )
    row = lax.broadcasted_iota(jnp.int32, (rows_local, 2 * per), 0)
    match = (slots_ref[:, : 2 * per] == row).astype(jnp.float32).astype(jnp.bfloat16)
    for i in range(q_heads):
        part = scaled[pl.ds(i, per, stride=q_heads), :]
        high = part.astype(jnp.bfloat16)
        low = (part - high.astype(jnp.float32)).astype(jnp.bfloat16)
        out[:, i * HD : (i + 1) * HD] = jnp.dot(
            match, jnp.concatenate([high, low], 0), preferred_element_type=jnp.float32
        ).astype(jnp.bfloat16)


def exchange(parts, order):
    got = list(parts)
    for k in order:
        got[k] = lax.ppermute(parts[k], "pool", [(i, i ^ k) for i in range(len(parts))])
    return got


def in_hbm(x):
    return pltpu.with_memory_space_constraint(x, pltpu.HBM)


SMEM = pl.BlockSpec(memory_space=pltpu.SMEM)
VMEM = pl.BlockSpec(memory_space=pltpu.VMEM)
HBM = pl.BlockSpec(memory_space=pltpu.HBM)


def body(
    hidden_in,
    norm_gain,
    w_query,
    w_key,
    w_value,
    cache_keys,
    cache_values,
    send_row,
    piece_len,
    row_len,
):
    pool = lax.axis_size("pool")
    me = lax.axis_index("pool").astype(jnp.int32)
    n_rows, depth = hidden_in.shape
    width_d = depth * pool
    rows_local = n_rows // pool
    slots = send_row.shape[2]
    per = pool * slots
    seg = cache_keys.shape[0] // per
    q_cols, kv_cols = w_query.shape[1], w_key.shape[1]
    q_heads, kv_heads = q_cols // HD, kv_cols // HD
    group = q_heads // kv_heads
    cols = q_cols + 2 * kv_cols + HD

    if pool <= 8:
        indices = [send_row, piece_len, row_len]
    else:
        indices = [send_row.reshape(-1), piece_len.reshape(-1), row_len]
    deep = divides(depth, DEEP)
    count = depth // deep
    halves = 2 if count % 2 == 0 else 1
    widths = [3 * q_cols // 4, q_cols // 4]

    def parts(width):
        return [jax.ShapeDtypeStruct((per, width), jnp.bfloat16)] * pool

    operands = [in_hbm(x) for x in (*indices, hidden_in, norm_gain, w_key, w_value, w_query)]
    *first_terms, lhs, pick, positions, marks, home_rows, home_slots = pl.pallas_call(
        functools.partial(project_kernel, pool, slots, rows_local),
        out_shape=[
            *parts(2 * kv_cols + widths[0] + HD),
            jax.ShapeDtypeStruct((count, n_rows, deep), jnp.bfloat16),
            jax.ShapeDtypeStruct((pool * per, n_rows), jnp.float32),
            jax.ShapeDtypeStruct((per, HD), jnp.float32),
            jax.ShapeDtypeStruct((2, per * group), jnp.int32),
            jax.ShapeDtypeStruct((pool, HD), jnp.int32),
            jax.ShapeDtypeStruct((1, HD), jnp.int32),
        ],
        in_specs=[SMEM] + [HBM] * 8,
        out_specs=[VMEM] * (pool + 6),
        scratch_shapes=[
            *(pltpu.SMEM(x.shape, jnp.int32) for x in indices),
            pltpu.VMEM((n_rows, depth), jnp.bfloat16),
            pltpu.VMEM((depth,), jnp.bfloat16),
            pltpu.VMEM((count, deep, widths[0] // 2), jnp.bfloat16),
            pltpu.VMEM((halves, depth // halves, kv_cols), jnp.bfloat16),
            pltpu.VMEM((halves, depth // halves, kv_cols), jnp.bfloat16),
            pltpu.VMEM((count, deep, widths[0] // 2), jnp.bfloat16),
            pltpu.VMEM((n_rows, 2 * kv_cols + widths[0]), jnp.float32),
            pltpu.VMEM((n_rows, HD), jnp.float32),
            pltpu.SemaphoreType.DMA((5,)),
            pltpu.SemaphoreType.DMA((2 * count + 2 * halves,)),
        ],
        compiler_params=pltpu.CompilerParams(vmem_limit_bytes=46 * 2**20),
        name="project",
    )(me[None], *operands)
    first_cols = 2 * kv_cols + widths[0] + HD
    rest_shapes = parts(widths[1])
    rest_shapes[1] = jax.ShapeDtypeStruct((per, first_cols + widths[1]), jnp.bfloat16)
    rest_terms = pl.pallas_call(
        functools.partial(project_rest_kernel, pool, widths[0]),
        out_shape=rest_shapes,
        in_specs=[VMEM, VMEM, HBM, VMEM],
        out_specs=[VMEM] * pool,
        scratch_shapes=[
            pltpu.VMEM((count, deep, widths[1]), jnp.bfloat16),
            pltpu.VMEM((n_rows, widths[1]), jnp.float32),
            pltpu.SemaphoreType.DMA((count,)),
        ],
        compiler_params=pltpu.CompilerParams(vmem_limit_bytes=40 * 2**20),
        cost_estimate=pl.CostEstimate(
            flops=2 * n_rows * depth * widths[1],
            bytes_accessed=2 * depth * (widths[1] + n_rows),
            transcendentals=0,
        ),
        name="project_rest",
    )(lhs, pick, operands[-1], first_terms[1])
    first_terms = exchange(first_terms, range(2, pool))
    first_terms[2], rest_terms = lax.optimization_barrier((first_terms[2], list(rest_terms)))
    rest_terms = exchange(rest_terms, range(1, pool))
    terms = [first_terms[0], *rest_terms[:2], *first_terms[2:], *rest_terms[2:]]

    half = HD // 2
    freq = THETA ** (-(np.arange(half) * 2.0) / HD)
    angles = positions * np.concatenate([freq, freq]).astype(np.float32)[None, :]
    sign = np.concatenate([-np.ones(half), np.ones(half)]).astype(np.float32)[None, :]
    cosines, sines = jnp.cos(angles), jnp.sin(angles) * sign

    found = pl.pallas_call(
        functools.partial(attend_kernel, pool, slots, seg, width_d, q_heads, kv_heads),
        out_shape=[jax.ShapeDtypeStruct((slots * q_heads + LEVELS, HD), jnp.bfloat16)] * pool,
        in_specs=[SMEM] + [VMEM] * (2 * pool + 4),
        out_specs=[VMEM] * pool,
        scratch_shapes=[pltpu.VMEM((q_heads * per, HD), jnp.float32)],
        compiler_params=pltpu.CompilerParams(vmem_limit_bytes=24 * 2**20),
        name="attend",
    )(me[None], *terms, cosines, sines, marks, cache_keys, cache_values)

    found = exchange(found, [*range(2, pool), 1])

    return pl.pallas_call(
        functools.partial(merge_kernel, pool, slots, rows_local, q_heads, kv_heads),
        out_shape=jax.ShapeDtypeStruct((rows_local, q_cols), jnp.bfloat16),
        in_specs=[VMEM] * (2 + pool),
        out_specs=VMEM,
        scratch_shapes=[
            pltpu.VMEM((per * q_heads, HD), jnp.float32),
        ],
        compiler_params=pltpu.CompilerParams(vmem_limit_bytes=24 * 2**20),
        name="merge",
    )(home_slots, home_rows, *found)


def solution(mesh):
    return jax.shard_map(
        body,
        mesh=mesh,
        in_specs=(
            P("groups", "pool"),
            P("pool"),
            P("pool", "tensor"),
            P("pool", "tensor"),
            P("pool", "tensor"),
            P(("groups", "pool"), "tensor"),
            P(("groups", "pool"), "tensor"),
            P("groups", None, None),
            P(("groups", "pool"), None, None),
            P("groups"),
        ),
        out_specs=P(("groups", "pool"), "tensor"),
        check_vma=False,
    )
```

```python
import functools

import jax
import jax.numpy as jnp
import numpy as np
from jax import lax
from jax.experimental import pallas as pl
from jax.experimental.pallas import tpu as pltpu
from jax.sharding import PartitionSpec as P

HD = 128
EPS = 1e-05
THETA = 500000.0
LOW = -1e30
WINDOW = 8
DEEP = 1024
LEVELS = 16


def divides(width, limit):
    while width % limit:
        limit //= 2
    return limit


def split3(x):
    a = x.astype(jnp.bfloat16).astype(jnp.float32)
    r = x - a
    b = r.astype(jnp.bfloat16).astype(jnp.float32)
    return a, b, (r - b).astype(jnp.bfloat16).astype(jnp.float32)


def partner(me, k):
    return lax.bitwise_xor(me, k)


def project_blocks(plan, sems):
    blocks = [(n, t) for n, entry in enumerate(plan) for t in range(entry[2].shape[0])]

    def copy(n, t, i):
        w, column, buf, _ = plan[n]
        _, deep, width = buf.shape
        at = t * deep if isinstance(t, int) else pl.multiple_of(t * deep, deep)
        return pltpu.make_async_copy(
            w.at[pl.ds(at, deep), column : column + width], buf.at[t], sems.at[i]
        )

    def begin():
        for i in range(min(WINDOW, len(blocks))):
            copy(*blocks[i], i).start()

    def finish(between=None):
        first = 0
        for n, (_, _, buf, use) in enumerate(plan):
            count = buf.shape[0]
            if n == len(plan) - 1 and between is not None:
                between()

            def work(t, carry, n=n, first=first, use=use):
                copy(n, t, first + t).wait()
                use(t)
                return carry

            t = 0
            while t < count:
                ahead = first + t + WINDOW
                if ahead < len(blocks):
                    m, u = blocks[ahead]
                    run = 1
                    while (
                        t + run < count
                        and ahead + run < len(blocks)
                        and blocks[ahead + run][0] == m
                    ):
                        run += 1

                    def step(q, carry, m=m, u=u, t=t, ahead=ahead, work=work):
                        copy(m, u + q, ahead + q).start()
                        return work(t + q, carry)

                    lax.fori_loop(0, run, step, 0)
                else:
                    run = count - t
                    lax.fori_loop(t, count, work, 0)
                t += run
            first += count

    return begin, finish


def add_products(left, buf, t, sums):
    width = buf.shape[2]
    tile = divides(width, 512)
    for at in range(0, width, tile):
        sums[:, at : at + tile] += jnp.dot(
            left, buf[t, :, at : at + tile], preferred_element_type=jnp.float32
        )


def spread(chosen, sums, outs, at):
    width = sums.shape[1]
    tile = divides(width, 512)
    per = chosen.shape[0] // len(outs)
    for column in range(0, width, tile):
        rows = jnp.dot(
            chosen,
            sums[:, column : column + tile].astype(jnp.bfloat16),
            preferred_element_type=jnp.float32,
        ).astype(jnp.bfloat16)
        for k, out in enumerate(outs):
            out[:, at + column : at + column + tile] = rows[k * per : (k + 1) * per]


def project_kernel(pool, slots, rows_local, me_ref, send, lens, row_len, hidden, gain, *rest):
    w_key, w_value, w_query, *rest = rest
    outs, rest = rest[:pool], rest[pool:]
    lhs, pick, positions, marks, home_rows, home_slots, *rest = rest
    send_buf, lens_buf, row_len_buf, x_buf, g_buf, *rest = rest
    query_buf, key_buf, value_buf, late_buf, sums, squares, in_sem, sems = rest
    per = pool * slots
    n_rows, depth = x_buf.shape
    count, deep, _ = query_buf.shape
    me = me_ref[0]

    def named(home, owner, c):
        if len(send_buf.shape) == 3:
            return send_buf[home, owner, c]
        return send_buf[home * per + owner * slots + c]

    lane = lax.broadcasted_iota(jnp.int32, (1, n_rows), 1)
    place = lax.broadcasted_iota(jnp.int32, (1, HD), 1)
    group = marks.shape[1] // per
    slot_of = lax.broadcasted_iota(jnp.int32, (1, marks.shape[1]), 1) // group

    def choose(i):
        owner = partner(me, i // per)
        s = lax.rem(i, per)
        home = partner(owner, s // slots)
        r = named(home, owner, lax.rem(s, slots))
        row = jnp.where(r >= 0, home * rows_local + r, -1)
        pick[pl.ds(i, 1), :] = (lane == row).astype(jnp.float32)

    def describe(s):
        k, c = s // slots, lax.rem(s, slots)
        home = partner(me, k)
        r = named(home, me, c)
        at = row_len_buf[home * rows_local + jnp.maximum(r, 0)].astype(jnp.float32)
        positions[pl.ds(s, 1), :] = jnp.full((1, HD), at, jnp.float32)
        length = lens_buf[0, home, c] if len(lens_buf.shape) == 3 else lens_buf[home * slots + c]
        earlier = jnp.int32(0)
        for e in range(per):
            same = (named(home, e // slots, e % slots) == r) & (e < me * slots + c)
            earlier = earlier | same.astype(jnp.int32)
        first = jnp.where((earlier == 0) & (r >= 0), 1, 0)
        marks[0:1, :] = jnp.where(slot_of == s, length, marks[0:1, :])
        marks[1:2, :] = jnp.where(slot_of == s, first, marks[1:2, :])
        mine = named(me, home, c)
        home_slots[...] = jnp.where(lax.rem(place, per) == s, mine, home_slots[...])
        home_rows[pl.ds(k, 1), :] = jnp.where(
            lax.rem(place // group, slots) == c, mine, home_rows[pl.ds(k, 1), :]
        )

    def each(do, total, t):
        share = -(-total // count)
        if share <= 16 and total % count == 0:
            for q in range(share):
                do(t * share + q)
        else:

            @pl.when(t == 0)
            def _():
                def one(i, carry):
                    do(i)
                    return carry

                lax.fori_loop(0, total, one, 0)

    def use_query(t):
        short = divides(deep, 512)
        for part in range(0, deep, short):
            at = pl.multiple_of(t * deep + part, short)
            x = x_buf[:, pl.ds(at, short)].astype(jnp.float32)
            gains = g_buf[pl.ds(at, short)].astype(jnp.float32).reshape(1, short)
            lhs[t, :, part : part + short] = (x * gains).astype(jnp.bfloat16)
            squared = x * x
            total = squared[:, :HD]
            for column in range(HD, short, HD):
                total = total + squared[:, column : column + HD]
            squares[...] += total
        add_products(lhs[t], query_buf, t, sums.at[:, 2 * kv_cols : late])
        each(choose, pool * per, t)
        each(describe, per, t)

    def use_late(t):
        add_products(lhs[t], late_buf, t, sums.at[:, late:])

    kv_cols = w_key.shape[1]
    late = 2 * kv_cols + query_buf.shape[2]

    def use_narrow(buf, at):
        halves, tall, _ = buf.shape

        def use(t):
            part = 0.0
            for k in range(tall // deep):
                part = part + jnp.dot(
                    lhs[t * (tall // deep) + k],
                    buf[t, k * deep : (k + 1) * deep, :],
                    preferred_element_type=jnp.float32,
                )
            sums[:, at : at + kv_cols] += part

        return use

    begin, finish = project_blocks(
        [
            (w_query, 0, query_buf, use_query),
            (w_key, 0, key_buf, use_narrow(key_buf, 0)),
            (w_value, 0, value_buf, use_narrow(value_buf, kv_cols)),
            (w_query, query_buf.shape[2], late_buf, use_late),
        ],
        sems,
    )
    inputs = [
        pltpu.make_async_copy(source, target, in_sem.at[i])
        for i, (source, target) in enumerate(
            (
                (gain, g_buf),
                (hidden, x_buf),
                (send, send_buf),
                (lens, lens_buf),
                (row_len, row_len_buf),
            )
        )
    ]
    for one in inputs:
        one.start()
    begin()
    sums[...] = jnp.zeros(sums.shape, jnp.float32)
    squares[...] = jnp.zeros((n_rows, HD), jnp.float32)
    marks[...] = jnp.zeros(marks.shape, jnp.int32)
    home_rows[...] = jnp.full(home_rows.shape, -1, jnp.int32)
    home_slots[...] = jnp.full(home_slots.shape, -1, jnp.int32)
    for one in inputs:
        one.wait()

    def between():
        power = jnp.sum(squares[...], axis=1, keepdims=True)
        at = lax.broadcasted_iota(jnp.int32, (n_rows, HD), 1)
        a, b, c = split3(power)
        squares[...] = jnp.where(at == 0, a, jnp.where(at == 1, b, jnp.where(at == 2, c, 0.0)))
        chosen = pick[...].astype(jnp.bfloat16)
        spread(chosen, squares, outs, sums.shape[1])
        spread(chosen, sums.at[:, :late], outs, 0)

    finish(between)
    spread(pick[...].astype(jnp.bfloat16), sums.at[:, late:], outs, late)


def project_rest_kernel(pool, column, lhs, pick, w_query, near, *rest):
    outs, (query_buf, sums, sems) = rest[:pool], rest[pool:]
    done = near.shape[1]

    def use(t):
        add_products(lhs[t], query_buf, t, sums)

    begin, finish = project_blocks([(w_query, column, query_buf, use)], sems)
    begin()
    sums[...] = jnp.zeros(sums.shape, jnp.float32)
    outs[1][:, :done] = near[...]
    finish()
    outs = [out.at[:, done:] if k == 1 else out for k, out in enumerate(outs)]
    spread(pick[...].astype(jnp.bfloat16), sums, outs, 0)


def attend_kernel(pool, slots, seg, width_d, q_heads, kv_heads, me_ref, *rest):
    terms, rest = rest[: 2 * pool - 1], rest[2 * pool - 1 :]
    cos, sin, marks, keys, values = rest[:5]
    outs, (q_buf,) = rest[5 : 5 + pool], rest[5 + pool :]
    per = pool * slots
    group = q_heads // kv_heads
    step = HD // group
    scale = HD ** (-0.5)

    own, own_rest, near = terms[:3]
    far, far_rest = terms[3 : 1 + pool], terms[1 + pool :]
    first_cols, cols = own.shape[1], near.shape[1]

    def total(at):
        if at < first_cols:
            got, others = own[:, at : at + HD], far
        else:
            got, others = own_rest[:, at - first_cols : at - first_cols + HD], far_rest
        got = got.astype(jnp.float32) + near[:, at : at + HD].astype(jnp.float32)
        at = at if at < first_cols else at - first_cols
        for part in others:
            got = got + part[:, at : at + HD].astype(jnp.float32)
        return got

    heads = [at for at in range(2 * kv_heads * HD, cols, HD) if at != first_cols - HD]
    power = jnp.sum(total(first_cols - HD), axis=1, keepdims=True)
    factor = lax.rsqrt(power * (1.0 / width_d) + EPS)
    cosines, sines = cos[...], sin[...]

    def rounded(x):
        return x.astype(jnp.bfloat16).astype(jnp.float32)

    def rotated(x):
        return rounded(x * cosines + pltpu.roll(x, HD // 2, axis=1) * sines)

    for i in range(q_heads):
        q_buf[i * per : (i + 1) * per, :] = rotated(total(heads[i]) * factor)
    keys_own = [rotated(total(g * HD) * factor) for g in range(kv_heads)]
    values_own = [
        rounded(total((kv_heads + g) * HD) * factor) for g in range(kv_heads)
    ]

    me = me_ref[0]

    def base(j):
        return pl.multiple_of(partner(me, j) * (slots * seg), slots * seg)

    lane = lax.broadcasted_iota(jnp.int32, (1, HD), 1)
    slot_of = lane // group
    at = lax.broadcasted_iota(jnp.int32, (seg, HD), 0)
    at_own = lax.broadcasted_iota(jnp.int32, (step, HD), 0)
    blocks = [(g, s) for s in range(0, per, step) for g in range(kv_heads)]
    columns = []
    for g, s in blocks:
        query = jnp.concatenate(
            [q_buf[pl.ds(g * group * per + s + u, group, stride=per), :] for u in range(step)], 0
        )
        columns.append(query.T.astype(jnp.bfloat16))
    scores = []
    for (g, s), query in zip(blocks, columns):
        score = None
        for u in range(0, step, slots):
            wide = jnp.dot(
                keys[pl.ds(base((s + u) // slots), slots * seg), g * HD : (g + 1) * HD],
                query,
                preferred_element_type=jnp.float32,
            )
            for c in range(slots):
                each = wide[c * seg : (c + 1) * seg]
                score = each if score is None else jnp.where(slot_of == u + c, each, score)
        own = jnp.dot(
            keys_own[g][s : s + step].astype(jnp.bfloat16),
            query,
            preferred_element_type=jnp.float32,
        )
        own = jnp.sum(jnp.where(at_own == slot_of, own, 0.0), axis=0, keepdims=True)
        scores.append((score * scale, own * scale))
    turned, levels = [], {}
    for (g, s), (score, own) in zip(blocks, scores):
        length = marks[0:1, s * group : s * group + HD]
        with_own = marks[1:2, s * group : s * group + HD] > 0
        usable = at < length
        own = jnp.where(with_own, own, LOW)
        top = jnp.maximum(jnp.max(jnp.where(usable, score, LOW), axis=0, keepdims=True), own)
        weight = jnp.where(usable, jnp.exp(score - top), 0.0)
        weight_own = jnp.where(with_own, jnp.exp(own - top), 0.0)
        sums = jnp.sum(weight, axis=0, keepdims=True) + weight_own
        sums = jnp.where(length > 0, sums, 1.0)
        level = top + jnp.log(sums)
        for u in range(0, step, slots):
            at_lane = g * slots * group
            moved = level if at_lane == u * group else pltpu.roll(level, (at_lane - u * group) % HD, axis=1)
            there = (lane >= at_lane) & (lane < at_lane + slots * group)
            home = (s + u) // slots
            levels[home] = jnp.where(there, moved, levels.get(home, 0.0))
        rows = [weight_own, 1.0 / sums, jnp.zeros((HD - seg - 2, HD), jnp.float32)]
        turned.append(jnp.concatenate([weight] + rows, 0).T)
    for (g, s), block in zip(blocks, turned):
        for u in range(step):
            home, c = (s + u) // slots, (s + u) % slots
            rows = block[u * group : (u + 1) * group]
            mixed = jnp.dot(
                rows[:, :seg].astype(jnp.bfloat16),
                values[pl.ds(base(home) + c * seg, seg), g * HD : (g + 1) * HD],
                preferred_element_type=jnp.float32,
            )
            mixed = mixed + rows[:, seg : seg + 1] * values_own[g][s + u : s + u + 1]
            to = c * q_heads + g * group
            outs[home][to : to + group, :] = (mixed * rows[:, seg + 1 : seg + 2]).astype(jnp.bfloat16)
    for home, level in levels.items():
        block = jnp.concatenate([*split3(level), jnp.zeros((LEVELS - 3, HD), jnp.float32)], 0)
        outs[home][slots * q_heads :, :] = block.astype(jnp.bfloat16)


def merge_kernel(pool, slots, rows_local, q_heads, kv_heads, slots_ref, rows_ref, *rest):
    found, (out, scaled) = rest[:pool], rest[pool:]
    per = pool * slots
    group = q_heads // kv_heads
    block = slots * q_heads
    span = slots * group
    level = jnp.concatenate(
        [jnp.sum(part[block : block + LEVELS, :].astype(jnp.float32), 0, keepdims=True) for part in found], 0
    )
    named = rows_ref[...]
    lane = lax.broadcasted_iota(jnp.int32, (pool, HD), 1)

    def turns(x):
        for c in range(slots):
            y = x
            if c:
                y = jnp.where(
                    lax.rem(lane, span) < span - c * group,
                    pltpu.roll(x, HD - c * group, axis=1),
                    pltpu.roll(x, span - c * group, axis=1),
                )
            for k in range(pool):
                yield jnp.concatenate([y[k:], y[:k]], 0) if k else y

    same = [other == named for other in turns(named)]
    top = level
    for match, other in zip(same, turns(level)):
        top = jnp.maximum(top, jnp.where(match, other, LOW))
    weight = jnp.exp(level - top)
    total = jnp.zeros_like(weight)
    for match, other in zip(same, turns(weight)):
        total = total + jnp.where(match, other, 0.0)
    share = jnp.where(named >= 0, weight / total, 0.0)
    share = jnp.concatenate([share, jnp.zeros((HD - pool, HD), jnp.float32)], 0).T
    for k in range(pool):
        for c in range(slots):
            for g in range(kv_heads):
                at = c * q_heads + g * group
                each = g * span + c * group
                scaled[k * block + at : k * block + at + group, :] = (
                    found[k][at : at + group, :].astype(jnp.float32)
                    * share[each : each + group, k : k + 1]
                )
    row = lax.broadcasted_iota(jnp.int32, (rows_local, 2 * per), 0)
    match = (slots_ref[:, : 2 * per] == row).astype(jnp.float32).astype(jnp.bfloat16)
    for i in range(q_heads):
        part = scaled[pl.ds(i, per, stride=q_heads), :]
        high = part.astype(jnp.bfloat16)
        low = (part - high.astype(jnp.float32)).astype(jnp.bfloat16)
        out[:, i * HD : (i + 1) * HD] = jnp.dot(
            match, jnp.concatenate([high, low], 0), preferred_element_type=jnp.float32
        ).astype(jnp.bfloat16)


def exchange(parts, order):
    got = list(parts)
    for k in order:
        got[k] = lax.ppermute(parts[k], "pool", [(i, i ^ k) for i in range(len(parts))])
    return got


def in_hbm(x):
    return pltpu.with_memory_space_constraint(x, pltpu.HBM)


SMEM = pl.BlockSpec(memory_space=pltpu.SMEM)
VMEM = pl.BlockSpec(memory_space=pltpu.VMEM)
HBM = pl.BlockSpec(memory_space=pltpu.HBM)


def body(
    hidden_in,
    norm_gain,
    w_query,
    w_key,
    w_value,
    cache_keys,
    cache_values,
    send_row,
    piece_len,
    row_len,
):
    pool = lax.axis_size("pool")
    me = lax.axis_index("pool").astype(jnp.int32)
    n_rows, depth = hidden_in.shape
    width_d = depth * pool
    rows_local = n_rows // pool
    slots = send_row.shape[2]
    per = pool * slots
    seg = cache_keys.shape[0] // per
    q_cols, kv_cols = w_query.shape[1], w_key.shape[1]
    q_heads, kv_heads = q_cols // HD, kv_cols // HD
    group = q_heads // kv_heads
    cols = q_cols + 2 * kv_cols + HD

    if pool <= 8:
        indices = [send_row, piece_len, row_len]
    else:
        indices = [send_row.reshape(-1), piece_len.reshape(-1), row_len]
    deep = divides(depth, DEEP)
    count = depth // deep
    halves = 1
    widths = [3 * q_cols // 4, q_cols // 4]

    def parts(width):
        return [jax.ShapeDtypeStruct((per, width), jnp.bfloat16)] * pool

    operands = [in_hbm(x) for x in (*indices, hidden_in, norm_gain, w_key, w_value, w_query)]
    *first_terms, lhs, pick, positions, marks, home_rows, home_slots = pl.pallas_call(
        functools.partial(project_kernel, pool, slots, rows_local),
        out_shape=[
            *parts(2 * kv_cols + widths[0] + HD),
            jax.ShapeDtypeStruct((count, n_rows, deep), jnp.bfloat16),
            jax.ShapeDtypeStruct((pool * per, n_rows), jnp.float32),
            jax.ShapeDtypeStruct((per, HD), jnp.float32),
            jax.ShapeDtypeStruct((2, per * group), jnp.int32),
            jax.ShapeDtypeStruct((pool, HD), jnp.int32),
            jax.ShapeDtypeStruct((1, HD), jnp.int32),
        ],
        in_specs=[SMEM] + [HBM] * 8,
        out_specs=[VMEM] * (pool + 6),
        scratch_shapes=[
            *(pltpu.SMEM(x.shape, jnp.int32) for x in indices),
            pltpu.VMEM((n_rows, depth), jnp.bfloat16),
            pltpu.VMEM((depth,), jnp.bfloat16),
            pltpu.VMEM((count, deep, widths[0] // 2), jnp.bfloat16),
            pltpu.VMEM((halves, depth // halves, kv_cols), jnp.bfloat16),
            pltpu.VMEM((halves, depth // halves, kv_cols), jnp.bfloat16),
            pltpu.VMEM((count, deep, widths[0] // 2), jnp.bfloat16),
            pltpu.VMEM((n_rows, 2 * kv_cols + widths[0]), jnp.float32),
            pltpu.VMEM((n_rows, HD), jnp.float32),
            pltpu.SemaphoreType.DMA((5,)),
            pltpu.SemaphoreType.DMA((2 * count + 2 * halves,)),
        ],
        compiler_params=pltpu.CompilerParams(vmem_limit_bytes=46 * 2**20),
        name="project",
    )(me[None], *operands)
    first_cols = 2 * kv_cols + widths[0] + HD
    rest_shapes = parts(widths[1])
    rest_shapes[1] = jax.ShapeDtypeStruct((per, first_cols + widths[1]), jnp.bfloat16)
    rest_terms = pl.pallas_call(
        functools.partial(project_rest_kernel, pool, widths[0]),
        out_shape=rest_shapes,
        in_specs=[VMEM, VMEM, HBM, VMEM],
        out_specs=[VMEM] * pool,
        scratch_shapes=[
            pltpu.VMEM((count, deep, widths[1]), jnp.bfloat16),
            pltpu.VMEM((n_rows, widths[1]), jnp.float32),
            pltpu.SemaphoreType.DMA((count,)),
        ],
        compiler_params=pltpu.CompilerParams(vmem_limit_bytes=40 * 2**20),
        cost_estimate=pl.CostEstimate(
            flops=2 * n_rows * depth * widths[1],
            bytes_accessed=2 * depth * (widths[1] + n_rows),
            transcendentals=0,
        ),
        name="project_rest",
    )(lhs, pick, operands[-1], first_terms[1])
    first_terms = exchange(first_terms, range(2, pool))
    rest_terms = list(rest_terms)
    early, late = range(2, pool), range(3, pool)
    got, tied = lax.optimization_barrier(
        ([first_terms[k] for k in early], [rest_terms[k] for k in late])
    )
    for k, part in zip(early, got):
        first_terms[k] = part
    for k, part in zip(late, tied):
        rest_terms[k] = part
    rest_terms = exchange(rest_terms, range(1, pool))
    terms = [first_terms[0], *rest_terms[:2], *first_terms[2:], *rest_terms[2:]]

    half = HD // 2
    freq = THETA ** (-(np.arange(half) * 2.0) / HD)
    angles = positions * np.concatenate([freq, freq]).astype(np.float32)[None, :]
    sign = np.concatenate([-np.ones(half), np.ones(half)]).astype(np.float32)[None, :]
    cosines, sines = jnp.cos(angles), jnp.sin(angles) * sign

    found = pl.pallas_call(
        functools.partial(attend_kernel, pool, slots, seg, width_d, q_heads, kv_heads),
        out_shape=[jax.ShapeDtypeStruct((slots * q_heads + LEVELS, HD), jnp.bfloat16)] * pool,
        in_specs=[SMEM] + [VMEM] * (2 * pool + 4),
        out_specs=[VMEM] * pool,
        scratch_shapes=[pltpu.VMEM((q_heads * per, HD), jnp.float32)],
        compiler_params=pltpu.CompilerParams(vmem_limit_bytes=24 * 2**20),
        name="attend",
    )(me[None], *terms, cosines, sines, marks, cache_keys, cache_values)

    found = exchange(found, [*range(2, pool), 1])

    return pl.pallas_call(
        functools.partial(merge_kernel, pool, slots, rows_local, q_heads, kv_heads),
        out_shape=jax.ShapeDtypeStruct((rows_local, q_cols), jnp.bfloat16),
        in_specs=[VMEM] * (2 + pool),
        out_specs=VMEM,
        scratch_shapes=[
            pltpu.VMEM((per * q_heads, HD), jnp.float32),
        ],
        compiler_params=pltpu.CompilerParams(vmem_limit_bytes=24 * 2**20),
        name="merge",
    )(home_slots, home_rows, *found)


def solution(mesh):
    return jax.shard_map(
        body,
        mesh=mesh,
        in_specs=(
            P("groups", "pool"),
            P("pool"),
            P("pool", "tensor"),
            P("pool", "tensor"),
            P("pool", "tensor"),
            P(("groups", "pool"), "tensor"),
            P(("groups", "pool"), "tensor"),
            P("groups", None, None),
            P(("groups", "pool"), None, None),
            P("groups"),
        ),
        out_specs=P(("groups", "pool"), "tensor"),
        check_vma=False,
    )
```

```python
import functools

import jax
import jax.numpy as jnp
import numpy as np
from jax import lax
from jax.experimental import pallas as pl
from jax.experimental.pallas import tpu as pltpu
from jax.sharding import PartitionSpec as P

HD = 128
EPS = 1e-05
THETA = 500000.0
LOW = -1e30
WINDOW = 3
DEEP = 512
LEVELS = 16


def divides(width, limit):
    while width % limit:
        limit //= 2
    return limit


def split3(x):
    a = x.astype(jnp.bfloat16).astype(jnp.float32)
    r = x - a
    b = r.astype(jnp.bfloat16).astype(jnp.float32)
    return a, b, (r - b).astype(jnp.bfloat16).astype(jnp.float32)


def partner(me, k):
    return lax.bitwise_xor(me, k)


def project_blocks(plan, sems, window):
    blocks = [(n, t) for n, entry in enumerate(plan) for t in range(entry[2].shape[0])]

    def copy(n, t, i):
        w, column, buf, _ = plan[n]
        _, deep, width = buf.shape
        at = t * deep if isinstance(t, int) else pl.multiple_of(t * deep, deep)
        return pltpu.make_async_copy(
            w.at[pl.ds(at, deep), column : column + width], buf.at[t], sems.at[i]
        )

    def begin():
        for i in range(min(window, len(blocks))):
            copy(*blocks[i], i).start()

    def finish():
        first = 0
        for n, (_, _, buf, use) in enumerate(plan):
            count = buf.shape[0]

            def work(t, carry, n=n, first=first, use=use):
                copy(n, t, first + t).wait()
                use(t)
                return carry

            t = 0
            while t < count:
                ahead = first + t + window
                if ahead < len(blocks):
                    m, u = blocks[ahead]
                    run = 1
                    while (
                        t + run < count
                        and ahead + run < len(blocks)
                        and blocks[ahead + run][0] == m
                    ):
                        run += 1

                    def step(q, carry, m=m, u=u, t=t, ahead=ahead, work=work):
                        copy(m, u + q, ahead + q).start()
                        return work(t + q, carry)

                    lax.fori_loop(0, run, step, 0)
                else:
                    run = count - t
                    lax.fori_loop(t, count, work, 0)
                t += run
            first += count

    return begin, finish


def add_products(left, buf, t, sums):
    width = buf.shape[2]
    tile = divides(width, 512)
    for at in range(0, width, tile):
        sums[:, at : at + tile] += jnp.dot(
            left, buf[t, :, at : at + tile], preferred_element_type=jnp.float32
        )


def spread(chosen, sums, outs, at):
    width = sums.shape[1]
    tile = divides(width, 512)
    per = chosen.shape[0] // len(outs)
    for column in range(0, width, tile):
        rows = jnp.dot(
            chosen,
            sums[:, column : column + tile].astype(jnp.bfloat16),
            preferred_element_type=jnp.float32,
        ).astype(jnp.bfloat16)
        for k, out in enumerate(outs):
            out[:, at + column : at + column + tile] = rows[k * per : (k + 1) * per]


def project_kernel(pool, slots, rows_local, me_ref, send, lens, row_len, hidden, gain, *rest):
    w_query, *rest = rest
    outs, rest = rest[:pool], rest[pool:]
    lhs, pick, positions, marks, home_rows, home_slots, *rest = rest
    send_buf, lens_buf, row_len_buf, x_buf, g_buf, *rest = rest
    query_buf, sums, squares, in_sem, sems = rest
    per = pool * slots
    n_rows, depth = x_buf.shape
    count, deep, _ = query_buf.shape
    me = me_ref[0]

    def named(home, owner, c):
        if len(send_buf.shape) == 3:
            return send_buf[home, owner, c]
        return send_buf[home * per + owner * slots + c]

    lane = lax.broadcasted_iota(jnp.int32, (1, n_rows), 1)
    place = lax.broadcasted_iota(jnp.int32, (1, HD), 1)
    group = marks.shape[1] // per
    slot_of = lax.broadcasted_iota(jnp.int32, (1, marks.shape[1]), 1) // group

    def choose(i):
        owner = partner(me, i // per)
        s = lax.rem(i, per)
        home = partner(owner, s // slots)
        r = named(home, owner, lax.rem(s, slots))
        row = jnp.where(r >= 0, home * rows_local + r, -1)
        pick[pl.ds(i, 1), :] = (lane == row).astype(jnp.float32)

    def describe(s):
        k, c = s // slots, lax.rem(s, slots)
        home = partner(me, k)
        r = named(home, me, c)
        at = row_len_buf[home * rows_local + jnp.maximum(r, 0)].astype(jnp.float32)
        positions[pl.ds(s, 1), :] = jnp.full((1, HD), at, jnp.float32)
        length = lens_buf[0, home, c] if len(lens_buf.shape) == 3 else lens_buf[home * slots + c]
        earlier = jnp.int32(0)
        for e in range(per):
            same = (named(home, e // slots, e % slots) == r) & (e < me * slots + c)
            earlier = earlier | same.astype(jnp.int32)
        first = jnp.where((earlier == 0) & (r >= 0), 1, 0)
        marks[0:1, :] = jnp.where(slot_of == s, length, marks[0:1, :])
        marks[1:2, :] = jnp.where(slot_of == s, first, marks[1:2, :])
        mine = named(me, home, c)
        home_slots[...] = jnp.where(lax.rem(place, per) == s, mine, home_slots[...])
        home_rows[pl.ds(k, 1), :] = jnp.where(
            lax.rem(place // group, slots) == c, mine, home_rows[pl.ds(k, 1), :]
        )

    def each(do, total, t):
        share = -(-total // count)
        if share <= 16 and total % count == 0:
            for q in range(share):
                do(t * share + q)
        else:

            @pl.when(t == 0)
            def _():
                def one(i, carry):
                    do(i)
                    return carry

                lax.fori_loop(0, total, one, 0)

    def use_query(t):
        short = divides(deep, 512)
        for part in range(0, deep, short):
            at = pl.multiple_of(t * deep + part, short)
            x = x_buf[:, pl.ds(at, short)].astype(jnp.float32)
            gains = g_buf[pl.ds(at, short)].astype(jnp.float32).reshape(1, short)
            lhs[t, :, part : part + short] = (x * gains).astype(jnp.bfloat16)
            squared = x * x
            total = squared[:, :HD]
            for column in range(HD, short, HD):
                total = total + squared[:, column : column + HD]
            squares[...] += total
        add_products(lhs[t], query_buf, t, sums)
        each(choose, pool * per, t)
        each(describe, per, t)

    begin, finish = project_blocks([(w_query, 0, query_buf, use_query)], sems, WINDOW)
    inputs = [
        pltpu.make_async_copy(source, target, in_sem.at[i])
        for i, (source, target) in enumerate(
            (
                (gain, g_buf),
                (hidden, x_buf),
                (send, send_buf),
                (lens, lens_buf),
                (row_len, row_len_buf),
            )
        )
    ]
    for one in inputs:
        one.start()
    begin()
    sums[...] = jnp.zeros(sums.shape, jnp.float32)
    squares[...] = jnp.zeros((n_rows, HD), jnp.float32)
    marks[...] = jnp.zeros(marks.shape, jnp.int32)
    home_rows[...] = jnp.full(home_rows.shape, -1, jnp.int32)
    home_slots[...] = jnp.full(home_slots.shape, -1, jnp.int32)
    for one in inputs:
        one.wait()
    finish()
    power = jnp.sum(squares[...], axis=1, keepdims=True)
    at = lax.broadcasted_iota(jnp.int32, (n_rows, HD), 1)
    a, b, c = split3(power)
    squares[...] = jnp.where(at == 0, a, jnp.where(at == 1, b, jnp.where(at == 2, c, 0.0)))
    chosen = pick[...].astype(jnp.bfloat16)
    spread(chosen, squares, outs, sums.shape[1])
    spread(chosen, sums, outs, 0)


def project_rest_kernel(pool, column, lhs, pick, w_key, w_value, w_query, near, *rest):
    outs, (query_buf, sums, sems) = rest[:pool], rest[pool:]
    done = near.shape[1]
    count, _, deep = lhs.shape
    kv_cols = w_key.shape[1]

    def use(t):
        add_products(lhs[t], query_buf, t, sums.at[:, 2 * kv_cols :])

    begin, finish = project_blocks([(w_query, column, query_buf, use)], sems, count)
    begin()
    for n, w in enumerate((w_key, w_value)):
        part = 0.0
        for k in range(count):
            part = part + jnp.dot(
                lhs[k], w[k * deep : (k + 1) * deep, :], preferred_element_type=jnp.float32
            )
        sums[:, n * kv_cols : (n + 1) * kv_cols] = part
    sums[:, 2 * kv_cols :] = jnp.zeros((sums.shape[0], sums.shape[1] - 2 * kv_cols), jnp.float32)
    outs[1][:, :done] = near[...]
    finish()
    outs = [out.at[:, done:] if k == 1 else out for k, out in enumerate(outs)]
    spread(pick[...].astype(jnp.bfloat16), sums, outs, 0)


def attend_kernel(pool, slots, seg, width_d, q_heads, kv_heads, me_ref, *rest):
    terms, rest = rest[: 2 * pool - 1], rest[2 * pool - 1 :]
    cos, sin, marks, keys, values = rest[:5]
    outs, (q_buf,) = rest[5 : 5 + pool], rest[5 + pool :]
    per = pool * slots
    group = q_heads // kv_heads
    step = HD // group
    scale = HD ** (-0.5)

    own, own_rest, near = terms[:3]
    far, far_rest = terms[3 : 1 + pool], terms[1 + pool :]
    first_cols, cols = own.shape[1], near.shape[1]

    def total(at):
        if at < first_cols:
            got, others = own[:, at : at + HD], far
        else:
            got, others = own_rest[:, at - first_cols : at - first_cols + HD], far_rest
        got = got.astype(jnp.float32) + near[:, at : at + HD].astype(jnp.float32)
        at = at if at < first_cols else at - first_cols
        for part in others:
            got = got + part[:, at : at + HD].astype(jnp.float32)
        return got

    late = first_cols + 2 * kv_heads * HD
    heads = [*range(0, first_cols - HD, HD), *range(late, cols, HD)]
    power = jnp.sum(total(first_cols - HD), axis=1, keepdims=True)
    factor = lax.rsqrt(power * (1.0 / width_d) + EPS)
    cosines, sines = cos[...], sin[...]

    def rounded(x):
        return x.astype(jnp.bfloat16).astype(jnp.float32)

    def rotated(x):
        return rounded(x * cosines + pltpu.roll(x, HD // 2, axis=1) * sines)

    for i in range(q_heads):
        q_buf[i * per : (i + 1) * per, :] = rotated(total(heads[i]) * factor)
    keys_own = [rotated(total(first_cols + g * HD) * factor) for g in range(kv_heads)]
    values_own = [
        rounded(total(first_cols + (kv_heads + g) * HD) * factor) for g in range(kv_heads)
    ]

    me = me_ref[0]

    def base(j):
        return pl.multiple_of(partner(me, j) * (slots * seg), slots * seg)

    lane = lax.broadcasted_iota(jnp.int32, (1, HD), 1)
    slot_of = lane // group
    at = lax.broadcasted_iota(jnp.int32, (seg, HD), 0)
    at_own = lax.broadcasted_iota(jnp.int32, (step, HD), 0)
    blocks = [(g, s) for s in range(0, per, step) for g in range(kv_heads)]
    columns = []
    for g, s in blocks:
        query = jnp.concatenate(
            [q_buf[pl.ds(g * group * per + s + u, group, stride=per), :] for u in range(step)], 0
        )
        columns.append(query.T.astype(jnp.bfloat16))
    scores = []
    for (g, s), query in zip(blocks, columns):
        score = None
        for u in range(0, step, slots):
            wide = jnp.dot(
                keys[pl.ds(base((s + u) // slots), slots * seg), g * HD : (g + 1) * HD],
                query,
                preferred_element_type=jnp.float32,
            )
            for c in range(slots):
                each = wide[c * seg : (c + 1) * seg]
                score = each if score is None else jnp.where(slot_of == u + c, each, score)
        own = jnp.dot(
            keys_own[g][s : s + step].astype(jnp.bfloat16),
            query,
            preferred_element_type=jnp.float32,
        )
        own = jnp.sum(jnp.where(at_own == slot_of, own, 0.0), axis=0, keepdims=True)
        scores.append((score * scale, own * scale))
    turned, levels = [], {}
    for (g, s), (score, own) in zip(blocks, scores):
        length = marks[0:1, s * group : s * group + HD]
        with_own = marks[1:2, s * group : s * group + HD] > 0
        usable = at < length
        own = jnp.where(with_own, own, LOW)
        top = jnp.maximum(jnp.max(jnp.where(usable, score, LOW), axis=0, keepdims=True), own)
        weight = jnp.where(usable, jnp.exp(score - top), 0.0)
        weight_own = jnp.where(with_own, jnp.exp(own - top), 0.0)
        sums = jnp.sum(weight, axis=0, keepdims=True) + weight_own
        sums = jnp.where(length > 0, sums, 1.0)
        level = top + jnp.log(sums)
        for u in range(0, step, slots):
            at_lane = g * slots * group
            moved = level if at_lane == u * group else pltpu.roll(level, (at_lane - u * group) % HD, axis=1)
            there = (lane >= at_lane) & (lane < at_lane + slots * group)
            home = (s + u) // slots
            levels[home] = jnp.where(there, moved, levels.get(home, 0.0))
        rows = [weight_own, 1.0 / sums, jnp.zeros((HD - seg - 2, HD), jnp.float32)]
        turned.append(jnp.concatenate([weight] + rows, 0).T)
    for (g, s), block in zip(blocks, turned):
        for u in range(step):
            home, c = (s + u) // slots, (s + u) % slots
            rows = block[u * group : (u + 1) * group]
            mixed = jnp.dot(
                rows[:, :seg].astype(jnp.bfloat16),
                values[pl.ds(base(home) + c * seg, seg), g * HD : (g + 1) * HD],
                preferred_element_type=jnp.float32,
            )
            mixed = mixed + rows[:, seg : seg + 1] * values_own[g][s + u : s + u + 1]
            to = c * q_heads + g * group
            outs[home][to : to + group, :] = (mixed * rows[:, seg + 1 : seg + 2]).astype(jnp.bfloat16)
    for home, level in levels.items():
        block = jnp.concatenate([*split3(level), jnp.zeros((LEVELS - 3, HD), jnp.float32)], 0)
        outs[home][slots * q_heads :, :] = block.astype(jnp.bfloat16)


def merge_kernel(pool, slots, rows_local, q_heads, kv_heads, slots_ref, rows_ref, own, *rest):
    found, (out, scaled) = [own, rest[pool - 2], *rest[: pool - 2]], rest[pool - 1 :]
    per = pool * slots
    group = q_heads // kv_heads
    block = slots * q_heads
    span = slots * group
    level = jnp.concatenate(
        [jnp.sum(part[block : block + LEVELS, :].astype(jnp.float32), 0, keepdims=True) for part in found], 0
    )
    named = rows_ref[...]
    lane = lax.broadcasted_iota(jnp.int32, (pool, HD), 1)

    def turns(x):
        for c in range(slots):
            y = x
            if c:
                y = jnp.where(
                    lax.rem(lane, span) < span - c * group,
                    pltpu.roll(x, HD - c * group, axis=1),
                    pltpu.roll(x, span - c * group, axis=1),
                )
            for k in range(pool):
                yield jnp.concatenate([y[k:], y[:k]], 0) if k else y

    same = [other == named for other in turns(named)]
    top = level
    for match, other in zip(same, turns(level)):
        top = jnp.maximum(top, jnp.where(match, other, LOW))
    weight = jnp.exp(level - top)
    total = jnp.zeros_like(weight)
    for match, other in zip(same, turns(weight)):
        total = total + jnp.where(match, other, 0.0)
    share = jnp.where(named >= 0, weight / total, 0.0)
    share = jnp.concatenate([share, jnp.zeros((HD - pool, HD), jnp.float32)], 0).T
    for k in range(pool):
        for c in range(slots):
            for g in range(kv_heads):
                at = c * q_heads + g * group
                each = g * span + c * group
                scaled[k * block + at : k * block + at + group, :] = (
                    found[k][at : at + group, :].astype(jnp.float32)
                    * share[each : each + group, k : k + 1]
                )
    row = lax.broadcasted_iota(jnp.int32, (rows_local, 2 * per), 0)
    match = (slots_ref[:, : 2 * per] == row).astype(jnp.float32).astype(jnp.bfloat16)
    for i in range(q_heads):
        part = scaled[pl.ds(i, per, stride=q_heads), :]
        high = part.astype(jnp.bfloat16)
        low = (part - high.astype(jnp.float32)).astype(jnp.bfloat16)
        out[:, i * HD : (i + 1) * HD] = jnp.dot(
            match, jnp.concatenate([high, low], 0), preferred_element_type=jnp.float32
        ).astype(jnp.bfloat16)


def exchange(parts, order):
    got = list(parts)
    for k in order:
        got[k] = lax.ppermute(parts[k], "pool", [(i, i ^ k) for i in range(len(parts))])
    return got


def in_hbm(x):
    return pltpu.with_memory_space_constraint(x, pltpu.HBM)


SMEM = pl.BlockSpec(memory_space=pltpu.SMEM)
VMEM = pl.BlockSpec(memory_space=pltpu.VMEM)
HBM = pl.BlockSpec(memory_space=pltpu.HBM)


def body(
    hidden_in,
    norm_gain,
    w_query,
    w_key,
    w_value,
    cache_keys,
    cache_values,
    send_row,
    piece_len,
    row_len,
):
    pool = lax.axis_size("pool")
    me = lax.axis_index("pool").astype(jnp.int32)
    n_rows, depth = hidden_in.shape
    width_d = depth * pool
    rows_local = n_rows // pool
    slots = send_row.shape[2]
    per = pool * slots
    seg = cache_keys.shape[0] // per
    q_cols, kv_cols = w_query.shape[1], w_key.shape[1]
    q_heads, kv_heads = q_cols // HD, kv_cols // HD
    group = q_heads // kv_heads
    cols = q_cols + 2 * kv_cols + HD

    if pool <= 8:
        indices = [send_row, piece_len, row_len]
    else:
        indices = [send_row.reshape(-1), piece_len.reshape(-1), row_len]
    deep = divides(depth, DEEP)
    count = depth // deep
    widths = [3 * q_cols // 4, q_cols // 4]

    def parts(width):
        return [jax.ShapeDtypeStruct((per, width), jnp.bfloat16)] * pool

    operands = [in_hbm(x) for x in (*indices, hidden_in, norm_gain, w_query)]
    *first_terms, lhs, pick, positions, marks, home_rows, home_slots = pl.pallas_call(
        functools.partial(project_kernel, pool, slots, rows_local),
        out_shape=[
            *parts(widths[0] + HD),
            jax.ShapeDtypeStruct((count, n_rows, deep), jnp.bfloat16),
            jax.ShapeDtypeStruct((pool * per, n_rows), jnp.float32),
            jax.ShapeDtypeStruct((per, HD), jnp.float32),
            jax.ShapeDtypeStruct((2, per * group), jnp.int32),
            jax.ShapeDtypeStruct((pool, HD), jnp.int32),
            jax.ShapeDtypeStruct((1, HD), jnp.int32),
        ],
        in_specs=[SMEM] + [HBM] * 6,
        out_specs=[VMEM] * (pool + 6),
        scratch_shapes=[
            *(pltpu.SMEM(x.shape, jnp.int32) for x in indices),
            pltpu.VMEM((n_rows, depth), jnp.bfloat16),
            pltpu.VMEM((depth,), jnp.bfloat16),
            pltpu.VMEM((count, deep, widths[0]), jnp.bfloat16),
            pltpu.VMEM((n_rows, widths[0]), jnp.float32),
            pltpu.VMEM((n_rows, HD), jnp.float32),
            pltpu.SemaphoreType.DMA((5,)),
            pltpu.SemaphoreType.DMA((count,)),
        ],
        compiler_params=pltpu.CompilerParams(vmem_limit_bytes=46 * 2**20),
        name="project",
    )(me[None], *operands)
    first_terms, kv_weights = lax.optimization_barrier((list(first_terms), (w_key, w_value)))
    rest_cols = 2 * kv_cols + widths[1]
    rest_shapes = parts(rest_cols)
    rest_shapes[1] = jax.ShapeDtypeStruct((per, widths[0] + HD + rest_cols), jnp.bfloat16)
    rest_terms = pl.pallas_call(
        functools.partial(project_rest_kernel, pool, widths[0]),
        out_shape=rest_shapes,
        in_specs=[VMEM, VMEM, VMEM, VMEM, HBM, VMEM],
        out_specs=[VMEM] * pool,
        scratch_shapes=[
            pltpu.VMEM((count, deep, widths[1]), jnp.bfloat16),
            pltpu.VMEM((n_rows, rest_cols), jnp.float32),
            pltpu.SemaphoreType.DMA((count,)),
        ],
        compiler_params=pltpu.CompilerParams(vmem_limit_bytes=40 * 2**20),
        cost_estimate=pl.CostEstimate(
            flops=2 * n_rows * depth * rest_cols,
            bytes_accessed=2 * depth * (rest_cols + n_rows),
            transcendentals=0,
        ),
        name="project_rest",
    )(lhs, pick, *kv_weights, operands[-1], first_terms[1])
    first_terms = exchange(first_terms, range(2, pool))
    rest_terms = list(rest_terms)
    early, late = range(2, pool), range(3, pool)
    got, tied = lax.optimization_barrier(
        ([first_terms[k] for k in early], [rest_terms[k] for k in late])
    )
    for k, part in zip(early, got):
        first_terms[k] = part
    for k, part in zip(late, tied):
        rest_terms[k] = part
    rest_terms = exchange(rest_terms, range(1, pool))
    terms = [first_terms[0], *rest_terms[:2], *first_terms[2:], *rest_terms[2:]]

    half = HD // 2
    freq = THETA ** (-(np.arange(half) * 2.0) / HD)
    angles = positions * np.concatenate([freq, freq]).astype(np.float32)[None, :]
    sign = np.concatenate([-np.ones(half), np.ones(half)]).astype(np.float32)[None, :]
    cosines, sines = jnp.cos(angles), jnp.sin(angles) * sign

    found = pl.pallas_call(
        functools.partial(attend_kernel, pool, slots, seg, width_d, q_heads, kv_heads),
        out_shape=[jax.ShapeDtypeStruct((slots * q_heads + LEVELS, HD), jnp.bfloat16)] * pool,
        in_specs=[SMEM] + [VMEM] * (2 * pool + 4),
        out_specs=[VMEM] * pool,
        scratch_shapes=[pltpu.VMEM((q_heads * per, HD), jnp.float32)],
        compiler_params=pltpu.CompilerParams(vmem_limit_bytes=24 * 2**20),
        name="attend",
    )(me[None], *terms, cosines, sines, marks, cache_keys, cache_values)

    found = exchange(found, [*range(2, pool), 1])

    return pl.pallas_call(
        functools.partial(merge_kernel, pool, slots, rows_local, q_heads, kv_heads),
        out_shape=jax.ShapeDtypeStruct((rows_local, q_cols), jnp.bfloat16),
        in_specs=[VMEM] * (2 + pool),
        out_specs=VMEM,
        scratch_shapes=[
            pltpu.VMEM((per * q_heads, HD), jnp.float32),
        ],
        compiler_params=pltpu.CompilerParams(vmem_limit_bytes=24 * 2**20),
        name="merge",
    )(home_slots, home_rows, found[0], *found[2:], found[1])


def solution(mesh):
    return jax.shard_map(
        body,
        mesh=mesh,
        in_specs=(
            P("groups", "pool"),
            P("pool"),
            P("pool", "tensor"),
            P("pool", "tensor"),
            P("pool", "tensor"),
            P(("groups", "pool"), "tensor"),
            P(("groups", "pool"), "tensor"),
            P("groups", None, None),
            P(("groups", "pool"), None, None),
            P("groups"),
        ),
        out_specs=P(("groups", "pool"), "tensor"),
        check_vma=False,
    )
```

```python
import functools

import jax
import jax.numpy as jnp
import numpy as np
from jax import lax
from jax.experimental import pallas as pl
from jax.experimental.pallas import tpu as pltpu
from jax.sharding import PartitionSpec as P

HD = 128
EPS = 1e-05
THETA = 500000.0
LOW = -1e30
WINDOW = 3
DEEP = 512
LEVELS = 16


def divides(width, limit):
    while width % limit:
        limit //= 2
    return limit


def split3(x):
    a = x.astype(jnp.bfloat16).astype(jnp.float32)
    r = x - a
    b = r.astype(jnp.bfloat16).astype(jnp.float32)
    return a, b, (r - b).astype(jnp.bfloat16).astype(jnp.float32)


def partner(me, k):
    return lax.bitwise_xor(me, k)


def project_blocks(plan, sems, window):
    blocks = [(n, t) for n, entry in enumerate(plan) for t in range(entry[2].shape[0])]

    def copy(n, t, i):
        w, column, buf, _ = plan[n]
        _, deep, width = buf.shape
        at = t * deep if isinstance(t, int) else pl.multiple_of(t * deep, deep)
        return pltpu.make_async_copy(
            w.at[pl.ds(at, deep), column : column + width], buf.at[t], sems.at[i]
        )

    def begin():
        for i in range(min(window, len(blocks))):
            copy(*blocks[i], i).start()

    def finish():
        first = 0
        for n, (_, _, buf, use) in enumerate(plan):
            count = buf.shape[0]

            def work(t, carry, n=n, first=first, use=use):
                copy(n, t, first + t).wait()
                use(t)
                return carry

            t = 0
            while t < count:
                ahead = first + t + window
                if ahead < len(blocks):
                    m, u = blocks[ahead]
                    run = 1
                    while (
                        t + run < count
                        and ahead + run < len(blocks)
                        and blocks[ahead + run][0] == m
                    ):
                        run += 1

                    def step(q, carry, m=m, u=u, t=t, ahead=ahead, work=work):
                        copy(m, u + q, ahead + q).start()
                        return work(t + q, carry)

                    lax.fori_loop(0, run, step, 0)
                else:
                    run = count - t
                    lax.fori_loop(t, count, work, 0)
                t += run
            first += count

    return begin, finish


def add_products(left, buf, t, sums):
    width = buf.shape[2]
    tile = divides(width, 512)
    for at in range(0, width, tile):
        sums[:, at : at + tile] += jnp.dot(
            left, buf[t, :, at : at + tile], preferred_element_type=jnp.float32
        )


def spread(chosen, sums, outs, at):
    width = sums.shape[1]
    tile = divides(width, 512)
    per = chosen.shape[0] // len(outs)
    for column in range(0, width, tile):
        rows = jnp.dot(
            chosen,
            sums[:, column : column + tile].astype(jnp.bfloat16),
            preferred_element_type=jnp.float32,
        ).astype(jnp.bfloat16)
        for k, out in enumerate(outs):
            out[:, at + column : at + column + tile] = rows[k * per : (k + 1) * per]


def project_kernel(pool, slots, rows_local, me_ref, send, lens, row_len, hidden, gain, *rest):
    w_query, *rest = rest
    outs, rest = rest[:pool], rest[pool:]
    lhs, pick, positions, marks, home_rows, home_slots, *rest = rest
    send_buf, lens_buf, row_len_buf, x_buf, g_buf, *rest = rest
    query_buf, sums, squares, in_sem, sems = rest
    per = pool * slots
    n_rows, depth = x_buf.shape
    count, deep, _ = query_buf.shape
    me = me_ref[0]

    def named(home, owner, c):
        if len(send_buf.shape) == 3:
            return send_buf[home, owner, c]
        return send_buf[home * per + owner * slots + c]

    lane = lax.broadcasted_iota(jnp.int32, (1, n_rows), 1)
    place = lax.broadcasted_iota(jnp.int32, (1, HD), 1)
    group = marks.shape[1] // per
    slot_of = lax.broadcasted_iota(jnp.int32, (1, marks.shape[1]), 1) // group

    def choose(i):
        owner = partner(me, i // per)
        s = lax.rem(i, per)
        home = partner(owner, s // slots)
        r = named(home, owner, lax.rem(s, slots))
        row = jnp.where(r >= 0, home * rows_local + r, -1)
        pick[pl.ds(i, 1), :] = (lane == row).astype(jnp.float32)

    def describe(s):
        k, c = s // slots, lax.rem(s, slots)
        home = partner(me, k)
        r = named(home, me, c)
        at = row_len_buf[home * rows_local + jnp.maximum(r, 0)].astype(jnp.float32)
        positions[pl.ds(s, 1), :] = jnp.full((1, HD), at, jnp.float32)
        length = lens_buf[0, home, c] if len(lens_buf.shape) == 3 else lens_buf[home * slots + c]
        earlier = jnp.int32(0)
        for e in range(per):
            same = (named(home, e // slots, e % slots) == r) & (e < me * slots + c)
            earlier = earlier | same.astype(jnp.int32)
        first = jnp.where((earlier == 0) & (r >= 0), 1, 0)
        marks[0:1, :] = jnp.where(slot_of == s, length, marks[0:1, :])
        marks[1:2, :] = jnp.where(slot_of == s, first, marks[1:2, :])
        mine = named(me, home, c)
        home_slots[...] = jnp.where(lax.rem(place, per) == s, mine, home_slots[...])
        home_rows[pl.ds(k, 1), :] = jnp.where(
            lax.rem(place // group, slots) == c, mine, home_rows[pl.ds(k, 1), :]
        )

    def each(do, total, t):
        share = -(-total // count)
        if share <= 16 and total % count == 0:
            for q in range(share):
                do(t * share + q)
        else:

            @pl.when(t == 0)
            def _():
                def one(i, carry):
                    do(i)
                    return carry

                lax.fori_loop(0, total, one, 0)

    def use_query(t):
        short = divides(deep, 512)
        for part in range(0, deep, short):
            at = pl.multiple_of(t * deep + part, short)
            x = x_buf[:, pl.ds(at, short)].astype(jnp.float32)
            gains = g_buf[pl.ds(at, short)].astype(jnp.float32).reshape(1, short)
            lhs[t, :, part : part + short] = (x * gains).astype(jnp.bfloat16)
            squared = x * x
            total = squared[:, :HD]
            for column in range(HD, short, HD):
                total = total + squared[:, column : column + HD]
            squares[...] += total
        add_products(lhs[t], query_buf, t, sums)
        each(choose, pool * per, t)
        each(describe, per, t)

    begin, finish = project_blocks([(w_query, 0, query_buf, use_query)], sems, WINDOW)
    inputs = [
        pltpu.make_async_copy(source, target, in_sem.at[i])
        for i, (source, target) in enumerate(
            (
                (gain, g_buf),
                (hidden, x_buf),
                (send, send_buf),
                (lens, lens_buf),
                (row_len, row_len_buf),
            )
        )
    ]
    for one in inputs:
        one.start()
    begin()
    sums[...] = jnp.zeros(sums.shape, jnp.float32)
    squares[...] = jnp.zeros((n_rows, HD), jnp.float32)
    marks[...] = jnp.zeros(marks.shape, jnp.int32)
    home_rows[...] = jnp.full(home_rows.shape, -1, jnp.int32)
    home_slots[...] = jnp.full(home_slots.shape, -1, jnp.int32)
    for one in inputs:
        one.wait()
    finish()
    power = jnp.sum(squares[...], axis=1, keepdims=True)
    at = lax.broadcasted_iota(jnp.int32, (n_rows, HD), 1)
    a, b, c = split3(power)
    squares[...] = jnp.where(at == 0, a, jnp.where(at == 1, b, jnp.where(at == 2, c, 0.0)))
    chosen = pick[...].astype(jnp.bfloat16)
    spread(chosen, squares, outs, sums.shape[1])
    spread(chosen, sums, outs, 0)


def project_rest_kernel(pool, column, lhs, pick, near, w_key, w_value, w_query, *rest):
    outs, (key_buf, value_buf, query_buf, sums, sems) = rest[:pool], rest[pool:]
    done = near.shape[1]
    count, _, deep = lhs.shape
    kv_cols = w_key.shape[1]

    def use_narrow(buf, at):
        def use(t):
            part = 0.0
            for k in range(count):
                part = part + jnp.dot(
                    lhs[k], buf[t, k * deep : (k + 1) * deep, :], preferred_element_type=jnp.float32
                )
            sums[:, at : at + kv_cols] = part

        return use

    def use_query(t):
        add_products(lhs[t], query_buf, t, sums.at[:, 2 * kv_cols :])

    begin, finish = project_blocks(
        [
            (w_key, 0, key_buf, use_narrow(key_buf, 0)),
            (w_value, 0, value_buf, use_narrow(value_buf, kv_cols)),
            (w_query, column, query_buf, use_query),
        ],
        sems,
        2 * WINDOW,
    )
    begin()
    sums[:, 2 * kv_cols :] = jnp.zeros((sums.shape[0], sums.shape[1] - 2 * kv_cols), jnp.float32)
    outs[1][:, :done] = near[...]
    finish()
    outs = [out.at[:, done:] if k == 1 else out for k, out in enumerate(outs)]
    spread(pick[...].astype(jnp.bfloat16), sums, outs, 0)


def attend_kernel(pool, slots, seg, width_d, q_heads, kv_heads, me_ref, *rest):
    terms, rest = rest[: 2 * pool - 1], rest[2 * pool - 1 :]
    cos, sin, marks, keys, values = rest[:5]
    outs, (q_buf,) = rest[5 : 5 + pool], rest[5 + pool :]
    per = pool * slots
    group = q_heads // kv_heads
    step = HD // group
    scale = HD ** (-0.5)

    own, own_rest, near = terms[0], terms[1], terms[-1]
    far_rest, far = terms[2:pool], terms[pool:-1]
    first_cols, cols = own.shape[1], near.shape[1]

    def total(at):
        if at < first_cols:
            got, others = own[:, at : at + HD], far
        else:
            got, others = own_rest[:, at - first_cols : at - first_cols + HD], far_rest
        got = got.astype(jnp.float32) + near[:, at : at + HD].astype(jnp.float32)
        at = at if at < first_cols else at - first_cols
        for part in others:
            got = got + part[:, at : at + HD].astype(jnp.float32)
        return got

    late = first_cols + 2 * kv_heads * HD
    heads = [*range(0, first_cols - HD, HD), *range(late, cols, HD)]
    power = jnp.sum(total(first_cols - HD), axis=1, keepdims=True)
    factor = lax.rsqrt(power * (1.0 / width_d) + EPS)
    cosines, sines = cos[...], sin[...]

    def rounded(x):
        return x.astype(jnp.bfloat16).astype(jnp.float32)

    def rotated(x):
        return rounded(x * cosines + pltpu.roll(x, HD // 2, axis=1) * sines)

    for i in range(q_heads):
        q_buf[i * per : (i + 1) * per, :] = rotated(total(heads[i]) * factor)
    keys_own = [rotated(total(first_cols + g * HD) * factor) for g in range(kv_heads)]
    values_own = [
        rounded(total(first_cols + (kv_heads + g) * HD) * factor) for g in range(kv_heads)
    ]

    me = me_ref[0]

    def base(j):
        return pl.multiple_of(partner(me, j) * (slots * seg), slots * seg)

    lane = lax.broadcasted_iota(jnp.int32, (1, HD), 1)
    slot_of = lane // group
    at = lax.broadcasted_iota(jnp.int32, (seg, HD), 0)
    at_own = lax.broadcasted_iota(jnp.int32, (step, HD), 0)
    blocks = [(g, s) for s in range(0, per, step) for g in range(kv_heads)]
    columns = []
    for g, s in blocks:
        query = jnp.concatenate(
            [q_buf[pl.ds(g * group * per + s + u, group, stride=per), :] for u in range(step)], 0
        )
        columns.append(query.T.astype(jnp.bfloat16))
    scores = []
    for (g, s), query in zip(blocks, columns):
        score = None
        for u in range(0, step, slots):
            wide = jnp.dot(
                keys[pl.ds(base((s + u) // slots), slots * seg), g * HD : (g + 1) * HD],
                query,
                preferred_element_type=jnp.float32,
            )
            for c in range(slots):
                each = wide[c * seg : (c + 1) * seg]
                score = each if score is None else jnp.where(slot_of == u + c, each, score)
        own = jnp.dot(
            keys_own[g][s : s + step].astype(jnp.bfloat16),
            query,
            preferred_element_type=jnp.float32,
        )
        own = jnp.sum(jnp.where(at_own == slot_of, own, 0.0), axis=0, keepdims=True)
        scores.append((score * scale, own * scale))
    turned, levels = [], {}
    for (g, s), (score, own) in zip(blocks, scores):
        length = marks[0:1, s * group : s * group + HD]
        with_own = marks[1:2, s * group : s * group + HD] > 0
        usable = at < length
        own = jnp.where(with_own, own, LOW)
        top = jnp.maximum(jnp.max(jnp.where(usable, score, LOW), axis=0, keepdims=True), own)
        weight = jnp.where(usable, jnp.exp(score - top), 0.0)
        weight_own = jnp.where(with_own, jnp.exp(own - top), 0.0)
        sums = jnp.sum(weight, axis=0, keepdims=True) + weight_own
        sums = jnp.where(length > 0, sums, 1.0)
        level = top + jnp.log(sums)
        for u in range(0, step, slots):
            at_lane = g * slots * group
            moved = level if at_lane == u * group else pltpu.roll(level, (at_lane - u * group) % HD, axis=1)
            there = (lane >= at_lane) & (lane < at_lane + slots * group)
            home = (s + u) // slots
            levels[home] = jnp.where(there, moved, levels.get(home, 0.0))
        rows = [weight_own, 1.0 / sums, jnp.zeros((HD - seg - 2, HD), jnp.float32)]
        turned.append(jnp.concatenate([weight] + rows, 0).T)
    for (g, s), block in zip(blocks, turned):
        for u in range(step):
            home, c = (s + u) // slots, (s + u) % slots
            rows = block[u * group : (u + 1) * group]
            mixed = jnp.dot(
                rows[:, :seg].astype(jnp.bfloat16),
                values[pl.ds(base(home) + c * seg, seg), g * HD : (g + 1) * HD],
                preferred_element_type=jnp.float32,
            )
            mixed = mixed + rows[:, seg : seg + 1] * values_own[g][s + u : s + u + 1]
            to = c * q_heads + g * group
            outs[home][to : to + group, :] = (mixed * rows[:, seg + 1 : seg + 2]).astype(jnp.bfloat16)
    for home, level in levels.items():
        block = jnp.concatenate([*split3(level), jnp.zeros((LEVELS - 3, HD), jnp.float32)], 0)
        outs[home][slots * q_heads :, :] = block.astype(jnp.bfloat16)


def merge_kernel(pool, slots, rows_local, q_heads, kv_heads, slots_ref, rows_ref, own, *rest):
    found, (out, scaled) = [own, rest[pool - 2], *rest[: pool - 2]], rest[pool - 1 :]
    per = pool * slots
    group = q_heads // kv_heads
    block = slots * q_heads
    span = slots * group
    level = jnp.concatenate(
        [jnp.sum(part[block : block + LEVELS, :].astype(jnp.float32), 0, keepdims=True) for part in found], 0
    )
    named = rows_ref[...]
    lane = lax.broadcasted_iota(jnp.int32, (pool, HD), 1)

    def turns(x):
        for c in range(slots):
            y = x
            if c:
                y = jnp.where(
                    lax.rem(lane, span) < span - c * group,
                    pltpu.roll(x, HD - c * group, axis=1),
                    pltpu.roll(x, span - c * group, axis=1),
                )
            for k in range(pool):
                yield jnp.concatenate([y[k:], y[:k]], 0) if k else y

    same = [other == named for other in turns(named)]
    top = level
    for match, other in zip(same, turns(level)):
        top = jnp.maximum(top, jnp.where(match, other, LOW))
    weight = jnp.exp(level - top)
    total = jnp.zeros_like(weight)
    for match, other in zip(same, turns(weight)):
        total = total + jnp.where(match, other, 0.0)
    share = jnp.where(named >= 0, weight / total, 0.0)
    share = jnp.concatenate([share, jnp.zeros((HD - pool, HD), jnp.float32)], 0).T
    for k in range(pool):
        for c in range(slots):
            for g in range(kv_heads):
                at = c * q_heads + g * group
                each = g * span + c * group
                scaled[k * block + at : k * block + at + group, :] = (
                    found[k][at : at + group, :].astype(jnp.float32)
                    * share[each : each + group, k : k + 1]
                )
    row = lax.broadcasted_iota(jnp.int32, (rows_local, 2 * per), 0)
    match = (slots_ref[:, : 2 * per] == row).astype(jnp.float32).astype(jnp.bfloat16)
    for i in range(q_heads):
        part = scaled[pl.ds(i, per, stride=q_heads), :]
        high = part.astype(jnp.bfloat16)
        low = (part - high.astype(jnp.float32)).astype(jnp.bfloat16)
        out[:, i * HD : (i + 1) * HD] = jnp.dot(
            match, jnp.concatenate([high, low], 0), preferred_element_type=jnp.float32
        ).astype(jnp.bfloat16)


def exchange(parts, order):
    got = list(parts)
    for k in order:
        got[k] = lax.ppermute(parts[k], "pool", [(i, i ^ k) for i in range(len(parts))])
    return got


def in_hbm(x):
    return pltpu.with_memory_space_constraint(x, pltpu.HBM)


SMEM = pl.BlockSpec(memory_space=pltpu.SMEM)
VMEM = pl.BlockSpec(memory_space=pltpu.VMEM)
HBM = pl.BlockSpec(memory_space=pltpu.HBM)


def body(
    hidden_in,
    norm_gain,
    w_query,
    w_key,
    w_value,
    cache_keys,
    cache_values,
    send_row,
    piece_len,
    row_len,
):
    pool = lax.axis_size("pool")
    me = lax.axis_index("pool").astype(jnp.int32)
    n_rows, depth = hidden_in.shape
    width_d = depth * pool
    rows_local = n_rows // pool
    slots = send_row.shape[2]
    per = pool * slots
    seg = cache_keys.shape[0] // per
    q_cols, kv_cols = w_query.shape[1], w_key.shape[1]
    q_heads, kv_heads = q_cols // HD, kv_cols // HD
    group = q_heads // kv_heads
    cols = q_cols + 2 * kv_cols + HD

    if pool <= 8:
        indices = [send_row, piece_len, row_len]
    else:
        indices = [send_row.reshape(-1), piece_len.reshape(-1), row_len]
    deep = divides(depth, DEEP)
    count = depth // deep
    widths = [11 * q_cols // 16, 5 * q_cols // 16]

    def parts(width):
        return [jax.ShapeDtypeStruct((per, width), jnp.bfloat16)] * pool

    operands = [in_hbm(x) for x in (*indices, hidden_in, norm_gain, w_query, w_key, w_value)]
    *first_terms, lhs, pick, positions, marks, home_rows, home_slots = pl.pallas_call(
        functools.partial(project_kernel, pool, slots, rows_local),
        out_shape=[
            *parts(widths[0] + HD),
            jax.ShapeDtypeStruct((count, n_rows, deep), jnp.bfloat16),
            jax.ShapeDtypeStruct((pool * per, n_rows), jnp.float32),
            jax.ShapeDtypeStruct((per, HD), jnp.float32),
            jax.ShapeDtypeStruct((2, per * group), jnp.int32),
            jax.ShapeDtypeStruct((pool, HD), jnp.int32),
            jax.ShapeDtypeStruct((1, HD), jnp.int32),
        ],
        in_specs=[SMEM] + [HBM] * 6,
        out_specs=[VMEM] * (pool + 6),
        scratch_shapes=[
            *(pltpu.SMEM(x.shape, jnp.int32) for x in indices),
            pltpu.VMEM((n_rows, depth), jnp.bfloat16),
            pltpu.VMEM((depth,), jnp.bfloat16),
            pltpu.VMEM((count, deep, widths[0]), jnp.bfloat16),
            pltpu.VMEM((n_rows, widths[0]), jnp.float32),
            pltpu.VMEM((n_rows, HD), jnp.float32),
            pltpu.SemaphoreType.DMA((5,)),
            pltpu.SemaphoreType.DMA((count,)),
        ],
        compiler_params=pltpu.CompilerParams(vmem_limit_bytes=46 * 2**20),
        name="project",
    )(me[None], *operands[:6])
    rest_cols = 2 * kv_cols + widths[1]
    rest_shapes = parts(rest_cols)
    rest_shapes[1] = jax.ShapeDtypeStruct((per, widths[0] + HD + rest_cols), jnp.bfloat16)
    rest_terms = pl.pallas_call(
        functools.partial(project_rest_kernel, pool, widths[0]),
        out_shape=rest_shapes,
        in_specs=[VMEM] * 3 + [HBM] * 3,
        out_specs=[VMEM] * pool,
        scratch_shapes=[
            pltpu.VMEM((1, depth, kv_cols), jnp.bfloat16),
            pltpu.VMEM((1, depth, kv_cols), jnp.bfloat16),
            pltpu.VMEM((count, deep, widths[1]), jnp.bfloat16),
            pltpu.VMEM((n_rows, rest_cols), jnp.float32),
            pltpu.SemaphoreType.DMA((count + 2,)),
        ],
        compiler_params=pltpu.CompilerParams(vmem_limit_bytes=40 * 2**20),
        cost_estimate=pl.CostEstimate(
            flops=2 * n_rows * depth * rest_cols,
            bytes_accessed=2 * depth * (rest_cols + n_rows),
            transcendentals=0,
        ),
        name="project_rest",
    )(lhs, pick, first_terms[1], operands[6], operands[7], operands[5])
    first_terms = exchange(first_terms, range(2, pool))
    rest_terms = list(rest_terms)
    early, late = range(2, pool), range(3, pool)
    got, tied = lax.optimization_barrier(
        ([first_terms[k] for k in early], [rest_terms[k] for k in late])
    )
    for k, part in zip(early, got):
        first_terms[k] = part
    for k, part in zip(late, tied):
        rest_terms[k] = part
    rest_terms = exchange(rest_terms, range(1, pool))
    terms = [first_terms[0], rest_terms[0], *rest_terms[2:], *first_terms[2:], rest_terms[1]]

    half = HD // 2
    freq = THETA ** (-(np.arange(half) * 2.0) / HD)
    angles = positions * np.concatenate([freq, freq]).astype(np.float32)[None, :]
    sign = np.concatenate([-np.ones(half), np.ones(half)]).astype(np.float32)[None, :]
    cosines, sines = jnp.cos(angles), jnp.sin(angles) * sign

    found = pl.pallas_call(
        functools.partial(attend_kernel, pool, slots, seg, width_d, q_heads, kv_heads),
        out_shape=[jax.ShapeDtypeStruct((slots * q_heads + LEVELS, HD), jnp.bfloat16)] * pool,
        in_specs=[SMEM] + [VMEM] * (2 * pool + 4),
        out_specs=[VMEM] * pool,
        scratch_shapes=[pltpu.VMEM((q_heads * per, HD), jnp.float32)],
        compiler_params=pltpu.CompilerParams(vmem_limit_bytes=24 * 2**20),
        name="attend",
    )(me[None], *terms, cosines, sines, marks, cache_keys, cache_values)

    found = exchange(found, [*range(2, pool), 1])

    return pl.pallas_call(
        functools.partial(merge_kernel, pool, slots, rows_local, q_heads, kv_heads),
        out_shape=jax.ShapeDtypeStruct((rows_local, q_cols), jnp.bfloat16),
        in_specs=[VMEM] * (2 + pool),
        out_specs=VMEM,
        scratch_shapes=[
            pltpu.VMEM((per * q_heads, HD), jnp.float32),
        ],
        compiler_params=pltpu.CompilerParams(vmem_limit_bytes=24 * 2**20),
        name="merge",
    )(home_slots, home_rows, found[0], *found[2:], found[1])


def solution(mesh):
    return jax.shard_map(
        body,
        mesh=mesh,
        in_specs=(
            P("groups", "pool"),
            P("pool"),
            P("pool", "tensor"),
            P("pool", "tensor"),
            P("pool", "tensor"),
            P(("groups", "pool"), "tensor"),
            P(("groups", "pool"), "tensor"),
            P("groups", None, None),
            P(("groups", "pool"), None, None),
            P("groups"),
        ),
        out_specs=P(("groups", "pool"), "tensor"),
        check_vma=False,
    )
```

```python
import functools

import jax
import jax.numpy as jnp
import numpy as np
from jax import lax
from jax.experimental import pallas as pl
from jax.experimental.pallas import tpu as pltpu
from jax.sharding import PartitionSpec as P

HD = 128
EPS = 1e-05
THETA = 500000.0
LOW = -1e30
DEEP = 512
LEVELS = 16


def divides(width, limit):
    while width % limit:
        limit //= 2
    return limit


def split3(x):
    a = x.astype(jnp.bfloat16).astype(jnp.float32)
    r = x - a
    b = r.astype(jnp.bfloat16).astype(jnp.float32)
    return a, b, (r - b).astype(jnp.bfloat16).astype(jnp.float32)


def partner(me, k):
    return lax.bitwise_xor(me, k)


def stream(count, pieces, following, ahead):
    def begin():
        for t in range(min(ahead, count)):
            for copy in pieces(t):
                copy.start()
        for copy in following[: max(ahead - count, 0)]:
            copy.start()

    def advance(t):
        @pl.when(t + ahead < count)
        def _():
            for copy in pieces(t + ahead):
                copy.start()

        for j, copy in enumerate(following):
            pl.when(t + ahead == count + j)(copy.start)

    return begin, advance


def add_products(left, block, sums):
    width = block.shape[1]
    tile = divides(width, 512)
    for at in range(0, width, tile):
        sums[:, at : at + tile] += jnp.dot(
            left, block[:, at : at + tile], preferred_element_type=jnp.float32
        )


def spread(chosen, sums, outs, at):
    width = sums.shape[1]
    per = chosen.shape[0] // len(outs)
    rows = jnp.dot(
        chosen, sums.astype(jnp.bfloat16), preferred_element_type=jnp.float32
    ).astype(jnp.bfloat16)
    for k, out in enumerate(outs):
        out[:, at : at + width] = rows[k * per : (k + 1) * per]


def spread_products(chosen, left, block, sums, outs, to):
    width = block.shape[1]
    tile = divides(width, 512)
    for at in range(0, width, tile):
        done = sums[:, at : at + tile] + jnp.dot(
            left, block[:, at : at + tile], preferred_element_type=jnp.float32
        )
        spread(chosen, done, outs, to + at)


def project_kernel(pool, slots, rows_local, me_ref, send, lens, row_len, hidden, gain, *rest):
    w_query, *rest = rest
    outs, rest = rest[:pool], rest[pool:]
    lhs, pick, positions, marks, home_rows, home_slots, *rest = rest
    send_buf, lens_buf, row_len_buf, x_buf, g_buf, *rest = rest
    *bufs, sums, squares, in_sem, sems = rest
    per = pool * slots
    n_rows, depth = x_buf.shape
    count, deep, _ = bufs[0].shape
    me = me_ref[0]

    def named(home, owner, c):
        if len(send_buf.shape) == 3:
            return send_buf[home, owner, c]
        return send_buf[home * per + owner * slots + c]

    lane = lax.broadcasted_iota(jnp.int32, (1, n_rows), 1)
    place = lax.broadcasted_iota(jnp.int32, (1, HD), 1)
    group = marks.shape[1] // per
    slot_of = lax.broadcasted_iota(jnp.int32, (1, marks.shape[1]), 1) // group

    def choose(i):
        owner = partner(me, i // per)
        s = lax.rem(i, per)
        home = partner(owner, s // slots)
        r = named(home, owner, lax.rem(s, slots))
        row = jnp.where(r >= 0, home * rows_local + r, -1)
        pick[pl.ds(i, 1), :] = (lane == row).astype(jnp.float32)

    def describe(s):
        k, c = s // slots, lax.rem(s, slots)
        home = partner(me, k)
        r = named(home, me, c)
        at = row_len_buf[home * rows_local + jnp.maximum(r, 0)].astype(jnp.float32)
        positions[pl.ds(s, 1), :] = jnp.full((1, HD), at, jnp.float32)
        length = lens_buf[0, home, c] if len(lens_buf.shape) == 3 else lens_buf[home * slots + c]
        earlier = jnp.int32(0)
        for e in range(per):
            same = (named(home, e // slots, e % slots) == r) & (e < me * slots + c)
            earlier = earlier | same.astype(jnp.int32)
        first = jnp.where((earlier == 0) & (r >= 0), 1, 0)
        marks[0:1, :] = jnp.where(slot_of == s, length, marks[0:1, :])
        marks[1:2, :] = jnp.where(slot_of == s, first, marks[1:2, :])
        mine = named(me, home, c)
        home_slots[...] = jnp.where(lax.rem(place, per) == s, mine, home_slots[...])
        home_rows[pl.ds(k, 1), :] = jnp.where(
            lax.rem(place // group, slots) == c, mine, home_rows[pl.ds(k, 1), :]
        )

    chore_steps = max(count // 2, 1)

    def each(do, total, t):
        share = -(-total // chore_steps)
        if share <= 16 and total % chore_steps == 0:
            for q in range(share):
                do(t * share + q)
        else:

            @pl.when(t == 0)
            def _():
                def one(i, carry):
                    do(i)
                    return carry

                lax.fori_loop(0, total, one, 0)

    def scale(t):
        at = pl.multiple_of(t * deep, deep)
        x = x_buf[:, pl.ds(at, deep)].astype(jnp.float32)
        gains = g_buf[pl.ds(at, deep)].astype(jnp.float32).reshape(1, deep)
        left = (x * gains).astype(jnp.bfloat16)
        lhs[t] = left
        squared = x * x
        total = squares[...]
        for column in range(0, deep, HD):
            total = total + squared[:, column : column + HD]
        squares[...] = total
        return left

    starts = [sum(buf.shape[2] for buf in bufs[:n]) for n in range(len(bufs))]

    def pieces(t):
        rows = pl.ds(pl.multiple_of(t * deep, deep), deep)
        return [
            pltpu.make_async_copy(
                w_query.at[rows, start : start + buf.shape[2]], buf.at[t], sems.at[n, t]
            )
            for n, (buf, start) in enumerate(zip(bufs, starts))
        ]

    begin, advance = stream(count, pieces, [], 2)

    def use(t):
        advance(t)
        left = scale(t)
        for copy, buf, start in zip(pieces(t), bufs, starts):
            copy.wait()
            add_products(left, buf.at[t], sums.at[:, start : start + buf.shape[2]])

    def use_early(t):
        use(t)
        each(choose, pool * per, t)
        each(describe, per, t)

    def use_last(t):
        left = scale(t)
        if count == 1:
            each(choose, pool * per, t)
            each(describe, per, t)
        chosen = pick[...].astype(jnp.bfloat16)
        for copy, buf, start in zip(pieces(t), bufs, starts):
            copy.wait()
            part = sums.at[:, start : start + buf.shape[2]]
            spread_products(chosen, left, buf.at[t], part, outs, start)
        power = jnp.sum(squares[...], axis=1, keepdims=True)
        at = lax.broadcasted_iota(jnp.int32, (n_rows, HD), 1)
        a, b, c = split3(power)
        parts = jnp.where(at == 0, a, jnp.where(at == 1, b, jnp.where(at == 2, c, 0.0)))
        spread(chosen, parts, outs, sums.shape[1])

    inputs = [
        pltpu.make_async_copy(source, target, in_sem.at[i])
        for i, (source, target) in enumerate(
            (
                (gain, g_buf),
                (hidden, x_buf),
                (send, send_buf),
                (lens, lens_buf),
                (row_len, row_len_buf),
            )
        )
    ]
    for one in inputs:
        one.start()
    begin()
    sums[...] = jnp.zeros(sums.shape, jnp.float32)
    squares[...] = jnp.zeros((n_rows, HD), jnp.float32)
    marks[...] = jnp.zeros(marks.shape, jnp.int32)
    home_rows[...] = jnp.full(home_rows.shape, -1, jnp.int32)
    home_slots[...] = jnp.full(home_slots.shape, -1, jnp.int32)
    for one in inputs:
        one.wait()
    early = min(chore_steps, count - 1)
    pl.loop(0, early)(use_early)
    pl.loop(early, count - 1)(use)
    use_last(count - 1)


def project_rest_kernel(pool, column, lhs, pick, near, w_key, w_value, w_query, *rest):
    outs, (query_buf, key_buf, value_buf, sums, sems) = rest[:pool], rest[pool:]
    done = near.shape[1]
    count, _, deep = lhs.shape
    halves, tall, kv_cols = key_buf.shape
    chosen = pick[...].astype(jnp.bfloat16)
    targets = [out.at[:, done:] if k == 1 else out for k, out in enumerate(outs)]

    def pieces(t):
        rows = pl.ds(pl.multiple_of(t * deep, deep), deep)
        block = w_query.at[rows, column : column + query_buf.shape[2]]
        return [pltpu.make_async_copy(block, query_buf.at[t], sems.at[t])]

    narrow = [(n, half) for n in range(2) for half in range(halves)]
    following = [
        pltpu.make_async_copy(
            (w_key, w_value)[n].at[half * tall : (half + 1) * tall, :],
            (key_buf, value_buf)[n].at[half],
            sems.at[count + n * halves + half],
        )
        for n, half in narrow
    ]
    begin, advance = stream(count, pieces, following, 4)
    begin()
    sums[...] = jnp.zeros(sums.shape, jnp.float32)
    outs[1][:, :done] = near[...]

    @pl.loop(0, count - 1)
    def _(t):
        advance(t)
        pieces(t)[0].wait()
        add_products(lhs[t], query_buf.at[t], sums)

    advance(count - 1)
    pieces(count - 1)[0].wait()
    spread_products(chosen, lhs[count - 1], query_buf.at[count - 1], sums, targets, 2 * kv_cols)
    part = 0.0
    for (n, half), copy in zip(narrow, following):
        copy.wait()
        for k in range(tall // deep):
            part = part + jnp.dot(
                lhs[half * (tall // deep) + k],
                (key_buf, value_buf)[n][half, k * deep : (k + 1) * deep, :],
                preferred_element_type=jnp.float32,
            )
        if half == halves - 1:
            spread(chosen, part, targets, n * kv_cols)
            part = 0.0


def attend_kernel(pool, slots, seg, width_d, q_heads, kv_heads, me_ref, *rest):
    terms, rest = rest[: 2 * pool - 1], rest[2 * pool - 1 :]
    cos, sin, marks, keys, values = rest[:5]
    outs, (q_buf,) = rest[5 : 5 + pool], rest[5 + pool :]
    per = pool * slots
    group = q_heads // kv_heads
    step = HD // group
    scale = HD ** (-0.5)

    own, own_rest, near = terms[0], terms[1], terms[-1]
    far_rest, far = terms[2:pool], terms[pool:-1]
    first_cols, cols = own.shape[1], near.shape[1]

    def total(at):
        if at < first_cols:
            got, others = own[:, at : at + HD], far
        else:
            got, others = own_rest[:, at - first_cols : at - first_cols + HD], far_rest
        got = got.astype(jnp.float32) + near[:, at : at + HD].astype(jnp.float32)
        at = at if at < first_cols else at - first_cols
        for part in others:
            got = got + part[:, at : at + HD].astype(jnp.float32)
        return got

    late = first_cols + 2 * kv_heads * HD
    heads = [*range(0, first_cols - HD, HD), *range(late, cols, HD)]
    power = jnp.sum(total(first_cols - HD), axis=1, keepdims=True)
    factor = lax.rsqrt(power * (1.0 / width_d) + EPS)
    cosines, sines = cos[...], sin[...]

    def rounded(x):
        return x.astype(jnp.bfloat16).astype(jnp.float32)

    def rotated(x):
        return rounded(x * cosines + pltpu.roll(x, HD // 2, axis=1) * sines)

    for i in range(q_heads):
        q_buf[i * per : (i + 1) * per, :] = rotated(total(heads[i]) * factor)
    keys_own = [rotated(total(first_cols + g * HD) * factor) for g in range(kv_heads)]
    values_own = [
        rounded(total(first_cols + (kv_heads + g) * HD) * factor) for g in range(kv_heads)
    ]

    me = me_ref[0]

    def base(j):
        return pl.multiple_of(partner(me, j) * (slots * seg), slots * seg)

    lane = lax.broadcasted_iota(jnp.int32, (1, HD), 1)
    slot_of = lane // group
    at = lax.broadcasted_iota(jnp.int32, (seg, HD), 0)
    at_own = lax.broadcasted_iota(jnp.int32, (step, HD), 0)
    blocks = [(g, s) for s in range(0, per, step) for g in range(kv_heads)]
    columns = []
    for g, s in blocks:
        query = jnp.concatenate(
            [q_buf[pl.ds(g * group * per + s + u, group, stride=per), :] for u in range(step)], 0
        )
        columns.append(query.T.astype(jnp.bfloat16))
    scores = []
    for (g, s), query in zip(blocks, columns):
        score = None
        for u in range(0, step, slots):
            wide = jnp.dot(
                keys[pl.ds(base((s + u) // slots), slots * seg), g * HD : (g + 1) * HD],
                query,
                preferred_element_type=jnp.float32,
            )
            for c in range(slots):
                each = wide[c * seg : (c + 1) * seg]
                score = each if score is None else jnp.where(slot_of == u + c, each, score)
        own = jnp.dot(
            keys_own[g][s : s + step].astype(jnp.bfloat16),
            query,
            preferred_element_type=jnp.float32,
        )
        own = jnp.sum(jnp.where(at_own == slot_of, own, 0.0), axis=0, keepdims=True)
        scores.append((score * scale, own * scale))
    turned, levels = [], {}
    for (g, s), (score, own) in zip(blocks, scores):
        length = marks[0:1, s * group : s * group + HD]
        with_own = marks[1:2, s * group : s * group + HD] > 0
        usable = at < length
        own = jnp.where(with_own, own, LOW)
        top = jnp.maximum(jnp.max(jnp.where(usable, score, LOW), axis=0, keepdims=True), own)
        weight = jnp.where(usable, jnp.exp(score - top), 0.0)
        weight_own = jnp.where(with_own, jnp.exp(own - top), 0.0)
        sums = jnp.sum(weight, axis=0, keepdims=True) + weight_own
        sums = jnp.where(length > 0, sums, 1.0)
        level = top + jnp.log(sums)
        for u in range(0, step, slots):
            at_lane = g * slots * group
            moved = level if at_lane == u * group else pltpu.roll(level, (at_lane - u * group) % HD, axis=1)
            there = (lane >= at_lane) & (lane < at_lane + slots * group)
            home = (s + u) // slots
            levels[home] = jnp.where(there, moved, levels.get(home, 0.0))
        rows = [weight_own, 1.0 / sums, jnp.zeros((HD - seg - 2, HD), jnp.float32)]
        turned.append(jnp.concatenate([weight] + rows, 0).T)
    for (g, s), block in zip(blocks, turned):
        for u in range(step):
            home, c = (s + u) // slots, (s + u) % slots
            rows = block[u * group : (u + 1) * group]
            mixed = jnp.dot(
                rows[:, :seg].astype(jnp.bfloat16),
                values[pl.ds(base(home) + c * seg, seg), g * HD : (g + 1) * HD],
                preferred_element_type=jnp.float32,
            )
            mixed = mixed + rows[:, seg : seg + 1] * values_own[g][s + u : s + u + 1]
            to = c * q_heads + g * group
            outs[home][to : to + group, :] = (mixed * rows[:, seg + 1 : seg + 2]).astype(jnp.bfloat16)
    for home, level in levels.items():
        block = jnp.concatenate([*split3(level), jnp.zeros((LEVELS - 3, HD), jnp.float32)], 0)
        outs[home][slots * q_heads :, :] = block.astype(jnp.bfloat16)


def merge_kernel(pool, slots, rows_local, q_heads, kv_heads, slots_ref, rows_ref, own, *rest):
    found, (out, scaled) = [own, rest[pool - 2], *rest[: pool - 2]], rest[pool - 1 :]
    per = pool * slots
    group = q_heads // kv_heads
    block = slots * q_heads
    span = slots * group
    level = jnp.concatenate(
        [jnp.sum(part[block : block + LEVELS, :].astype(jnp.float32), 0, keepdims=True) for part in found], 0
    )
    named = rows_ref[...]
    lane = lax.broadcasted_iota(jnp.int32, (pool, HD), 1)

    def turns(x):
        for c in range(slots):
            y = x
            if c:
                y = jnp.where(
                    lax.rem(lane, span) < span - c * group,
                    pltpu.roll(x, HD - c * group, axis=1),
                    pltpu.roll(x, span - c * group, axis=1),
                )
            for k in range(pool):
                yield jnp.concatenate([y[k:], y[:k]], 0) if k else y

    same = [other == named for other in turns(named)]
    top = level
    for match, other in zip(same, turns(level)):
        top = jnp.maximum(top, jnp.where(match, other, LOW))
    weight = jnp.exp(level - top)
    total = jnp.zeros_like(weight)
    for match, other in zip(same, turns(weight)):
        total = total + jnp.where(match, other, 0.0)
    share = jnp.where(named >= 0, weight / total, 0.0)
    share = jnp.concatenate([share, jnp.zeros((HD - pool, HD), jnp.float32)], 0).T
    for k in range(pool):
        for c in range(slots):
            for g in range(kv_heads):
                at = c * q_heads + g * group
                each = g * span + c * group
                scaled[k * block + at : k * block + at + group, :] = (
                    found[k][at : at + group, :].astype(jnp.float32)
                    * share[each : each + group, k : k + 1]
                )
    row = lax.broadcasted_iota(jnp.int32, (rows_local, 2 * per), 0)
    match = (slots_ref[:, : 2 * per] == row).astype(jnp.float32).astype(jnp.bfloat16)
    for i in range(q_heads):
        part = scaled[pl.ds(i, per, stride=q_heads), :]
        high = part.astype(jnp.bfloat16)
        low = (part - high.astype(jnp.float32)).astype(jnp.bfloat16)
        out[:, i * HD : (i + 1) * HD] = jnp.dot(
            match, jnp.concatenate([high, low], 0), preferred_element_type=jnp.float32
        ).astype(jnp.bfloat16)


def exchange(parts, order):
    got = list(parts)
    for k in order:
        got[k] = lax.ppermute(parts[k], "pool", [(i, i ^ k) for i in range(len(parts))])
    return got


def in_hbm(x):
    return pltpu.with_memory_space_constraint(x, pltpu.HBM)


SMEM = pl.BlockSpec(memory_space=pltpu.SMEM)
VMEM = pl.BlockSpec(memory_space=pltpu.VMEM)
HBM = pl.BlockSpec(memory_space=pltpu.HBM)


def body(
    hidden_in,
    norm_gain,
    w_query,
    w_key,
    w_value,
    cache_keys,
    cache_values,
    send_row,
    piece_len,
    row_len,
):
    pool = lax.axis_size("pool")
    me = lax.axis_index("pool").astype(jnp.int32)
    n_rows, depth = hidden_in.shape
    width_d = depth * pool
    rows_local = n_rows // pool
    slots = send_row.shape[2]
    per = pool * slots
    seg = cache_keys.shape[0] // per
    q_cols, kv_cols = w_query.shape[1], w_key.shape[1]
    q_heads, kv_heads = q_cols // HD, kv_cols // HD
    group = q_heads // kv_heads
    cols = q_cols + 2 * kv_cols + HD

    if pool <= 8:
        indices = [send_row, piece_len, row_len]
    else:
        indices = [send_row.reshape(-1), piece_len.reshape(-1), row_len]
    deep = divides(depth, DEEP)
    count = depth // deep
    widths = [11 * q_cols // 16, 5 * q_cols // 16]

    left_cols = -(-widths[0] // 512) * 256
    halves = 2 if count % 2 == 0 else 1

    def parts(width):
        return [jax.ShapeDtypeStruct((per, width), jnp.bfloat16)] * pool

    operands = [in_hbm(x) for x in (*indices, hidden_in, norm_gain, w_query, w_key, w_value)]
    *first_terms, lhs, pick, positions, marks, home_rows, home_slots = pl.pallas_call(
        functools.partial(project_kernel, pool, slots, rows_local),
        out_shape=[
            *parts(widths[0] + HD),
            jax.ShapeDtypeStruct((count, n_rows, deep), jnp.bfloat16),
            jax.ShapeDtypeStruct((pool * per, n_rows), jnp.float32),
            jax.ShapeDtypeStruct((per, HD), jnp.float32),
            jax.ShapeDtypeStruct((2, per * group), jnp.int32),
            jax.ShapeDtypeStruct((pool, HD), jnp.int32),
            jax.ShapeDtypeStruct((1, HD), jnp.int32),
        ],
        in_specs=[SMEM] + [HBM] * 6,
        out_specs=[VMEM] * (pool + 6),
        scratch_shapes=[
            *(pltpu.SMEM(x.shape, jnp.int32) for x in indices),
            pltpu.VMEM((n_rows, depth), jnp.bfloat16),
            pltpu.VMEM((depth,), jnp.bfloat16),
            pltpu.VMEM((count, deep, left_cols), jnp.bfloat16),
            pltpu.VMEM((count, deep, widths[0] - left_cols), jnp.bfloat16),
            pltpu.VMEM((n_rows, widths[0]), jnp.float32),
            pltpu.VMEM((n_rows, HD), jnp.float32),
            pltpu.SemaphoreType.DMA((5,)),
            pltpu.SemaphoreType.DMA((2, count)),
        ],
        compiler_params=pltpu.CompilerParams(vmem_limit_bytes=46 * 2**20),
        name="project",
    )(me[None], *operands[:6])
    rest_cols = 2 * kv_cols + widths[1]
    rest_shapes = parts(rest_cols)
    rest_shapes[1] = jax.ShapeDtypeStruct((per, widths[0] + HD + rest_cols), jnp.bfloat16)
    rest_terms = pl.pallas_call(
        functools.partial(project_rest_kernel, pool, widths[0]),
        out_shape=rest_shapes,
        in_specs=[VMEM] * 3 + [HBM] * 3,
        out_specs=[VMEM] * pool,
        scratch_shapes=[
            pltpu.VMEM((count, deep, widths[1]), jnp.bfloat16),
            pltpu.VMEM((halves, depth // halves, kv_cols), jnp.bfloat16),
            pltpu.VMEM((halves, depth // halves, kv_cols), jnp.bfloat16),
            pltpu.VMEM((n_rows, widths[1]), jnp.float32),
            pltpu.SemaphoreType.DMA((count + 2 * halves,)),
        ],
        compiler_params=pltpu.CompilerParams(vmem_limit_bytes=40 * 2**20),
        cost_estimate=pl.CostEstimate(
            flops=2 * n_rows * depth * rest_cols,
            bytes_accessed=2 * depth * (rest_cols + n_rows),
            transcendentals=0,
        ),
        name="project_rest",
    )(lhs, pick, first_terms[1], operands[6], operands[7], operands[5])
    first_terms = exchange(first_terms, range(2, pool))
    rest_terms = list(rest_terms)
    early, late = range(2, pool), range(3, pool)
    got, tied = lax.optimization_barrier(
        ([first_terms[k] for k in early], [rest_terms[k] for k in late])
    )
    for k, part in zip(early, got):
        first_terms[k] = part
    for k, part in zip(late, tied):
        rest_terms[k] = part
    rest_terms = exchange(rest_terms, range(1, pool))
    terms = [first_terms[0], rest_terms[0], *rest_terms[2:], *first_terms[2:], rest_terms[1]]

    half = HD // 2
    freq = THETA ** (-(np.arange(half) * 2.0) / HD)
    angles = positions * np.concatenate([freq, freq]).astype(np.float32)[None, :]
    sign = np.concatenate([-np.ones(half), np.ones(half)]).astype(np.float32)[None, :]
    cosines, sines = jnp.cos(angles), jnp.sin(angles) * sign

    found = pl.pallas_call(
        functools.partial(attend_kernel, pool, slots, seg, width_d, q_heads, kv_heads),
        out_shape=[jax.ShapeDtypeStruct((slots * q_heads + LEVELS, HD), jnp.bfloat16)] * pool,
        in_specs=[SMEM] + [VMEM] * (2 * pool + 4),
        out_specs=[VMEM] * pool,
        scratch_shapes=[pltpu.VMEM((q_heads * per, HD), jnp.float32)],
        compiler_params=pltpu.CompilerParams(vmem_limit_bytes=24 * 2**20),
        name="attend",
    )(me[None], *terms, cosines, sines, marks, cache_keys, cache_values)

    found = exchange(found, [*range(2, pool), 1])

    return pl.pallas_call(
        functools.partial(merge_kernel, pool, slots, rows_local, q_heads, kv_heads),
        out_shape=jax.ShapeDtypeStruct((rows_local, q_cols), jnp.bfloat16),
        in_specs=[VMEM] * (2 + pool),
        out_specs=VMEM,
        scratch_shapes=[
            pltpu.VMEM((per * q_heads, HD), jnp.float32),
        ],
        compiler_params=pltpu.CompilerParams(vmem_limit_bytes=24 * 2**20),
        name="merge",
    )(home_slots, home_rows, found[0], *found[2:], found[1])


def solution(mesh):
    return jax.shard_map(
        body,
        mesh=mesh,
        in_specs=(
            P("groups", "pool"),
            P("pool"),
            P("pool", "tensor"),
            P("pool", "tensor"),
            P("pool", "tensor"),
            P(("groups", "pool"), "tensor"),
            P(("groups", "pool"), "tensor"),
            P("groups", None, None),
            P(("groups", "pool"), None, None),
            P("groups"),
        ),
        out_specs=P(("groups", "pool"), "tensor"),
        check_vma=False,
    )
```

```python
import functools

import jax
import jax.numpy as jnp
import numpy as np
from jax import lax
from jax.experimental import pallas as pl
from jax.experimental.pallas import tpu as pltpu
from jax.sharding import PartitionSpec as P

HD = 128
EPS = 1e-05
THETA = 500000.0
LOW = -1e30
DEEP = 512
LEVELS = 16


def divides(width, limit):
    while width % limit:
        limit //= 2
    return limit


def split3(x):
    a = x.astype(jnp.bfloat16).astype(jnp.float32)
    r = x - a
    b = r.astype(jnp.bfloat16).astype(jnp.float32)
    return a, b, (r - b).astype(jnp.bfloat16).astype(jnp.float32)


def partner(me, k):
    return lax.bitwise_xor(me, k)


def stream(count, pieces, following, ahead):
    def begin():
        for t in range(min(ahead, count)):
            for copy in pieces(t):
                copy.start()
        for copy in following[: max(ahead - count, 0)]:
            copy.start()

    def advance(t):
        @pl.when(t + ahead < count)
        def _():
            for copy in pieces(t + ahead):
                copy.start()

        for j, copy in enumerate(following):
            pl.when(t + ahead == count + j)(copy.start)

    return begin, advance


def add_products(left, block, sums):
    width = block.shape[1]
    tile = divides(width, 512)
    for at in range(0, width, tile):
        sums[:, at : at + tile] += jnp.dot(
            left, block[:, at : at + tile], preferred_element_type=jnp.float32
        )


def spread(chosen, sums, outs, at):
    width = sums.shape[1]
    per = chosen.shape[0] // len(outs)
    rows = jnp.dot(
        chosen, sums.astype(jnp.bfloat16), preferred_element_type=jnp.float32
    ).astype(jnp.bfloat16)
    for k, out in enumerate(outs):
        out[:, at : at + width] = rows[k * per : (k + 1) * per]


def spread_products(chosen, left, block, sums, outs, to):
    width = block.shape[1]
    tile = divides(width, 512)
    for at in range(0, width, tile):
        done = sums[:, at : at + tile] + jnp.dot(
            left, block[:, at : at + tile], preferred_element_type=jnp.float32
        )
        spread(chosen, done, outs, to + at)


def project_kernel(pool, slots, rows_local, me_ref, send, lens, row_len, hidden, gain, *rest):
    w_query, w_key, w_value, *rest = rest
    outs, rest = rest[:pool], rest[pool:]
    lhs, pick, positions, marks, home_rows, home_slots, key_out, value_out, *rest = rest
    send_buf, lens_buf, row_len_buf, x_buf, g_buf, *rest = rest
    query_buf, sums, squares, in_sem, sems = rest
    per = pool * slots
    n_rows, depth = x_buf.shape
    count, deep, width = query_buf.shape
    me = me_ref[0]

    def named(home, owner, c):
        if len(send_buf.shape) == 3:
            return send_buf[home, owner, c]
        return send_buf[home * per + owner * slots + c]

    lane = lax.broadcasted_iota(jnp.int32, (1, n_rows), 1)
    place = lax.broadcasted_iota(jnp.int32, (1, HD), 1)
    group = marks.shape[1] // per
    slot_of = lax.broadcasted_iota(jnp.int32, (1, marks.shape[1]), 1) // group

    def choose(i):
        owner = partner(me, i // per)
        s = lax.rem(i, per)
        home = partner(owner, s // slots)
        r = named(home, owner, lax.rem(s, slots))
        row = jnp.where(r >= 0, home * rows_local + r, -1)
        pick[pl.ds(i, 1), :] = (lane == row).astype(jnp.float32)

    def describe(s):
        k, c = s // slots, lax.rem(s, slots)
        home = partner(me, k)
        r = named(home, me, c)
        at = row_len_buf[home * rows_local + jnp.maximum(r, 0)].astype(jnp.float32)
        positions[pl.ds(s, 1), :] = jnp.full((1, HD), at, jnp.float32)
        length = lens_buf[0, home, c] if len(lens_buf.shape) == 3 else lens_buf[home * slots + c]
        earlier = jnp.int32(0)
        for e in range(per):
            same = (named(home, e // slots, e % slots) == r) & (e < me * slots + c)
            earlier = earlier | same.astype(jnp.int32)
        first = jnp.where((earlier == 0) & (r >= 0), 1, 0)
        marks[0:1, :] = jnp.where(slot_of == s, length, marks[0:1, :])
        marks[1:2, :] = jnp.where(slot_of == s, first, marks[1:2, :])
        mine = named(me, home, c)
        home_slots[...] = jnp.where(lax.rem(place, per) == s, mine, home_slots[...])
        home_rows[pl.ds(k, 1), :] = jnp.where(
            lax.rem(place // group, slots) == c, mine, home_rows[pl.ds(k, 1), :]
        )

    chore_steps = 4
    spread_chores = count > chore_steps + 1 and pool * per <= 64 and per % chore_steps == 0

    def each(do, total, t):
        share = -(-total // chore_steps)
        if spread_chores:
            for q in range(share):
                do(t * share + q)
        else:
            assert isinstance(t, int)
            pl.loop(0, total)(do)

    def scale(t):
        at = pl.multiple_of(t * deep, deep)
        x = x_buf[:, pl.ds(at, deep)].astype(jnp.float32)
        gains = g_buf[pl.ds(at, deep)].astype(jnp.float32).reshape(1, deep)
        left = (x * gains).astype(jnp.bfloat16)
        lhs[t] = left
        squared = x * x
        total = squares[...]
        for column in range(0, deep, HD):
            total = total + squared[:, column : column + HD]
        squares[...] = total
        return left

    cuts = [0, deep // 4, deep // 2, deep] if count > 1 else [0, deep]

    def pieces(t):
        if isinstance(t, int) and t == 0:
            return [
                pltpu.make_async_copy(
                    w_query.at[a:b, :width], query_buf.at[0, a:b], sems.at[0 if n == 0 else count + n]
                )
                for n, (a, b) in enumerate(zip(cuts[:-1], cuts[1:]))
            ]
        rows = pl.ds(pl.multiple_of(t * deep, deep), deep)
        return [pltpu.make_async_copy(w_query.at[rows, :width], query_buf.at[t], sems.at[t])]

    following = [
        pltpu.make_async_copy(w, target, in_sem.at[5 + n])
        for n, (w, target) in enumerate(((w_key, key_out), (w_value, value_out)))
    ]
    begin, advance = stream(count, pieces, following, 3)

    def use(t):
        advance(t)
        left = scale(t)
        for copy in pieces(t):
            copy.wait()
        add_products(left, query_buf.at[t], sums)

    def use_early(t):
        use(t)
        each(choose, pool * per, t - 1)
        each(describe, per, t - 1)

    def use_first():
        advance(0)
        left = scale(0)
        for copy, a, b in zip(pieces(0), cuts[:-1], cuts[1:]):
            copy.wait()
            add_products(left[:, a:b], query_buf.at[0, a:b], sums)

    def use_last(t):
        left = scale(t)
        for copy in pieces(t):
            copy.wait()
        chosen = pick[...].astype(jnp.bfloat16)
        spread_products(chosen, left, query_buf.at[t], sums, outs, 0)
        power = jnp.sum(squares[...], axis=1, keepdims=True)
        at = lax.broadcasted_iota(jnp.int32, (n_rows, HD), 1)
        a, b, c = split3(power)
        parts = jnp.where(at == 0, a, jnp.where(at == 1, b, jnp.where(at == 2, c, 0.0)))
        spread(chosen, parts, outs, sums.shape[1])

    inputs = [
        pltpu.make_async_copy(source, target, in_sem.at[i])
        for i, (source, target) in enumerate(
            (
                (gain, g_buf),
                (hidden, x_buf),
                (send, send_buf),
                (lens, lens_buf),
                (row_len, row_len_buf),
            )
        )
    ]
    for one in inputs:
        one.start()
    begin()
    sums[...] = jnp.zeros(sums.shape, jnp.float32)
    squares[...] = jnp.zeros((n_rows, HD), jnp.float32)
    marks[...] = jnp.zeros(marks.shape, jnp.int32)
    home_rows[...] = jnp.full(home_rows.shape, -1, jnp.int32)
    home_slots[...] = jnp.full(home_slots.shape, -1, jnp.int32)
    for one in inputs:
        one.wait()
    if not spread_chores:
        each(choose, pool * per, 0)
        each(describe, per, 0)
    if count > 1:
        use_first()
    early = 1 + chore_steps if spread_chores else 1
    if spread_chores:
        pl.loop(1, early)(use_early)
    if count > early + 1:
        pl.loop(early, count - 1)(use)
    use_last(count - 1)
    for copy in following:
        copy.wait()


def project_rest_kernel(pool, column, lhs, pick, near, w_key, w_value, w_query, *rest):
    outs, (query_buf, sums, sems) = rest[:pool], rest[pool:]
    done = near.shape[1]
    count, _, deep = lhs.shape
    kv_cols = w_key.shape[1]
    chosen = pick[...].astype(jnp.bfloat16)
    targets = [out.at[:, done:] if k == 1 else out for k, out in enumerate(outs)]

    def pieces(t):
        rows = pl.ds(pl.multiple_of(t * deep, deep), deep)
        block = w_query.at[rows, column : column + query_buf.shape[2]]
        return [pltpu.make_async_copy(block, query_buf.at[t], sems.at[t])]

    begin, _ = stream(count, pieces, [], count)
    begin()
    sums[...] = jnp.zeros(sums.shape, jnp.float32)
    outs[1][:, :done] = near[...]
    for n, w in enumerate((w_key, w_value)):
        part = 0.0
        for k in range(count):
            part = part + jnp.dot(
                lhs[k], w[k * deep : (k + 1) * deep, :], preferred_element_type=jnp.float32
            )
        spread(chosen, part, targets, n * kv_cols)

    @pl.loop(0, count - 1)
    def _(t):
        pieces(t)[0].wait()
        add_products(lhs[t], query_buf.at[t], sums)

    pieces(count - 1)[0].wait()
    spread_products(chosen, lhs[count - 1], query_buf.at[count - 1], sums, targets, 2 * kv_cols)


def attend_kernel(pool, slots, seg, width_d, q_heads, kv_heads, me_ref, *rest):
    terms, rest = rest[: 2 * pool - 1], rest[2 * pool - 1 :]
    cos, sin, marks, keys, values = rest[:5]
    outs, (q_buf,) = rest[5 : 5 + pool], rest[5 + pool :]
    per = pool * slots
    group = q_heads // kv_heads
    step = HD // group
    scale = HD ** (-0.5)

    own, own_rest, near = terms[0], terms[1], terms[-1]
    far_rest, far = terms[2:pool], terms[pool:-1]
    first_cols, cols = own.shape[1], near.shape[1]

    def total(at):
        if at < first_cols:
            got, others = own[:, at : at + HD], far
        else:
            got, others = own_rest[:, at - first_cols : at - first_cols + HD], far_rest
        got = got.astype(jnp.float32) + near[:, at : at + HD].astype(jnp.float32)
        at = at if at < first_cols else at - first_cols
        for part in others:
            got = got + part[:, at : at + HD].astype(jnp.float32)
        return got

    late = first_cols + 2 * kv_heads * HD
    heads = [*range(0, first_cols - HD, HD), *range(late, cols, HD)]
    power = jnp.sum(total(first_cols - HD), axis=1, keepdims=True)
    factor = lax.rsqrt(power * (1.0 / width_d) + EPS)
    cosines, sines = cos[...], sin[...]

    def rounded(x):
        return x.astype(jnp.bfloat16).astype(jnp.float32)

    def rotated(x):
        return rounded(x * cosines + pltpu.roll(x, HD // 2, axis=1) * sines)

    for i in range(q_heads):
        q_buf[i * per : (i + 1) * per, :] = rotated(total(heads[i]) * factor)
    keys_own = [rotated(total(first_cols + g * HD) * factor) for g in range(kv_heads)]
    values_own = [
        rounded(total(first_cols + (kv_heads + g) * HD) * factor) for g in range(kv_heads)
    ]

    me = me_ref[0]

    def base(j):
        return pl.multiple_of(partner(me, j) * (slots * seg), slots * seg)

    lane = lax.broadcasted_iota(jnp.int32, (1, HD), 1)
    slot_of = lane // group
    at = lax.broadcasted_iota(jnp.int32, (seg, HD), 0)
    at_own = lax.broadcasted_iota(jnp.int32, (step, HD), 0)
    blocks = [(g, s) for s in range(0, per, step) for g in range(kv_heads)]
    columns = []
    for g, s in blocks:
        query = jnp.concatenate(
            [q_buf[pl.ds(g * group * per + s + u, group, stride=per), :] for u in range(step)], 0
        )
        columns.append(query.T.astype(jnp.bfloat16))
    scores = []
    for (g, s), query in zip(blocks, columns):
        score = None
        for u in range(0, step, slots):
            wide = jnp.dot(
                keys[pl.ds(base((s + u) // slots), slots * seg), g * HD : (g + 1) * HD],
                query,
                preferred_element_type=jnp.float32,
            )
            for c in range(slots):
                each = wide[c * seg : (c + 1) * seg]
                score = each if score is None else jnp.where(slot_of == u + c, each, score)
        own = jnp.dot(
            keys_own[g][s : s + step].astype(jnp.bfloat16),
            query,
            preferred_element_type=jnp.float32,
        )
        own = jnp.sum(jnp.where(at_own == slot_of, own, 0.0), axis=0, keepdims=True)
        scores.append((score * scale, own * scale))
    turned, levels = [], {}
    for (g, s), (score, own) in zip(blocks, scores):
        length = marks[0:1, s * group : s * group + HD]
        with_own = marks[1:2, s * group : s * group + HD] > 0
        usable = at < length
        own = jnp.where(with_own, own, LOW)
        top = jnp.maximum(jnp.max(jnp.where(usable, score, LOW), axis=0, keepdims=True), own)
        weight = jnp.where(usable, jnp.exp(score - top), 0.0)
        weight_own = jnp.where(with_own, jnp.exp(own - top), 0.0)
        sums = jnp.sum(weight, axis=0, keepdims=True) + weight_own
        sums = jnp.where(length > 0, sums, 1.0)
        level = top + jnp.log(sums)
        for u in range(0, step, slots):
            at_lane = g * slots * group
            moved = level if at_lane == u * group else pltpu.roll(level, (at_lane - u * group) % HD, axis=1)
            there = (lane >= at_lane) & (lane < at_lane + slots * group)
            home = (s + u) // slots
            levels[home] = jnp.where(there, moved, levels.get(home, 0.0))
        rows = [weight_own, 1.0 / sums, jnp.zeros((HD - seg - 2, HD), jnp.float32)]
        turned.append(jnp.concatenate([weight] + rows, 0).T)
    for (g, s), block in zip(blocks, turned):
        for u in range(step):
            home, c = (s + u) // slots, (s + u) % slots
            rows = block[u * group : (u + 1) * group]
            mixed = jnp.dot(
                rows[:, :seg].astype(jnp.bfloat16),
                values[pl.ds(base(home) + c * seg, seg), g * HD : (g + 1) * HD],
                preferred_element_type=jnp.float32,
            )
            mixed = mixed + rows[:, seg : seg + 1] * values_own[g][s + u : s + u + 1]
            to = c * q_heads + g * group
            outs[home][to : to + group, :] = (mixed * rows[:, seg + 1 : seg + 2]).astype(jnp.bfloat16)
    for home, level in levels.items():
        block = jnp.concatenate([*split3(level), jnp.zeros((LEVELS - 3, HD), jnp.float32)], 0)
        outs[home][slots * q_heads :, :] = block.astype(jnp.bfloat16)


def merge_kernel(pool, slots, rows_local, q_heads, kv_heads, slots_ref, rows_ref, own, *rest):
    found, (out, scaled) = [own, rest[pool - 2], *rest[: pool - 2]], rest[pool - 1 :]
    per = pool * slots
    group = q_heads // kv_heads
    block = slots * q_heads
    span = slots * group
    level = jnp.concatenate(
        [jnp.sum(part[block : block + LEVELS, :].astype(jnp.float32), 0, keepdims=True) for part in found], 0
    )
    named = rows_ref[...]
    lane = lax.broadcasted_iota(jnp.int32, (pool, HD), 1)

    def turns(x):
        for c in range(slots):
            y = x
            if c:
                y = jnp.where(
                    lax.rem(lane, span) < span - c * group,
                    pltpu.roll(x, HD - c * group, axis=1),
                    pltpu.roll(x, span - c * group, axis=1),
                )
            for k in range(pool):
                yield jnp.concatenate([y[k:], y[:k]], 0) if k else y

    same = [other == named for other in turns(named)]
    top = level
    for match, other in zip(same, turns(level)):
        top = jnp.maximum(top, jnp.where(match, other, LOW))
    weight = jnp.exp(level - top)
    total = jnp.zeros_like(weight)
    for match, other in zip(same, turns(weight)):
        total = total + jnp.where(match, other, 0.0)
    share = jnp.where(named >= 0, weight / total, 0.0)
    share = jnp.concatenate([share, jnp.zeros((HD - pool, HD), jnp.float32)], 0).T
    for k in range(pool):
        for c in range(slots):
            for g in range(kv_heads):
                at = c * q_heads + g * group
                each = g * span + c * group
                scaled[k * block + at : k * block + at + group, :] = (
                    found[k][at : at + group, :].astype(jnp.float32)
                    * share[each : each + group, k : k + 1]
                )
    row = lax.broadcasted_iota(jnp.int32, (rows_local, 2 * per), 0)
    match = (slots_ref[:, : 2 * per] == row).astype(jnp.float32).astype(jnp.bfloat16)
    for i in range(q_heads):
        part = scaled[pl.ds(i, per, stride=q_heads), :]
        high = part.astype(jnp.bfloat16)
        low = (part - high.astype(jnp.float32)).astype(jnp.bfloat16)
        out[:, i * HD : (i + 1) * HD] = jnp.dot(
            match, jnp.concatenate([high, low], 0), preferred_element_type=jnp.float32
        ).astype(jnp.bfloat16)


def exchange(parts, order):
    got = list(parts)
    for k in order:
        got[k] = lax.ppermute(parts[k], "pool", [(i, i ^ k) for i in range(len(parts))])
    return got


def in_hbm(x):
    return pltpu.with_memory_space_constraint(x, pltpu.HBM)


SMEM = pl.BlockSpec(memory_space=pltpu.SMEM)
VMEM = pl.BlockSpec(memory_space=pltpu.VMEM)
HBM = pl.BlockSpec(memory_space=pltpu.HBM)


def body(
    hidden_in,
    norm_gain,
    w_query,
    w_key,
    w_value,
    cache_keys,
    cache_values,
    send_row,
    piece_len,
    row_len,
):
    pool = lax.axis_size("pool")
    me = lax.axis_index("pool").astype(jnp.int32)
    n_rows, depth = hidden_in.shape
    width_d = depth * pool
    rows_local = n_rows // pool
    slots = send_row.shape[2]
    per = pool * slots
    seg = cache_keys.shape[0] // per
    q_cols, kv_cols = w_query.shape[1], w_key.shape[1]
    q_heads, kv_heads = q_cols // HD, kv_cols // HD
    group = q_heads // kv_heads
    cols = q_cols + 2 * kv_cols + HD

    if pool <= 8:
        indices = [send_row, piece_len, row_len]
    else:
        indices = [send_row.reshape(-1), piece_len.reshape(-1), row_len]
    deep = divides(depth, DEEP)
    count = depth // deep
    widths = [11 * q_cols // 16, 5 * q_cols // 16]


    def parts(width):
        return [jax.ShapeDtypeStruct((per, width), jnp.bfloat16)] * pool

    operands = [in_hbm(x) for x in (*indices, hidden_in, norm_gain, w_query, w_key, w_value)]
    *first_terms, lhs, pick, positions, marks, home_rows, home_slots, key_in, value_in = pl.pallas_call(
        functools.partial(project_kernel, pool, slots, rows_local),
        out_shape=[
            *parts(widths[0] + HD),
            jax.ShapeDtypeStruct((count, n_rows, deep), jnp.bfloat16),
            jax.ShapeDtypeStruct((pool * per, n_rows), jnp.float32),
            jax.ShapeDtypeStruct((per, HD), jnp.float32),
            jax.ShapeDtypeStruct((2, per * group), jnp.int32),
            jax.ShapeDtypeStruct((pool, HD), jnp.int32),
            jax.ShapeDtypeStruct((1, HD), jnp.int32),
            jax.ShapeDtypeStruct(w_key.shape, jnp.bfloat16),
            jax.ShapeDtypeStruct(w_value.shape, jnp.bfloat16),
        ],
        in_specs=[SMEM] + [HBM] * 8,
        out_specs=[VMEM] * (pool + 8),
        scratch_shapes=[
            *(pltpu.SMEM(x.shape, jnp.int32) for x in indices),
            pltpu.VMEM((n_rows, depth), jnp.bfloat16),
            pltpu.VMEM((depth,), jnp.bfloat16),
            pltpu.VMEM((count, deep, widths[0]), jnp.bfloat16),
            pltpu.VMEM((n_rows, widths[0]), jnp.float32),
            pltpu.VMEM((n_rows, HD), jnp.float32),
            pltpu.SemaphoreType.DMA((7,)),
            pltpu.SemaphoreType.DMA((count + 3,)),
        ],
        compiler_params=pltpu.CompilerParams(vmem_limit_bytes=46 * 2**20),
        name="project",
    )(me[None], *operands)
    rest_cols = 2 * kv_cols + widths[1]
    rest_shapes = parts(rest_cols)
    rest_shapes[1] = jax.ShapeDtypeStruct((per, widths[0] + HD + rest_cols), jnp.bfloat16)
    rest_terms = pl.pallas_call(
        functools.partial(project_rest_kernel, pool, widths[0]),
        out_shape=rest_shapes,
        in_specs=[VMEM] * 5 + [HBM],
        out_specs=[VMEM] * pool,
        scratch_shapes=[
            pltpu.VMEM((count, deep, widths[1]), jnp.bfloat16),
            pltpu.VMEM((n_rows, widths[1]), jnp.float32),
            pltpu.SemaphoreType.DMA((count,)),
        ],
        compiler_params=pltpu.CompilerParams(vmem_limit_bytes=40 * 2**20),
        cost_estimate=pl.CostEstimate(
            flops=2 * n_rows * depth * rest_cols,
            bytes_accessed=2 * depth * (rest_cols + n_rows),
            transcendentals=0,
        ),
        name="project_rest",
    )(lhs, pick, first_terms[1], key_in, value_in, operands[5])
    first_terms = exchange(first_terms, range(2, pool))
    rest_terms = list(rest_terms)
    early, late = range(2, pool), range(3, pool)
    got, tied = lax.optimization_barrier(
        ([first_terms[k] for k in early], [rest_terms[k] for k in late])
    )
    for k, part in zip(early, got):
        first_terms[k] = part
    for k, part in zip(late, tied):
        rest_terms[k] = part
    rest_terms = exchange(rest_terms, range(1, pool))
    terms = [first_terms[0], rest_terms[0], *rest_terms[2:], *first_terms[2:], rest_terms[1]]

    half = HD // 2
    freq = THETA ** (-(np.arange(half) * 2.0) / HD)
    angles = positions * np.concatenate([freq, freq]).astype(np.float32)[None, :]
    sign = np.concatenate([-np.ones(half), np.ones(half)]).astype(np.float32)[None, :]
    cosines, sines = jnp.cos(angles), jnp.sin(angles) * sign

    found = pl.pallas_call(
        functools.partial(attend_kernel, pool, slots, seg, width_d, q_heads, kv_heads),
        out_shape=[jax.ShapeDtypeStruct((slots * q_heads + LEVELS, HD), jnp.bfloat16)] * pool,
        in_specs=[SMEM] + [VMEM] * (2 * pool + 4),
        out_specs=[VMEM] * pool,
        scratch_shapes=[pltpu.VMEM((q_heads * per, HD), jnp.float32)],
        compiler_params=pltpu.CompilerParams(vmem_limit_bytes=24 * 2**20),
        name="attend",
    )(me[None], *terms, cosines, sines, marks, cache_keys, cache_values)

    found = exchange(found, [*range(2, pool), 1])

    return pl.pallas_call(
        functools.partial(merge_kernel, pool, slots, rows_local, q_heads, kv_heads),
        out_shape=jax.ShapeDtypeStruct((rows_local, q_cols), jnp.bfloat16),
        in_specs=[VMEM] * (2 + pool),
        out_specs=VMEM,
        scratch_shapes=[
            pltpu.VMEM((per * q_heads, HD), jnp.float32),
        ],
        compiler_params=pltpu.CompilerParams(vmem_limit_bytes=24 * 2**20),
        name="merge",
    )(home_slots, home_rows, found[0], *found[2:], found[1])


def solution(mesh):
    return jax.shard_map(
        body,
        mesh=mesh,
        in_specs=(
            P("groups", "pool"),
            P("pool"),
            P("pool", "tensor"),
            P("pool", "tensor"),
            P("pool", "tensor"),
            P(("groups", "pool"), "tensor"),
            P(("groups", "pool"), "tensor"),
            P("groups", None, None),
            P(("groups", "pool"), None, None),
            P("groups"),
        ),
        out_specs=P(("groups", "pool"), "tensor"),
        check_vma=False,
    )
```

```python
import functools

import jax
import jax.numpy as jnp
import numpy as np
from jax import lax
from jax.experimental import pallas as pl
from jax.experimental.pallas import tpu as pltpu
from jax.sharding import PartitionSpec as P

HD = 128
EPS = 1e-05
THETA = 500000.0
LOW = -1e30
DEEP = 512
LEVELS = 16
TILE = 1536


def divides(width, limit):
    while width % limit:
        limit //= 2
    return limit


def widest(width, limit):
    return max(tile for tile in range(128, limit + 1, 128) if width % tile == 0)


def split3(x):
    a = x.astype(jnp.bfloat16).astype(jnp.float32)
    r = x - a
    b = r.astype(jnp.bfloat16).astype(jnp.float32)
    return a, b, (r - b).astype(jnp.bfloat16).astype(jnp.float32)


def partner(me, k):
    return lax.bitwise_xor(me, k)


def stream(count, pieces, following, ahead):
    def begin():
        for t in range(min(ahead, count)):
            for copy in pieces(t):
                copy.start()
        for copy in following[: max(ahead - count, 0)]:
            copy.start()

    def advance(t):
        @pl.when(t + ahead < count)
        def _():
            for copy in pieces(t + ahead):
                copy.start()

        for j, copy in enumerate(following):
            pl.when(t + ahead == count + j)(copy.start)

    return begin, advance


def add_products(left, block, sums):
    width = block.shape[1]
    tile = widest(width, TILE)
    for at in range(0, width, tile):
        sums[:, at : at + tile] += jnp.dot(
            left, block[:, at : at + tile], preferred_element_type=jnp.float32
        )


def spread(chosen, sums, outs, at):
    width = sums.shape[1]
    per = chosen.shape[0] // len(outs)
    rows = jnp.dot(
        chosen, sums.astype(jnp.bfloat16), preferred_element_type=jnp.float32
    ).astype(jnp.bfloat16)
    for k, out in enumerate(outs):
        out[:, at : at + width] = rows[k * per : (k + 1) * per]


def spread_products(chosen, left, block, sums, outs, to):
    width = block.shape[1]
    tile = widest(width, TILE)
    for at in range(0, width, tile):
        done = sums[:, at : at + tile] + jnp.dot(
            left, block[:, at : at + tile], preferred_element_type=jnp.float32
        )
        spread(chosen, done, outs, to + at)


def project_kernel(pool, slots, rows_local, me_ref, send, lens, row_len, hidden, gain, *rest):
    w_query, w_key, w_value, *rest = rest
    outs, rest = rest[:pool], rest[pool:]
    lhs, pick, positions, marks, home_rows, home_slots, narrow, *rest = rest
    send_buf, lens_buf, row_len_buf, x_buf, g_buf, *rest = rest
    query_buf, sums, squares, in_sem, sems = rest
    per = pool * slots
    n_rows, depth = x_buf.shape
    count, deep, width = query_buf.shape
    me = me_ref[0]

    def named(home, owner, c):
        if len(send_buf.shape) == 3:
            return send_buf[home, owner, c]
        return send_buf[home * per + owner * slots + c]

    lane = lax.broadcasted_iota(jnp.int32, (1, n_rows), 1)
    place = lax.broadcasted_iota(jnp.int32, (1, HD), 1)
    group = marks.shape[1] // per
    slot_of = lax.broadcasted_iota(jnp.int32, (1, marks.shape[1]), 1) // group

    def choose(i):
        owner = partner(me, i // per)
        s = lax.rem(i, per)
        home = partner(owner, s // slots)
        r = named(home, owner, lax.rem(s, slots))
        row = jnp.where(r >= 0, home * rows_local + r, -1)
        pick[pl.ds(i, 1), :] = (lane == row).astype(jnp.float32)

    def describe(s):
        k, c = s // slots, lax.rem(s, slots)
        home = partner(me, k)
        r = named(home, me, c)
        at = row_len_buf[home * rows_local + jnp.maximum(r, 0)].astype(jnp.float32)
        positions[pl.ds(s, 1), :] = jnp.full((1, HD), at, jnp.float32)
        length = lens_buf[0, home, c] if len(lens_buf.shape) == 3 else lens_buf[home * slots + c]
        earlier = jnp.int32(0)
        for e in range(per):
            same = (named(home, e // slots, e % slots) == r) & (e < me * slots + c)
            earlier = earlier | same.astype(jnp.int32)
        first = jnp.where((earlier == 0) & (r >= 0), 1, 0)
        marks[0:1, :] = jnp.where(slot_of == s, length, marks[0:1, :])
        marks[1:2, :] = jnp.where(slot_of == s, first, marks[1:2, :])
        mine = named(me, home, c)
        home_slots[...] = jnp.where(lax.rem(place, per) == s, mine, home_slots[...])
        home_rows[pl.ds(k, 1), :] = jnp.where(
            lax.rem(place // group, slots) == c, mine, home_rows[pl.ds(k, 1), :]
        )

    chore_steps = 4
    spread_chores = count > chore_steps + 1 and pool * per <= 64 and per % chore_steps == 0

    def each(do, total, t):
        share = -(-total // chore_steps)
        if spread_chores:
            for q in range(share):
                do(t * share + q)
        else:
            assert isinstance(t, int)
            pl.loop(0, total)(do)

    def scale(t):
        at = pl.multiple_of(t * deep, deep)
        x = x_buf[:, pl.ds(at, deep)].astype(jnp.float32)
        gains = g_buf[pl.ds(at, deep)].astype(jnp.float32).reshape(1, deep)
        left = (x * gains).astype(jnp.bfloat16)
        lhs[:, pl.ds(at, deep)] = left
        squared = x * x
        total = squares[...]
        for column in range(0, deep, HD):
            total = total + squared[:, column : column + HD]
        squares[...] = total
        return left

    kv_cols = w_key.shape[1]
    cuts = [0, deep // 4, deep // 2, deep] if count > 1 else [0, deep]

    def pieces(t):
        if isinstance(t, int) and t == 0:
            return [
                pltpu.make_async_copy(
                    w_query.at[a:b, :width], query_buf.at[0, a:b], sems.at[0 if n == 0 else count + n]
                )
                for n, (a, b) in enumerate(zip(cuts[:-1], cuts[1:]))
            ]
        rows = pl.ds(pl.multiple_of(t * deep, deep), deep)
        return [pltpu.make_async_copy(w_query.at[rows, :width], query_buf.at[t], sems.at[t])]

    following = [
        pltpu.make_async_copy(w, target, in_sem.at[5 + n])
        for n, (w, target) in enumerate(
            ((w_key, narrow.at[:, :kv_cols]), (w_value, narrow.at[:, kv_cols:]))
        )
    ]
    begin, advance = stream(count, pieces, following, 3)

    def use(t):
        advance(t)
        left = scale(t)
        for copy in pieces(t):
            copy.wait()
        add_products(left, query_buf.at[t], sums)

    def use_early(t):
        use(t)
        each(choose, pool * per, t - 1)
        each(describe, per, t - 1)

    def use_first():
        advance(0)
        left = scale(0)
        for copy, a, b in zip(pieces(0), cuts[:-1], cuts[1:]):
            copy.wait()
            add_products(left[:, a:b], query_buf.at[0, a:b], sums)

    def use_last(t):
        left = scale(t)
        for copy in pieces(t):
            copy.wait()
        chosen = pick[...].astype(jnp.bfloat16)
        spread_products(chosen, left, query_buf.at[t], sums, outs, 0)
        power = jnp.sum(squares[...], axis=1, keepdims=True)
        at = lax.broadcasted_iota(jnp.int32, (n_rows, HD), 1)
        a, b, c = split3(power)
        parts = jnp.where(at == 0, a, jnp.where(at == 1, b, jnp.where(at == 2, c, 0.0)))
        spread(chosen, parts, outs, sums.shape[1])

    inputs = [
        pltpu.make_async_copy(source, target, in_sem.at[i])
        for i, (source, target) in enumerate(
            (
                (gain, g_buf),
                (hidden, x_buf),
                (send, send_buf),
                (lens, lens_buf),
                (row_len, row_len_buf),
            )
        )
    ]
    for one in inputs:
        one.start()
    begin()
    sums[...] = jnp.zeros(sums.shape, jnp.float32)
    squares[...] = jnp.zeros((n_rows, HD), jnp.float32)
    marks[...] = jnp.zeros(marks.shape, jnp.int32)
    home_rows[...] = jnp.full(home_rows.shape, -1, jnp.int32)
    home_slots[...] = jnp.full(home_slots.shape, -1, jnp.int32)
    for one in inputs:
        one.wait()
    if not spread_chores:
        each(choose, pool * per, 0)
        each(describe, per, 0)
    if count > 1:
        use_first()
    early = 1 + chore_steps if spread_chores else 1
    if spread_chores:
        pl.loop(1, early)(use_early)
    if count > early + 1:
        pl.loop(early, count - 1)(use)
    use_last(count - 1)
    for copy in following:
        copy.wait()


def project_rest_kernel(pool, column, lhs, pick, near, narrow, w_query, *rest):
    outs, (query_buf, sums, sems) = rest[:pool], rest[pool:]
    done = near.shape[1]
    count, deep, _ = query_buf.shape
    chosen = pick[...].astype(jnp.bfloat16)
    targets = [out.at[:, done:] if k == 1 else out for k, out in enumerate(outs)]

    def pieces(t):
        rows = pl.ds(pl.multiple_of(t * deep, deep), deep)
        block = w_query.at[rows, column : column + query_buf.shape[2]]
        return [pltpu.make_async_copy(block, query_buf.at[t], sems.at[t])]

    begin, _ = stream(count, pieces, [], count)
    begin()
    sums[...] = jnp.zeros(sums.shape, jnp.float32)
    outs[1][:, :done] = near[...]
    part = jnp.dot(lhs[...], narrow[...], preferred_element_type=jnp.float32)
    spread(chosen, part, targets, 0)

    @pl.loop(0, count - 1)
    def _(t):
        pieces(t)[0].wait()
        add_products(lhs[:, pl.ds(pl.multiple_of(t * deep, deep), deep)], query_buf.at[t], sums)

    pieces(count - 1)[0].wait()
    left = lhs[:, (count - 1) * deep :]
    spread_products(chosen, left, query_buf.at[count - 1], sums, targets, narrow.shape[1])


def attend_kernel(pool, slots, seg, width_d, q_heads, kv_heads, me_ref, *rest):
    terms, rest = rest[: 2 * pool - 1], rest[2 * pool - 1 :]
    cos, sin, marks, keys, values = rest[:5]
    outs, (q_buf,) = rest[5 : 5 + pool], rest[5 + pool :]
    per = pool * slots
    group = q_heads // kv_heads
    step = HD // group
    scale = HD ** (-0.5)

    own, own_rest, near = terms[0], terms[1], terms[-1]
    far_rest, far = terms[2:pool], terms[pool:-1]
    first_cols, cols = own.shape[1], near.shape[1]

    def total(at):
        if at < first_cols:
            got, others = own[:, at : at + HD], far
        else:
            got, others = own_rest[:, at - first_cols : at - first_cols + HD], far_rest
        got = got.astype(jnp.float32) + near[:, at : at + HD].astype(jnp.float32)
        at = at if at < first_cols else at - first_cols
        for part in others:
            got = got + part[:, at : at + HD].astype(jnp.float32)
        return got

    late = first_cols + 2 * kv_heads * HD
    heads = [*range(0, first_cols - HD, HD), *range(late, cols, HD)]
    power = jnp.sum(total(first_cols - HD), axis=1, keepdims=True)
    factor = lax.rsqrt(power * (1.0 / width_d) + EPS)
    cosines, sines = cos[...], sin[...]

    def rounded(x):
        return x.astype(jnp.bfloat16).astype(jnp.float32)

    def rotated(x):
        return rounded(x * cosines + pltpu.roll(x, HD // 2, axis=1) * sines)

    for i in range(q_heads):
        q_buf[i * per : (i + 1) * per, :] = rotated(total(heads[i]) * factor)
    keys_own = [rotated(total(first_cols + g * HD) * factor) for g in range(kv_heads)]
    values_own = [
        rounded(total(first_cols + (kv_heads + g) * HD) * factor) for g in range(kv_heads)
    ]

    me = me_ref[0]

    def base(j):
        return pl.multiple_of(partner(me, j) * (slots * seg), slots * seg)

    lane = lax.broadcasted_iota(jnp.int32, (1, HD), 1)
    slot_of = lane // group
    at = lax.broadcasted_iota(jnp.int32, (seg, HD), 0)
    at_own = lax.broadcasted_iota(jnp.int32, (step, HD), 0)
    blocks = [(g, s) for s in range(0, per, step) for g in range(kv_heads)]
    columns = []
    for g, s in blocks:
        query = jnp.concatenate(
            [q_buf[pl.ds(g * group * per + s + u, group, stride=per), :] for u in range(step)], 0
        )
        columns.append(query.T.astype(jnp.bfloat16))
    scores = []
    for (g, s), query in zip(blocks, columns):
        score = None
        for u in range(0, step, slots):
            wide = jnp.dot(
                keys[pl.ds(base((s + u) // slots), slots * seg), g * HD : (g + 1) * HD],
                query,
                preferred_element_type=jnp.float32,
            )
            for c in range(slots):
                each = wide[c * seg : (c + 1) * seg]
                score = each if score is None else jnp.where(slot_of == u + c, each, score)
        own = jnp.dot(
            keys_own[g][s : s + step].astype(jnp.bfloat16),
            query,
            preferred_element_type=jnp.float32,
        )
        own = jnp.sum(jnp.where(at_own == slot_of, own, 0.0), axis=0, keepdims=True)
        scores.append((score * scale, own * scale))
    turned, levels = [], {}
    for (g, s), (score, own) in zip(blocks, scores):
        length = marks[0:1, s * group : s * group + HD]
        with_own = marks[1:2, s * group : s * group + HD] > 0
        usable = at < length
        own = jnp.where(with_own, own, LOW)
        top = jnp.maximum(jnp.max(jnp.where(usable, score, LOW), axis=0, keepdims=True), own)
        weight = jnp.where(usable, jnp.exp(score - top), 0.0)
        weight_own = jnp.where(with_own, jnp.exp(own - top), 0.0)
        sums = jnp.sum(weight, axis=0, keepdims=True) + weight_own
        sums = jnp.where(length > 0, sums, 1.0)
        level = top + jnp.log(sums)
        for u in range(0, step, slots):
            at_lane = g * slots * group
            moved = level if at_lane == u * group else pltpu.roll(level, (at_lane - u * group) % HD, axis=1)
            there = (lane >= at_lane) & (lane < at_lane + slots * group)
            home = (s + u) // slots
            levels[home] = jnp.where(there, moved, levels.get(home, 0.0))
        rows = [weight_own, 1.0 / sums, jnp.zeros((HD - seg - 2, HD), jnp.float32)]
        turned.append(jnp.concatenate([weight] + rows, 0).T)
    for (g, s), block in zip(blocks, turned):
        for u in range(step):
            home, c = (s + u) // slots, (s + u) % slots
            rows = block[u * group : (u + 1) * group]
            mixed = jnp.dot(
                rows[:, :seg].astype(jnp.bfloat16),
                values[pl.ds(base(home) + c * seg, seg), g * HD : (g + 1) * HD],
                preferred_element_type=jnp.float32,
            )
            mixed = mixed + rows[:, seg : seg + 1] * values_own[g][s + u : s + u + 1]
            to = c * q_heads + g * group
            outs[home][to : to + group, :] = (mixed * rows[:, seg + 1 : seg + 2]).astype(jnp.bfloat16)
    for home, level in levels.items():
        block = jnp.concatenate([*split3(level), jnp.zeros((LEVELS - 3, HD), jnp.float32)], 0)
        outs[home][slots * q_heads :, :] = block.astype(jnp.bfloat16)


def merge_kernel(pool, slots, rows_local, q_heads, kv_heads, slots_ref, rows_ref, own, *rest):
    found, (out, scaled) = [own, rest[pool - 2], *rest[: pool - 2]], rest[pool - 1 :]
    per = pool * slots
    group = q_heads // kv_heads
    block = slots * q_heads
    span = slots * group
    level = jnp.concatenate(
        [jnp.sum(part[block : block + LEVELS, :].astype(jnp.float32), 0, keepdims=True) for part in found], 0
    )
    named = rows_ref[...]
    lane = lax.broadcasted_iota(jnp.int32, (pool, HD), 1)

    def turns(x):
        for c in range(slots):
            y = x
            if c:
                y = jnp.where(
                    lax.rem(lane, span) < span - c * group,
                    pltpu.roll(x, HD - c * group, axis=1),
                    pltpu.roll(x, span - c * group, axis=1),
                )
            for k in range(pool):
                yield jnp.concatenate([y[k:], y[:k]], 0) if k else y

    same = [other == named for other in turns(named)]
    top = level
    for match, other in zip(same, turns(level)):
        top = jnp.maximum(top, jnp.where(match, other, LOW))
    weight = jnp.exp(level - top)
    total = jnp.zeros_like(weight)
    for match, other in zip(same, turns(weight)):
        total = total + jnp.where(match, other, 0.0)
    share = jnp.where(named >= 0, weight / total, 0.0)
    share = jnp.concatenate([share, jnp.zeros((HD - pool, HD), jnp.float32)], 0).T
    for k in range(pool):
        for c in range(slots):
            for g in range(kv_heads):
                at = c * q_heads + g * group
                each = g * span + c * group
                scaled[k * block + at : k * block + at + group, :] = (
                    found[k][at : at + group, :].astype(jnp.float32)
                    * share[each : each + group, k : k + 1]
                )
    row = lax.broadcasted_iota(jnp.int32, (rows_local, 2 * per), 0)
    match = (slots_ref[:, : 2 * per] == row).astype(jnp.float32).astype(jnp.bfloat16)
    for i in range(q_heads):
        part = scaled[pl.ds(i, per, stride=q_heads), :]
        high = part.astype(jnp.bfloat16)
        low = (part - high.astype(jnp.float32)).astype(jnp.bfloat16)
        out[:, i * HD : (i + 1) * HD] = jnp.dot(
            match, jnp.concatenate([high, low], 0), preferred_element_type=jnp.float32
        ).astype(jnp.bfloat16)


def exchange(parts, order):
    got = list(parts)
    for k in order:
        got[k] = lax.ppermute(parts[k], "pool", [(i, i ^ k) for i in range(len(parts))])
    return got


def in_hbm(x):
    return pltpu.with_memory_space_constraint(x, pltpu.HBM)


SMEM = pl.BlockSpec(memory_space=pltpu.SMEM)
VMEM = pl.BlockSpec(memory_space=pltpu.VMEM)
HBM = pl.BlockSpec(memory_space=pltpu.HBM)


def body(
    hidden_in,
    norm_gain,
    w_query,
    w_key,
    w_value,
    cache_keys,
    cache_values,
    send_row,
    piece_len,
    row_len,
):
    pool = lax.axis_size("pool")
    me = lax.axis_index("pool").astype(jnp.int32)
    n_rows, depth = hidden_in.shape
    width_d = depth * pool
    rows_local = n_rows // pool
    slots = send_row.shape[2]
    per = pool * slots
    seg = cache_keys.shape[0] // per
    q_cols, kv_cols = w_query.shape[1], w_key.shape[1]
    q_heads, kv_heads = q_cols // HD, kv_cols // HD
    group = q_heads // kv_heads
    cols = q_cols + 2 * kv_cols + HD

    if pool <= 8:
        indices = [send_row, piece_len, row_len]
    else:
        indices = [send_row.reshape(-1), piece_len.reshape(-1), row_len]
    deep = divides(depth, DEEP)
    count = depth // deep
    widths = [5 * q_cols // 8, 3 * q_cols // 8]


    def parts(width):
        return [jax.ShapeDtypeStruct((per, width), jnp.bfloat16)] * pool

    operands = [in_hbm(x) for x in (*indices, hidden_in, norm_gain, w_query, w_key, w_value)]
    *first_terms, lhs, pick, positions, marks, home_rows, home_slots, narrow = pl.pallas_call(
        functools.partial(project_kernel, pool, slots, rows_local),
        out_shape=[
            *parts(widths[0] + HD),
            jax.ShapeDtypeStruct((n_rows, depth), jnp.bfloat16),
            jax.ShapeDtypeStruct((pool * per, n_rows), jnp.float32),
            jax.ShapeDtypeStruct((per, HD), jnp.float32),
            jax.ShapeDtypeStruct((2, per * group), jnp.int32),
            jax.ShapeDtypeStruct((pool, HD), jnp.int32),
            jax.ShapeDtypeStruct((1, HD), jnp.int32),
            jax.ShapeDtypeStruct((depth, 2 * kv_cols), jnp.bfloat16),
        ],
        in_specs=[SMEM] + [HBM] * 8,
        out_specs=[VMEM] * (pool + 7),
        scratch_shapes=[
            *(pltpu.SMEM(x.shape, jnp.int32) for x in indices),
            pltpu.VMEM((n_rows, depth), jnp.bfloat16),
            pltpu.VMEM((depth,), jnp.bfloat16),
            pltpu.VMEM((count, deep, widths[0]), jnp.bfloat16),
            pltpu.VMEM((n_rows, widths[0]), jnp.float32),
            pltpu.VMEM((n_rows, HD), jnp.float32),
            pltpu.SemaphoreType.DMA((7,)),
            pltpu.SemaphoreType.DMA((count + 3,)),
        ],
        compiler_params=pltpu.CompilerParams(vmem_limit_bytes=46 * 2**20),
        name="project",
    )(me[None], *operands)
    rest_cols = 2 * kv_cols + widths[1]
    rest_shapes = parts(rest_cols)
    rest_shapes[1] = jax.ShapeDtypeStruct((per, widths[0] + HD + rest_cols), jnp.bfloat16)
    rest_terms = pl.pallas_call(
        functools.partial(project_rest_kernel, pool, widths[0]),
        out_shape=rest_shapes,
        in_specs=[VMEM] * 4 + [HBM],
        out_specs=[VMEM] * pool,
        scratch_shapes=[
            pltpu.VMEM((count, deep, widths[1]), jnp.bfloat16),
            pltpu.VMEM((n_rows, widths[1]), jnp.float32),
            pltpu.SemaphoreType.DMA((count,)),
        ],
        compiler_params=pltpu.CompilerParams(vmem_limit_bytes=40 * 2**20),
        cost_estimate=pl.CostEstimate(
            flops=2 * n_rows * depth * rest_cols,
            bytes_accessed=2 * depth * (rest_cols + n_rows),
            transcendentals=0,
        ),
        name="project_rest",
    )(lhs, pick, first_terms[1], narrow, operands[5])
    first_terms = exchange(first_terms, range(2, pool))
    rest_terms = list(rest_terms)
    early, late = range(2, pool), range(3, pool)
    got, tied = lax.optimization_barrier(
        ([first_terms[k] for k in early], [rest_terms[k] for k in late])
    )
    for k, part in zip(early, got):
        first_terms[k] = part
    for k, part in zip(late, tied):
        rest_terms[k] = part
    rest_terms = exchange(rest_terms, range(1, pool))
    terms = [first_terms[0], rest_terms[0], *rest_terms[2:], *first_terms[2:], rest_terms[1]]

    half = HD // 2
    freq = THETA ** (-(np.arange(half) * 2.0) / HD)
    angles = positions * np.concatenate([freq, freq]).astype(np.float32)[None, :]
    sign = np.concatenate([-np.ones(half), np.ones(half)]).astype(np.float32)[None, :]
    cosines, sines = jnp.cos(angles), jnp.sin(angles) * sign

    found = pl.pallas_call(
        functools.partial(attend_kernel, pool, slots, seg, width_d, q_heads, kv_heads),
        out_shape=[jax.ShapeDtypeStruct((slots * q_heads + LEVELS, HD), jnp.bfloat16)] * pool,
        in_specs=[SMEM] + [VMEM] * (2 * pool + 4),
        out_specs=[VMEM] * pool,
        scratch_shapes=[pltpu.VMEM((q_heads * per, HD), jnp.float32)],
        compiler_params=pltpu.CompilerParams(vmem_limit_bytes=24 * 2**20),
        name="attend",
    )(me[None], *terms, cosines, sines, marks, cache_keys, cache_values)

    found = exchange(found, [*range(2, pool), 1])

    return pl.pallas_call(
        functools.partial(merge_kernel, pool, slots, rows_local, q_heads, kv_heads),
        out_shape=jax.ShapeDtypeStruct((rows_local, q_cols), jnp.bfloat16),
        in_specs=[VMEM] * (2 + pool),
        out_specs=VMEM,
        scratch_shapes=[
            pltpu.VMEM((per * q_heads, HD), jnp.float32),
        ],
        compiler_params=pltpu.CompilerParams(vmem_limit_bytes=24 * 2**20),
        name="merge",
    )(home_slots, home_rows, found[0], *found[2:], found[1])


def solution(mesh):
    return jax.shard_map(
        body,
        mesh=mesh,
        in_specs=(
            P("groups", "pool"),
            P("pool"),
            P("pool", "tensor"),
            P("pool", "tensor"),
            P("pool", "tensor"),
            P(("groups", "pool"), "tensor"),
            P(("groups", "pool"), "tensor"),
            P("groups", None, None),
            P(("groups", "pool"), None, None),
            P("groups"),
        ),
        out_specs=P(("groups", "pool"), "tensor"),
        check_vma=False,
    )
```

```python
import functools

import jax
import jax.numpy as jnp
import numpy as np
from jax import lax
from jax.experimental import pallas as pl
from jax.experimental.pallas import tpu as pltpu
from jax.sharding import PartitionSpec as P

HD = 128
EPS = 1e-05
THETA = 500000.0
LOW = -1e30
DEEP = 512
LEVELS = 16
TILE = 1536


def divides(width, limit):
    while width % limit:
        limit //= 2
    return limit


def widest(width, limit):
    return max(tile for tile in range(128, limit + 1, 128) if width % tile == 0)


def split3(x):
    a = x.astype(jnp.bfloat16).astype(jnp.float32)
    r = x - a
    b = r.astype(jnp.bfloat16).astype(jnp.float32)
    return a, b, (r - b).astype(jnp.bfloat16).astype(jnp.float32)


def partner(me, k):
    return lax.bitwise_xor(me, k)


def stream(count, pieces, following, ahead):
    def begin():
        for t in range(min(ahead, count)):
            for copy in pieces(t):
                copy.start()
        for copy in following[: max(ahead - count, 0)]:
            copy.start()

    def advance(t):
        @pl.when(t + ahead < count)
        def _():
            for copy in pieces(t + ahead):
                copy.start()

        for j, copy in enumerate(following):
            pl.when(t + ahead == count + j)(copy.start)

    return begin, advance


def add_products(left, block, sums):
    width = block.shape[1]
    tile = widest(width, TILE)
    for at in range(0, width, tile):
        sums[:, at : at + tile] += jnp.dot(
            left, block[:, at : at + tile], preferred_element_type=jnp.float32
        )


def spread(chosen, sums, outs, at):
    width = sums.shape[1]
    per = chosen.shape[0] // len(outs)
    rows = jnp.dot(
        chosen, sums.astype(jnp.bfloat16), preferred_element_type=jnp.float32
    ).astype(jnp.bfloat16)
    for k, out in enumerate(outs):
        out[:, at : at + width] = rows[k * per : (k + 1) * per]


def spread_products(chosen, left, block, sums, outs, to):
    width = block.shape[1]
    tile = widest(width, TILE)
    for at in range(0, width, tile):
        done = sums[:, at : at + tile] + jnp.dot(
            left, block[:, at : at + tile], preferred_element_type=jnp.float32
        )
        spread(chosen, done, outs, to + at)


def project_kernel(pool, slots, rows_local, me_ref, send, lens, row_len, hidden, gain, *rest):
    w_query, w_key, w_value, *rest = rest
    outs, rest = rest[:pool], rest[pool:]
    lhs, pick, positions, marks, home_rows, home_slots, narrow, *rest = rest
    send_buf, lens_buf, row_len_buf, x_buf, g_buf, *rest = rest
    query_buf, sums, squares, in_sem, sems = rest
    per = pool * slots
    n_rows, depth = x_buf.shape
    count, deep, width = query_buf.shape
    me = me_ref[0]

    def named(home, owner, c):
        if len(send_buf.shape) == 3:
            return send_buf[home, owner, c]
        return send_buf[home * per + owner * slots + c]

    lane = lax.broadcasted_iota(jnp.int32, (1, n_rows), 1)
    place = lax.broadcasted_iota(jnp.int32, (1, HD), 1)
    group = marks.shape[1] // per
    slot_of = lax.broadcasted_iota(jnp.int32, (1, marks.shape[1]), 1) // group

    def choose(i):
        owner = partner(me, i // per)
        s = lax.rem(i, per)
        home = partner(owner, s // slots)
        r = named(home, owner, lax.rem(s, slots))
        row = jnp.where(r >= 0, home * rows_local + r, -1)
        pick[pl.ds(i, 1), :] = (lane == row).astype(jnp.float32)

    def describe(s):
        k, c = s // slots, lax.rem(s, slots)
        home = partner(me, k)
        r = named(home, me, c)
        at = row_len_buf[home * rows_local + jnp.maximum(r, 0)].astype(jnp.float32)
        positions[pl.ds(s, 1), :] = jnp.full((1, HD), at, jnp.float32)
        length = lens_buf[0, home, c] if len(lens_buf.shape) == 3 else lens_buf[home * slots + c]
        earlier = jnp.int32(0)
        for e in range(per):
            same = (named(home, e // slots, e % slots) == r) & (e < me * slots + c)
            earlier = earlier | same.astype(jnp.int32)
        first = jnp.where((earlier == 0) & (r >= 0), 1, 0)
        marks[0:1, :] = jnp.where(slot_of == s, length, marks[0:1, :])
        marks[1:2, :] = jnp.where(slot_of == s, first, marks[1:2, :])
        mine = named(me, home, c)
        home_slots[...] = jnp.where(lax.rem(place, per) == s, mine, home_slots[...])
        home_rows[pl.ds(k, 1), :] = jnp.where(
            lax.rem(place // group, slots) == c, mine, home_rows[pl.ds(k, 1), :]
        )

    chore_steps = 4
    spread_chores = count > chore_steps + 1 and pool * per <= 64 and per % chore_steps == 0

    def each(do, total, t):
        share = -(-total // chore_steps)
        if spread_chores:
            for q in range(share):
                do(t * share + q)
        else:
            assert isinstance(t, int)
            pl.loop(0, total)(do)

    def scale(t):
        at = pl.multiple_of(t * deep, deep)
        x = x_buf[:, pl.ds(at, deep)].astype(jnp.float32)
        gains = g_buf[pl.ds(at, deep)].astype(jnp.float32).reshape(1, deep)
        left = (x * gains).astype(jnp.bfloat16)
        lhs[:, pl.ds(at, deep)] = left
        squared = x * x
        total = squares[...]
        for column in range(0, deep, HD):
            total = total + squared[:, column : column + HD]
        squares[...] = total
        return left

    kv_cols = w_key.shape[1]
    cuts = [0, deep // 4, deep // 2, deep] if count > 1 else [0, deep]

    def pieces(t):
        if isinstance(t, int) and t == 0:
            return [
                pltpu.make_async_copy(
                    w_query.at[a:b, :width], query_buf.at[0, a:b], sems.at[0 if n == 0 else count + n]
                )
                for n, (a, b) in enumerate(zip(cuts[:-1], cuts[1:]))
            ]
        rows = pl.ds(pl.multiple_of(t * deep, deep), deep)
        return [pltpu.make_async_copy(w_query.at[rows, :width], query_buf.at[t], sems.at[t])]

    following = [
        pltpu.make_async_copy(w, target, in_sem.at[5 + n])
        for n, (w, target) in enumerate(
            ((w_key, narrow.at[:, :kv_cols]), (w_value, narrow.at[:, kv_cols:]))
        )
    ]
    begin, advance = stream(count, pieces, following, 3)

    def use(t):
        advance(t)
        left = scale(t)
        for copy in pieces(t):
            copy.wait()
        add_products(left, query_buf.at[t], sums)

    def use_early(t):
        use(t)
        each(choose, pool * per, t - 1)
        each(describe, per, t - 1)

    def use_first():
        advance(0)
        left = scale(0)
        for copy, a, b in zip(pieces(0), cuts[:-1], cuts[1:]):
            copy.wait()
            add_products(left[:, a:b], query_buf.at[0, a:b], sums)

    def use_last(t):
        left = scale(t)
        for copy in pieces(t):
            copy.wait()
        chosen = pick[...].astype(jnp.bfloat16)
        spread_products(chosen, left, query_buf.at[t], sums, outs, 0)
        power = jnp.sum(squares[...], axis=1, keepdims=True)
        at = lax.broadcasted_iota(jnp.int32, (n_rows, HD), 1)
        a, b, c = split3(power)
        parts = jnp.where(at == 0, a, jnp.where(at == 1, b, jnp.where(at == 2, c, 0.0)))
        spread(chosen, parts, outs, sums.shape[1])

    inputs = [
        pltpu.make_async_copy(source, target, in_sem.at[i])
        for i, (source, target) in enumerate(
            (
                (gain, g_buf),
                (hidden, x_buf),
                (send, send_buf),
                (lens, lens_buf),
                (row_len, row_len_buf),
            )
        )
    ]
    for one in inputs:
        one.start()
    begin()
    sums[...] = jnp.zeros(sums.shape, jnp.float32)
    squares[...] = jnp.zeros((n_rows, HD), jnp.float32)
    marks[...] = jnp.zeros(marks.shape, jnp.int32)
    home_rows[...] = jnp.full(home_rows.shape, -1, jnp.int32)
    home_slots[...] = jnp.full(home_slots.shape, -1, jnp.int32)
    for one in inputs:
        one.wait()
    if not spread_chores:
        each(choose, pool * per, 0)
        each(describe, per, 0)
    if count > 1:
        use_first()
    early = 1 + chore_steps if spread_chores else 1
    if spread_chores:
        pl.loop(1, early)(use_early)
    if count > early + 1:
        pl.loop(early, count - 1)(use)
    use_last(count - 1)
    for copy in following:
        copy.wait()


def project_rest_kernel(pool, column, lhs, pick, near, narrow, w_query, *rest):
    outs, (query_buf, sums, sems) = rest[:pool], rest[pool:]
    done = near.shape[1]
    count, deep, _ = query_buf.shape
    chosen = pick[...].astype(jnp.bfloat16)
    targets = [out.at[:, done:] if k == 1 else out for k, out in enumerate(outs)]

    def pieces(t):
        rows = pl.ds(pl.multiple_of(t * deep, deep), deep)
        block = w_query.at[rows, column : column + query_buf.shape[2]]
        return [pltpu.make_async_copy(block, query_buf.at[t], sems.at[t])]

    begin, _ = stream(count, pieces, [], count)
    begin()
    sums[...] = jnp.zeros(sums.shape, jnp.float32)
    outs[1][:, :done] = near[...]
    part = jnp.dot(lhs[...], narrow[...], preferred_element_type=jnp.float32)
    spread(chosen, part, targets, 0)

    @pl.loop(0, count - 1)
    def _(t):
        pieces(t)[0].wait()
        add_products(lhs[:, pl.ds(pl.multiple_of(t * deep, deep), deep)], query_buf.at[t], sums)

    pieces(count - 1)[0].wait()
    left = lhs[:, (count - 1) * deep :]
    spread_products(chosen, left, query_buf.at[count - 1], sums, targets, narrow.shape[1])


def attend_kernel(pool, slots, seg, width_d, q_heads, kv_heads, me_ref, *rest):
    terms, rest = rest[: 2 * pool - 1], rest[2 * pool - 1 :]
    cos, sin, marks, keys, values = rest[:5]
    outs, (q_buf,) = rest[5 : 5 + pool], rest[5 + pool :]
    per = pool * slots
    group = q_heads // kv_heads
    step = HD // group
    scale = HD ** (-0.5)

    own, own_rest, near = terms[0], terms[1], terms[-1]
    far_rest, far = terms[2:pool], terms[pool:-1]
    first_cols, cols = own.shape[1], near.shape[1]

    def total(at):
        if at < first_cols:
            got, others = own[:, at : at + HD], far
        else:
            got, others = own_rest[:, at - first_cols : at - first_cols + HD], far_rest
        got = got.astype(jnp.float32) + near[:, at : at + HD].astype(jnp.float32)
        at = at if at < first_cols else at - first_cols
        for part in others:
            got = got + part[:, at : at + HD].astype(jnp.float32)
        return got

    late = first_cols + 2 * kv_heads * HD
    heads = [*range(0, first_cols - HD, HD), *range(late, cols, HD)]
    power = jnp.sum(total(first_cols - HD), axis=1, keepdims=True)
    factor = lax.rsqrt(power * (1.0 / width_d) + EPS)
    cosines, sines = cos[...], sin[...]

    def rounded(x):
        return x.astype(jnp.bfloat16).astype(jnp.float32)

    def rotated(x):
        return rounded(x * cosines + pltpu.roll(x, HD // 2, axis=1) * sines)

    for i in range(q_heads):
        q_buf[i * per : (i + 1) * per, :] = rotated(total(heads[i]) * factor)
    keys_own = [rotated(total(first_cols + g * HD) * factor) for g in range(kv_heads)]
    values_own = [
        rounded(total(first_cols + (kv_heads + g) * HD) * factor) for g in range(kv_heads)
    ]

    me = me_ref[0]

    def base(j):
        return pl.multiple_of(partner(me, j) * (slots * seg), slots * seg)

    lane = lax.broadcasted_iota(jnp.int32, (1, HD), 1)
    slot_of = lane // group
    at = lax.broadcasted_iota(jnp.int32, (seg, HD), 0)
    at_own = lax.broadcasted_iota(jnp.int32, (step, HD), 0)
    blocks = [(g, s) for s in range(0, per, step) for g in range(kv_heads)]
    columns = []
    for g, s in blocks:
        query = jnp.concatenate(
            [q_buf[pl.ds(g * group * per + s + u, group, stride=per), :] for u in range(step)], 0
        )
        columns.append(query.T.astype(jnp.bfloat16))
    scores = []
    for (g, s), query in zip(blocks, columns):
        score = None
        for u in range(0, step, slots):
            wide = jnp.dot(
                keys[pl.ds(base((s + u) // slots), slots * seg), g * HD : (g + 1) * HD],
                query,
                preferred_element_type=jnp.float32,
            )
            for c in range(slots):
                each = wide[c * seg : (c + 1) * seg]
                score = each if score is None else jnp.where(slot_of == u + c, each, score)
        own = jnp.dot(
            keys_own[g][s : s + step].astype(jnp.bfloat16),
            query,
            preferred_element_type=jnp.float32,
        )
        own = jnp.sum(jnp.where(at_own == slot_of, own, 0.0), axis=0, keepdims=True)
        scores.append((score * scale, own * scale))
    turned, levels = [], {}
    for (g, s), (score, own) in zip(blocks, scores):
        length = marks[0:1, s * group : s * group + HD]
        with_own = marks[1:2, s * group : s * group + HD] > 0
        usable = at < length
        own = jnp.where(with_own, own, LOW)
        top = jnp.maximum(jnp.max(jnp.where(usable, score, LOW), axis=0, keepdims=True), own)
        weight = jnp.where(usable, jnp.exp(score - top), 0.0)
        weight_own = jnp.where(with_own, jnp.exp(own - top), 0.0)
        sums = jnp.sum(weight, axis=0, keepdims=True) + weight_own
        sums = jnp.where(length > 0, sums, 1.0)
        level = top + jnp.log(sums)
        for u in range(0, step, slots):
            at_lane = g * slots * group
            moved = level if at_lane == u * group else pltpu.roll(level, (at_lane - u * group) % HD, axis=1)
            there = (lane >= at_lane) & (lane < at_lane + slots * group)
            home = (s + u) // slots
            levels[home] = jnp.where(there, moved, levels.get(home, 0.0))
        rows = [weight_own, 1.0 / sums, jnp.zeros((HD - seg - 2, HD), jnp.float32)]
        turned.append(jnp.concatenate([weight] + rows, 0).T)
    for (g, s), block in zip(blocks, turned):
        for u in range(step):
            home, c = (s + u) // slots, (s + u) % slots
            rows = block[u * group : (u + 1) * group]
            mixed = jnp.dot(
                rows[:, :seg].astype(jnp.bfloat16),
                values[pl.ds(base(home) + c * seg, seg), g * HD : (g + 1) * HD],
                preferred_element_type=jnp.float32,
            )
            mixed = mixed + rows[:, seg : seg + 1] * values_own[g][s + u : s + u + 1]
            to = c * q_heads + g * group
            outs[home][to : to + group, :] = (mixed * rows[:, seg + 1 : seg + 2]).astype(jnp.bfloat16)
    for home, level in levels.items():
        block = jnp.concatenate([*split3(level), jnp.zeros((LEVELS - 3, HD), jnp.float32)], 0)
        outs[home][slots * q_heads :, :] = block.astype(jnp.bfloat16)


def merge_kernel(pool, slots, rows_local, q_heads, kv_heads, slots_ref, rows_ref, own, *rest):
    found, (out, buf, scaled, sems) = [own, rest[pool - 2], *rest[: pool - 2]], rest[pool - 1 :]
    per = pool * slots
    group = q_heads // kv_heads
    block = slots * q_heads
    span = slots * group
    level = jnp.concatenate(
        [jnp.sum(part[block : block + LEVELS, :].astype(jnp.float32), 0, keepdims=True) for part in found], 0
    )
    named = rows_ref[...]
    lane = lax.broadcasted_iota(jnp.int32, (pool, HD), 1)

    def turns(x):
        for c in range(slots):
            y = x
            if c:
                y = jnp.where(
                    lax.rem(lane, span) < span - c * group,
                    pltpu.roll(x, HD - c * group, axis=1),
                    pltpu.roll(x, span - c * group, axis=1),
                )
            for k in range(pool):
                yield jnp.concatenate([y[k:], y[:k]], 0) if k else y

    same = [other == named for other in turns(named)]
    top = level
    for match, other in zip(same, turns(level)):
        top = jnp.maximum(top, jnp.where(match, other, LOW))
    weight = jnp.exp(level - top)
    total = jnp.zeros_like(weight)
    for match, other in zip(same, turns(weight)):
        total = total + jnp.where(match, other, 0.0)
    share = jnp.where(named >= 0, weight / total, 0.0)
    share = jnp.concatenate([share, jnp.zeros((HD - pool, HD), jnp.float32)], 0).T
    for k in range(pool):
        for c in range(slots):
            for g in range(kv_heads):
                at = c * q_heads + g * group
                each = g * span + c * group
                scaled[k * block + at : k * block + at + group, :] = (
                    found[k][at : at + group, :].astype(jnp.float32)
                    * share[each : each + group, k : k + 1]
                )
    row = lax.broadcasted_iota(jnp.int32, (rows_local, 2 * per), 0)
    match = (slots_ref[:, : 2 * per] == row).astype(jnp.float32).astype(jnp.bfloat16)
    quarter = q_heads // 4
    copies = [
        pltpu.make_async_copy(buf.at[:, columns], out.at[:, columns], sems.at[n])
        for n, columns in enumerate(pl.ds(n * quarter * HD, quarter * HD) for n in range(4))
    ]
    for i in range(q_heads):
        part = scaled[pl.ds(i, per, stride=q_heads), :]
        high = part.astype(jnp.bfloat16)
        low = (part - high.astype(jnp.float32)).astype(jnp.bfloat16)
        buf[:, i * HD : (i + 1) * HD] = jnp.dot(
            match, jnp.concatenate([high, low], 0), preferred_element_type=jnp.float32
        ).astype(jnp.bfloat16)
        if (i + 1) % quarter == 0:
            copies[i // quarter].start()
    for copy in copies:
        copy.wait()


def exchange(parts, order):
    got = list(parts)
    for k in order:
        got[k] = lax.ppermute(parts[k], "pool", [(i, i ^ k) for i in range(len(parts))])
    return got


def in_hbm(x):
    return pltpu.with_memory_space_constraint(x, pltpu.HBM)


SMEM = pl.BlockSpec(memory_space=pltpu.SMEM)
VMEM = pl.BlockSpec(memory_space=pltpu.VMEM)
HBM = pl.BlockSpec(memory_space=pltpu.HBM)


def body(
    hidden_in,
    norm_gain,
    w_query,
    w_key,
    w_value,
    cache_keys,
    cache_values,
    send_row,
    piece_len,
    row_len,
):
    pool = lax.axis_size("pool")
    me = lax.axis_index("pool").astype(jnp.int32)
    n_rows, depth = hidden_in.shape
    width_d = depth * pool
    rows_local = n_rows // pool
    slots = send_row.shape[2]
    per = pool * slots
    seg = cache_keys.shape[0] // per
    q_cols, kv_cols = w_query.shape[1], w_key.shape[1]
    q_heads, kv_heads = q_cols // HD, kv_cols // HD
    group = q_heads // kv_heads
    cols = q_cols + 2 * kv_cols + HD

    if pool <= 8:
        indices = [send_row, piece_len, row_len]
    else:
        indices = [send_row.reshape(-1), piece_len.reshape(-1), row_len]
    deep = divides(depth, DEEP)
    count = depth // deep
    widths = [11 * q_cols // 16, 5 * q_cols // 16]


    def parts(width):
        return [jax.ShapeDtypeStruct((per, width), jnp.bfloat16)] * pool

    operands = [in_hbm(x) for x in (*indices, hidden_in, norm_gain, w_query, w_key, w_value)]
    *first_terms, lhs, pick, positions, marks, home_rows, home_slots, narrow = pl.pallas_call(
        functools.partial(project_kernel, pool, slots, rows_local),
        out_shape=[
            *parts(widths[0] + HD),
            jax.ShapeDtypeStruct((n_rows, depth), jnp.bfloat16),
            jax.ShapeDtypeStruct((pool * per, n_rows), jnp.float32),
            jax.ShapeDtypeStruct((per, HD), jnp.float32),
            jax.ShapeDtypeStruct((2, per * group), jnp.int32),
            jax.ShapeDtypeStruct((pool, HD), jnp.int32),
            jax.ShapeDtypeStruct((1, HD), jnp.int32),
            jax.ShapeDtypeStruct((depth, 2 * kv_cols), jnp.bfloat16),
        ],
        in_specs=[SMEM] + [HBM] * 8,
        out_specs=[VMEM] * (pool + 7),
        scratch_shapes=[
            *(pltpu.SMEM(x.shape, jnp.int32) for x in indices),
            pltpu.VMEM((n_rows, depth), jnp.bfloat16),
            pltpu.VMEM((depth,), jnp.bfloat16),
            pltpu.VMEM((count, deep, widths[0]), jnp.bfloat16),
            pltpu.VMEM((n_rows, widths[0]), jnp.float32),
            pltpu.VMEM((n_rows, HD), jnp.float32),
            pltpu.SemaphoreType.DMA((7,)),
            pltpu.SemaphoreType.DMA((count + 3,)),
        ],
        compiler_params=pltpu.CompilerParams(vmem_limit_bytes=46 * 2**20),
        name="project",
    )(me[None], *operands)
    rest_cols = 2 * kv_cols + widths[1]
    rest_shapes = parts(rest_cols)
    rest_shapes[1] = jax.ShapeDtypeStruct((per, widths[0] + HD + rest_cols), jnp.bfloat16)
    rest_terms = pl.pallas_call(
        functools.partial(project_rest_kernel, pool, widths[0]),
        out_shape=rest_shapes,
        in_specs=[VMEM] * 4 + [HBM],
        out_specs=[VMEM] * pool,
        scratch_shapes=[
            pltpu.VMEM((count, deep, widths[1]), jnp.bfloat16),
            pltpu.VMEM((n_rows, widths[1]), jnp.float32),
            pltpu.SemaphoreType.DMA((count,)),
        ],
        compiler_params=pltpu.CompilerParams(vmem_limit_bytes=40 * 2**20),
        cost_estimate=pl.CostEstimate(
            flops=2 * n_rows * depth * rest_cols,
            bytes_accessed=2 * depth * (rest_cols + n_rows),
            transcendentals=0,
        ),
        name="project_rest",
    )(lhs, pick, first_terms[1], narrow, operands[5])
    first_terms = exchange(first_terms, range(2, pool))
    rest_terms = list(rest_terms)
    early, late = range(2, pool), range(3, pool)
    got, tied = lax.optimization_barrier(
        ([first_terms[k] for k in early], [rest_terms[k] for k in late])
    )
    for k, part in zip(early, got):
        first_terms[k] = part
    for k, part in zip(late, tied):
        rest_terms[k] = part
    rest_terms = exchange(rest_terms, range(1, pool))
    terms = [first_terms[0], rest_terms[0], *rest_terms[2:], *first_terms[2:], rest_terms[1]]

    half = HD // 2
    freq = THETA ** (-(np.arange(half) * 2.0) / HD)
    angles = positions * np.concatenate([freq, freq]).astype(np.float32)[None, :]
    sign = np.concatenate([-np.ones(half), np.ones(half)]).astype(np.float32)[None, :]
    cosines, sines = jnp.cos(angles), jnp.sin(angles) * sign

    found = pl.pallas_call(
        functools.partial(attend_kernel, pool, slots, seg, width_d, q_heads, kv_heads),
        out_shape=[jax.ShapeDtypeStruct((slots * q_heads + LEVELS, HD), jnp.bfloat16)] * pool,
        in_specs=[SMEM] + [VMEM] * (2 * pool + 4),
        out_specs=[VMEM] * pool,
        scratch_shapes=[pltpu.VMEM((q_heads * per, HD), jnp.float32)],
        compiler_params=pltpu.CompilerParams(vmem_limit_bytes=24 * 2**20),
        name="attend",
    )(me[None], *terms, cosines, sines, marks, cache_keys, cache_values)

    found = exchange(found, [*range(2, pool), 1])

    return pl.pallas_call(
        functools.partial(merge_kernel, pool, slots, rows_local, q_heads, kv_heads),
        out_shape=jax.ShapeDtypeStruct((rows_local, q_cols), jnp.bfloat16),
        in_specs=[VMEM] * (2 + pool),
        out_specs=HBM,
        scratch_shapes=[
            pltpu.VMEM((rows_local, q_cols), jnp.bfloat16),
            pltpu.VMEM((per * q_heads, HD), jnp.float32),
            pltpu.SemaphoreType.DMA((4,)),
        ],
        compiler_params=pltpu.CompilerParams(vmem_limit_bytes=24 * 2**20),
        name="merge",
    )(home_slots, home_rows, found[0], *found[2:], found[1])


def solution(mesh):
    return jax.shard_map(
        body,
        mesh=mesh,
        in_specs=(
            P("groups", "pool"),
            P("pool"),
            P("pool", "tensor"),
            P("pool", "tensor"),
            P("pool", "tensor"),
            P(("groups", "pool"), "tensor"),
            P(("groups", "pool"), "tensor"),
            P("groups", None, None),
            P(("groups", "pool"), None, None),
            P("groups"),
        ),
        out_specs=P(("groups", "pool"), "tensor"),
        check_vma=False,
    )
```

```python
import functools

import jax
import jax.numpy as jnp
import numpy as np
from jax import lax
from jax.experimental import pallas as pl
from jax.experimental.pallas import tpu as pltpu
from jax.sharding import PartitionSpec as P

HD = 128
EPS = 1e-05
THETA = 500000.0
LOW = -1e30
DEEP = 512
LEVELS = 16
TILE = 1536


def divides(width, limit):
    while width % limit:
        limit //= 2
    return limit


def widest(width, limit):
    return max(tile for tile in range(128, limit + 1, 128) if width % tile == 0)


def split3(x):
    a = x.astype(jnp.bfloat16).astype(jnp.float32)
    r = x - a
    b = r.astype(jnp.bfloat16).astype(jnp.float32)
    return a, b, (r - b).astype(jnp.bfloat16).astype(jnp.float32)


def partner(me, k):
    return lax.bitwise_xor(me, k)


def stream(count, pieces, ahead):
    def begin():
        for t in range(min(ahead, count)):
            for copy in pieces(t):
                copy.start()

    def advance(t):
        @pl.when(t + ahead < count)
        def _():
            for copy in pieces(t + ahead):
                copy.start()

    return begin, advance


def add_products(left, block, sums):
    width = block.shape[1]
    tile = widest(width, TILE)
    for at in range(0, width, tile):
        sums[:, at : at + tile] += jnp.dot(
            left, block[:, at : at + tile], preferred_element_type=jnp.float32
        )


def spread(chosen, sums, outs, at):
    width = sums.shape[1]
    per = chosen.shape[0] // len(outs)
    rows = jnp.dot(
        chosen, sums.astype(jnp.bfloat16), preferred_element_type=jnp.float32
    ).astype(jnp.bfloat16)
    for k, out in enumerate(outs):
        out[:, at : at + width] = rows[k * per : (k + 1) * per]


def spread_products(chosen, left, block, sums, outs, to):
    width = block.shape[1]
    tile = widest(width, TILE)
    for at in range(0, width, tile):
        done = sums[:, at : at + tile] + jnp.dot(
            left, block[:, at : at + tile], preferred_element_type=jnp.float32
        )
        spread(chosen, done, outs, to + at)


def project_kernel(pool, slots, rows_local, me_ref, send, lens, row_len, hidden, gain, *rest):
    w_query, *rest = rest
    outs, rest = rest[:pool], rest[pool:]
    lhs, pick, positions, marks, home_rows, home_slots, *rest = rest
    send_buf, lens_buf, row_len_buf, x_buf, g_buf, *rest = rest
    query_buf, sums, squares, in_sem, sems = rest
    per = pool * slots
    n_rows, depth = x_buf.shape
    count, deep, width = query_buf.shape
    me = me_ref[0]

    def named(home, owner, c):
        if len(send_buf.shape) == 3:
            return send_buf[home, owner, c]
        return send_buf[home * per + owner * slots + c]

    lane = lax.broadcasted_iota(jnp.int32, (1, n_rows), 1)
    place = lax.broadcasted_iota(jnp.int32, (1, HD), 1)
    group = marks.shape[1] // per
    slot_of = lax.broadcasted_iota(jnp.int32, (1, marks.shape[1]), 1) // group

    def choose(i):
        owner = partner(me, i // per)
        s = lax.rem(i, per)
        home = partner(owner, s // slots)
        r = named(home, owner, lax.rem(s, slots))
        row = jnp.where(r >= 0, home * rows_local + r, -1)
        pick[pl.ds(i, 1), :] = (lane == row).astype(jnp.float32)

    def describe(s):
        k, c = s // slots, lax.rem(s, slots)
        home = partner(me, k)
        r = named(home, me, c)
        at = row_len_buf[home * rows_local + jnp.maximum(r, 0)].astype(jnp.float32)
        positions[pl.ds(s, 1), :] = jnp.full((1, HD), at, jnp.float32)
        length = lens_buf[0, home, c] if len(lens_buf.shape) == 3 else lens_buf[home * slots + c]
        earlier = jnp.int32(0)
        for e in range(per):
            same = (named(home, e // slots, e % slots) == r) & (e < me * slots + c)
            earlier = earlier | same.astype(jnp.int32)
        first = jnp.where((earlier == 0) & (r >= 0), 1, 0)
        marks[0:1, :] = jnp.where(slot_of == s, length, marks[0:1, :])
        marks[1:2, :] = jnp.where(slot_of == s, first, marks[1:2, :])
        mine = named(me, home, c)
        home_slots[...] = jnp.where(lax.rem(place, per) == s, mine, home_slots[...])
        home_rows[pl.ds(k, 1), :] = jnp.where(
            lax.rem(place // group, slots) == c, mine, home_rows[pl.ds(k, 1), :]
        )

    chore_steps = 4
    spread_chores = count > chore_steps + 1 and pool * per <= 64 and per % chore_steps == 0

    def each(do, total, t):
        share = -(-total // chore_steps)
        if spread_chores:
            for q in range(share):
                do(t * share + q)
        else:
            assert isinstance(t, int)
            pl.loop(0, total)(do)

    def scale(t):
        at = pl.multiple_of(t * deep, deep)
        x = x_buf[:, pl.ds(at, deep)].astype(jnp.float32)
        gains = g_buf[pl.ds(at, deep)].astype(jnp.float32).reshape(1, deep)
        left = (x * gains).astype(jnp.bfloat16)
        lhs[:, pl.ds(at, deep)] = left
        squared = x * x
        total = squares[...]
        for column in range(0, deep, HD):
            total = total + squared[:, column : column + HD]
        squares[...] = total
        return left

    cuts = [0, deep // 4, deep // 2, deep] if count > 1 else [0, deep]

    def pieces(t):
        if isinstance(t, int) and t == 0:
            return [
                pltpu.make_async_copy(
                    w_query.at[a:b, :width], query_buf.at[0, a:b], sems.at[0 if n == 0 else count + n]
                )
                for n, (a, b) in enumerate(zip(cuts[:-1], cuts[1:]))
            ]
        rows = pl.ds(pl.multiple_of(t * deep, deep), deep)
        return [pltpu.make_async_copy(w_query.at[rows, :width], query_buf.at[t], sems.at[t])]

    begin, advance = stream(count, pieces, 3)

    def use(t):
        advance(t)
        left = scale(t)
        for copy in pieces(t):
            copy.wait()
        add_products(left, query_buf.at[t], sums)

    def use_early(t):
        use(t)
        each(choose, pool * per, t - 1)
        each(describe, per, t - 1)

    def use_first():
        advance(0)
        left = scale(0)
        for copy, a, b in zip(pieces(0), cuts[:-1], cuts[1:]):
            copy.wait()
            add_products(left[:, a:b], query_buf.at[0, a:b], sums)

    def use_last(t):
        left = scale(t)
        for copy in pieces(t):
            copy.wait()
        chosen = pick[...].astype(jnp.bfloat16)
        spread_products(chosen, left, query_buf.at[t], sums, outs, 0)
        power = jnp.sum(squares[...], axis=1, keepdims=True)
        at = lax.broadcasted_iota(jnp.int32, (n_rows, HD), 1)
        a, b, c = split3(power)
        parts = jnp.where(at == 0, a, jnp.where(at == 1, b, jnp.where(at == 2, c, 0.0)))
        spread(chosen, parts, outs, sums.shape[1])

    inputs = [
        pltpu.make_async_copy(source, target, in_sem.at[i])
        for i, (source, target) in enumerate(
            (
                (gain, g_buf),
                (hidden, x_buf),
                (send, send_buf),
                (lens, lens_buf),
                (row_len, row_len_buf),
            )
        )
    ]
    for one in inputs:
        one.start()
    begin()
    sums[...] = jnp.zeros(sums.shape, jnp.float32)
    squares[...] = jnp.zeros((n_rows, HD), jnp.float32)
    marks[...] = jnp.zeros(marks.shape, jnp.int32)
    home_rows[...] = jnp.full(home_rows.shape, -1, jnp.int32)
    home_slots[...] = jnp.full(home_slots.shape, -1, jnp.int32)
    for one in inputs:
        one.wait()
    if not spread_chores:
        each(choose, pool * per, 0)
        each(describe, per, 0)
    if count > 1:
        use_first()
    early = 1 + chore_steps if spread_chores else 1
    if spread_chores:
        pl.loop(1, early)(use_early)
    if count > early + 1:
        pl.loop(early, count - 1)(use)
    use_last(count - 1)


def project_rest_kernel(pool, column, lhs, pick, near, w_key, w_value, w_query, *rest):
    outs, (block_buf, sums, sems) = rest[:pool], rest[pool:]
    done = near.shape[1]
    count, deep, width = block_buf.shape
    kv_cols = w_key.shape[1]
    spans = [(w_key, 0, 0, kv_cols), (w_value, 0, kv_cols, kv_cols)]
    spans.append((w_query, column, 2 * kv_cols, width - 2 * kv_cols))

    def pieces(t):
        rows = pl.ds(pl.multiple_of(t * deep, deep), deep)
        return [
            pltpu.make_async_copy(
                w.at[rows, start : start + size], block_buf.at[t, :, to : to + size], sems.at[n, t]
            )
            for n, (w, start, to, size) in enumerate(spans)
        ]

    begin, _ = stream(count, pieces, count)
    begin()
    sums[...] = jnp.zeros(sums.shape, jnp.float32)
    outs[1][:, :done] = near[...]
    chosen = pick[...].astype(jnp.bfloat16)
    targets = [out.at[:, done:] if k == 1 else out for k, out in enumerate(outs)]

    @pl.loop(0, count - 1)
    def _(t):
        for copy in pieces(t):
            copy.wait()
        left = lhs[:, pl.ds(pl.multiple_of(t * deep, deep), deep)]
        add_products(left, block_buf.at[t], sums)

    for copy in pieces(count - 1):
        copy.wait()
    left = lhs[:, (count - 1) * deep :]
    spread_products(chosen, left, block_buf.at[count - 1], sums, targets, 0)


def attend_kernel(pool, slots, seg, width_d, q_heads, kv_heads, me_ref, *rest):
    terms, rest = rest[: 2 * pool - 1], rest[2 * pool - 1 :]
    cos, sin, marks, keys, values = rest[:5]
    outs, (q_buf,) = rest[5 : 5 + pool], rest[5 + pool :]
    per = pool * slots
    group = q_heads // kv_heads
    step = HD // group
    scale = HD ** (-0.5)

    own, own_rest, near = terms[0], terms[1], terms[-1]
    far_rest, far = terms[2:pool], terms[pool:-1]
    first_cols, cols = own.shape[1], near.shape[1]

    def total(at):
        if at < first_cols:
            got, others = own[:, at : at + HD], far
        else:
            got, others = own_rest[:, at - first_cols : at - first_cols + HD], far_rest
        got = got.astype(jnp.float32) + near[:, at : at + HD].astype(jnp.float32)
        at = at if at < first_cols else at - first_cols
        for part in others:
            got = got + part[:, at : at + HD].astype(jnp.float32)
        return got

    late = first_cols + 2 * kv_heads * HD
    heads = [*range(0, first_cols - HD, HD), *range(late, cols, HD)]
    power = jnp.sum(total(first_cols - HD), axis=1, keepdims=True)
    factor = lax.rsqrt(power * (1.0 / width_d) + EPS)
    cosines, sines = cos[...], sin[...]

    def rounded(x):
        return x.astype(jnp.bfloat16).astype(jnp.float32)

    def rotated(x):
        return rounded(x * cosines + pltpu.roll(x, HD // 2, axis=1) * sines)

    for i in range(q_heads):
        q_buf[i * per : (i + 1) * per, :] = rotated(total(heads[i]) * factor)
    keys_own = [rotated(total(first_cols + g * HD) * factor) for g in range(kv_heads)]
    values_own = [
        rounded(total(first_cols + (kv_heads + g) * HD) * factor) for g in range(kv_heads)
    ]

    me = me_ref[0]

    def base(j):
        return pl.multiple_of(partner(me, j) * (slots * seg), slots * seg)

    lane = lax.broadcasted_iota(jnp.int32, (1, HD), 1)
    slot_of = lane // group
    at = lax.broadcasted_iota(jnp.int32, (seg, HD), 0)
    at_own = lax.broadcasted_iota(jnp.int32, (step, HD), 0)
    blocks = [(g, s) for s in range(0, per, step) for g in range(kv_heads)]
    columns = []
    for g, s in blocks:
        query = jnp.concatenate(
            [q_buf[pl.ds(g * group * per + s + u, group, stride=per), :] for u in range(step)], 0
        )
        columns.append(query.T.astype(jnp.bfloat16))
    scores = []
    for (g, s), query in zip(blocks, columns):
        score = None
        for u in range(0, step, slots):
            wide = jnp.dot(
                keys[pl.ds(base((s + u) // slots), slots * seg), g * HD : (g + 1) * HD],
                query,
                preferred_element_type=jnp.float32,
            )
            for c in range(slots):
                each = wide[c * seg : (c + 1) * seg]
                score = each if score is None else jnp.where(slot_of == u + c, each, score)
        own = jnp.dot(
            keys_own[g][s : s + step].astype(jnp.bfloat16),
            query,
            preferred_element_type=jnp.float32,
        )
        own = jnp.sum(jnp.where(at_own == slot_of, own, 0.0), axis=0, keepdims=True)
        scores.append((score * scale, own * scale))
    turned, levels = [], {}
    for (g, s), (score, own) in zip(blocks, scores):
        length = marks[0:1, s * group : s * group + HD]
        with_own = marks[1:2, s * group : s * group + HD] > 0
        usable = at < length
        own = jnp.where(with_own, own, LOW)
        top = jnp.maximum(jnp.max(jnp.where(usable, score, LOW), axis=0, keepdims=True), own)
        weight = jnp.where(usable, jnp.exp(score - top), 0.0)
        weight_own = jnp.where(with_own, jnp.exp(own - top), 0.0)
        sums = jnp.sum(weight, axis=0, keepdims=True) + weight_own
        sums = jnp.where(length > 0, sums, 1.0)
        level = top + jnp.log(sums)
        for u in range(0, step, slots):
            at_lane = g * slots * group
            moved = level if at_lane == u * group else pltpu.roll(level, (at_lane - u * group) % HD, axis=1)
            there = (lane >= at_lane) & (lane < at_lane + slots * group)
            home = (s + u) // slots
            levels[home] = jnp.where(there, moved, levels.get(home, 0.0))
        rows = [weight_own, 1.0 / sums, jnp.zeros((HD - seg - 2, HD), jnp.float32)]
        turned.append(jnp.concatenate([weight] + rows, 0).T)
    for (g, s), block in zip(blocks, turned):
        for u in range(step):
            home, c = (s + u) // slots, (s + u) % slots
            rows = block[u * group : (u + 1) * group]
            mixed = jnp.dot(
                rows[:, :seg].astype(jnp.bfloat16),
                values[pl.ds(base(home) + c * seg, seg), g * HD : (g + 1) * HD],
                preferred_element_type=jnp.float32,
            )
            mixed = mixed + rows[:, seg : seg + 1] * values_own[g][s + u : s + u + 1]
            to = c * q_heads + g * group
            outs[home][to : to + group, :] = (mixed * rows[:, seg + 1 : seg + 2]).astype(jnp.bfloat16)
    for home, level in levels.items():
        block = jnp.concatenate([*split3(level), jnp.zeros((LEVELS - 3, HD), jnp.float32)], 0)
        outs[home][slots * q_heads :, :] = block.astype(jnp.bfloat16)


def merge_kernel(pool, slots, rows_local, q_heads, kv_heads, slots_ref, rows_ref, own, *rest):
    found, (out, buf, scaled, sems) = [own, rest[pool - 2], *rest[: pool - 2]], rest[pool - 1 :]
    per = pool * slots
    group = q_heads // kv_heads
    block = slots * q_heads
    span = slots * group
    level = jnp.concatenate(
        [jnp.sum(part[block : block + LEVELS, :].astype(jnp.float32), 0, keepdims=True) for part in found], 0
    )
    named = rows_ref[...]
    lane = lax.broadcasted_iota(jnp.int32, (pool, HD), 1)

    def turns(x):
        for c in range(slots):
            y = x
            if c:
                y = jnp.where(
                    lax.rem(lane, span) < span - c * group,
                    pltpu.roll(x, HD - c * group, axis=1),
                    pltpu.roll(x, span - c * group, axis=1),
                )
            for k in range(pool):
                yield jnp.concatenate([y[k:], y[:k]], 0) if k else y

    same = [other == named for other in turns(named)]
    top = level
    for match, other in zip(same, turns(level)):
        top = jnp.maximum(top, jnp.where(match, other, LOW))
    weight = jnp.exp(level - top)
    total = jnp.zeros_like(weight)
    for match, other in zip(same, turns(weight)):
        total = total + jnp.where(match, other, 0.0)
    share = jnp.where(named >= 0, weight / total, 0.0)
    share = jnp.concatenate([share, jnp.zeros((HD - pool, HD), jnp.float32)], 0).T
    for k in range(pool):
        for c in range(slots):
            for g in range(kv_heads):
                at = c * q_heads + g * group
                each = g * span + c * group
                scaled[k * block + at : k * block + at + group, :] = (
                    found[k][at : at + group, :].astype(jnp.float32)
                    * share[each : each + group, k : k + 1]
                )
    row = lax.broadcasted_iota(jnp.int32, (rows_local, 2 * per), 0)
    match = (slots_ref[:, : 2 * per] == row).astype(jnp.float32).astype(jnp.bfloat16)
    quarter = q_heads // 4
    copies = [
        pltpu.make_async_copy(buf.at[:, columns], out.at[:, columns], sems.at[n])
        for n, columns in enumerate(pl.ds(n * quarter * HD, quarter * HD) for n in range(4))
    ]
    for i in range(q_heads):
        part = scaled[pl.ds(i, per, stride=q_heads), :]
        high = part.astype(jnp.bfloat16)
        low = (part - high.astype(jnp.float32)).astype(jnp.bfloat16)
        buf[:, i * HD : (i + 1) * HD] = jnp.dot(
            match, jnp.concatenate([high, low], 0), preferred_element_type=jnp.float32
        ).astype(jnp.bfloat16)
        if (i + 1) % quarter == 0:
            copies[i // quarter].start()
    for copy in copies:
        copy.wait()


def exchange(parts, order):
    got = list(parts)
    for k in order:
        got[k] = lax.ppermute(parts[k], "pool", [(i, i ^ k) for i in range(len(parts))])
    return got


def in_hbm(x):
    return pltpu.with_memory_space_constraint(x, pltpu.HBM)


SMEM = pl.BlockSpec(memory_space=pltpu.SMEM)
VMEM = pl.BlockSpec(memory_space=pltpu.VMEM)
HBM = pl.BlockSpec(memory_space=pltpu.HBM)


def body(
    hidden_in,
    norm_gain,
    w_query,
    w_key,
    w_value,
    cache_keys,
    cache_values,
    send_row,
    piece_len,
    row_len,
):
    pool = lax.axis_size("pool")
    me = lax.axis_index("pool").astype(jnp.int32)
    n_rows, depth = hidden_in.shape
    width_d = depth * pool
    rows_local = n_rows // pool
    slots = send_row.shape[2]
    per = pool * slots
    seg = cache_keys.shape[0] // per
    q_cols, kv_cols = w_query.shape[1], w_key.shape[1]
    q_heads, kv_heads = q_cols // HD, kv_cols // HD
    group = q_heads // kv_heads
    cols = q_cols + 2 * kv_cols + HD

    if pool <= 8:
        indices = [send_row, piece_len, row_len]
    else:
        indices = [send_row.reshape(-1), piece_len.reshape(-1), row_len]
    deep = divides(depth, DEEP)
    count = depth // deep
    widths = [11 * q_cols // 16, 5 * q_cols // 16]


    def parts(width):
        return [jax.ShapeDtypeStruct((per, width), jnp.bfloat16)] * pool

    operands = [in_hbm(x) for x in (*indices, hidden_in, norm_gain, w_query, w_key, w_value)]
    *first_terms, lhs, pick, positions, marks, home_rows, home_slots = pl.pallas_call(
        functools.partial(project_kernel, pool, slots, rows_local),
        out_shape=[
            *parts(widths[0] + HD),
            jax.ShapeDtypeStruct((n_rows, depth), jnp.bfloat16),
            jax.ShapeDtypeStruct((pool * per, n_rows), jnp.float32),
            jax.ShapeDtypeStruct((per, HD), jnp.float32),
            jax.ShapeDtypeStruct((2, per * group), jnp.int32),
            jax.ShapeDtypeStruct((pool, HD), jnp.int32),
            jax.ShapeDtypeStruct((1, HD), jnp.int32),
        ],
        in_specs=[SMEM] + [HBM] * 6,
        out_specs=[VMEM] * (pool + 6),
        scratch_shapes=[
            *(pltpu.SMEM(x.shape, jnp.int32) for x in indices),
            pltpu.VMEM((n_rows, depth), jnp.bfloat16),
            pltpu.VMEM((depth,), jnp.bfloat16),
            pltpu.VMEM((count, deep, widths[0]), jnp.bfloat16),
            pltpu.VMEM((n_rows, widths[0]), jnp.float32),
            pltpu.VMEM((n_rows, HD), jnp.float32),
            pltpu.SemaphoreType.DMA((5,)),
            pltpu.SemaphoreType.DMA((count + 3,)),
        ],
        compiler_params=pltpu.CompilerParams(vmem_limit_bytes=46 * 2**20),
        name="project",
    )(me[None], *operands[:6])
    rest_cols = 2 * kv_cols + widths[1]
    rest_shapes = parts(rest_cols)
    rest_shapes[1] = jax.ShapeDtypeStruct((per, widths[0] + HD + rest_cols), jnp.bfloat16)
    rest_terms = pl.pallas_call(
        functools.partial(project_rest_kernel, pool, widths[0]),
        out_shape=rest_shapes,
        in_specs=[VMEM] * 3 + [HBM] * 3,
        out_specs=[VMEM] * pool,
        scratch_shapes=[
            pltpu.VMEM((count, deep, rest_cols), jnp.bfloat16),
            pltpu.VMEM((n_rows, rest_cols), jnp.float32),
            pltpu.SemaphoreType.DMA((3, count)),
        ],
        compiler_params=pltpu.CompilerParams(vmem_limit_bytes=40 * 2**20),
        cost_estimate=pl.CostEstimate(
            flops=2 * n_rows * depth * rest_cols,
            bytes_accessed=2 * depth * (rest_cols + n_rows),
            transcendentals=0,
        ),
        name="project_rest",
    )(lhs, pick, first_terms[1], operands[6], operands[7], operands[5])
    first_terms = exchange(first_terms, range(2, pool))
    rest_terms = list(rest_terms)
    early, late = range(2, pool), range(3, pool)
    got, tied = lax.optimization_barrier(
        ([first_terms[k] for k in early], [rest_terms[k] for k in late])
    )
    for k, part in zip(early, got):
        first_terms[k] = part
    for k, part in zip(late, tied):
        rest_terms[k] = part
    rest_terms = exchange(rest_terms, range(1, pool))
    terms = [first_terms[0], rest_terms[0], *rest_terms[2:], *first_terms[2:], rest_terms[1]]

    half = HD // 2
    freq = THETA ** (-(np.arange(half) * 2.0) / HD)
    angles = positions * np.concatenate([freq, freq]).astype(np.float32)[None, :]
    sign = np.concatenate([-np.ones(half), np.ones(half)]).astype(np.float32)[None, :]
    cosines, sines = jnp.cos(angles), jnp.sin(angles) * sign

    found = pl.pallas_call(
        functools.partial(attend_kernel, pool, slots, seg, width_d, q_heads, kv_heads),
        out_shape=[jax.ShapeDtypeStruct((slots * q_heads + LEVELS, HD), jnp.bfloat16)] * pool,
        in_specs=[SMEM] + [VMEM] * (2 * pool + 4),
        out_specs=[VMEM] * pool,
        scratch_shapes=[pltpu.VMEM((q_heads * per, HD), jnp.float32)],
        compiler_params=pltpu.CompilerParams(vmem_limit_bytes=24 * 2**20),
        name="attend",
    )(me[None], *terms, cosines, sines, marks, cache_keys, cache_values)

    found = exchange(found, [*range(2, pool), 1])

    return pl.pallas_call(
        functools.partial(merge_kernel, pool, slots, rows_local, q_heads, kv_heads),
        out_shape=jax.ShapeDtypeStruct((rows_local, q_cols), jnp.bfloat16),
        in_specs=[VMEM] * (2 + pool),
        out_specs=HBM,
        scratch_shapes=[
            pltpu.VMEM((rows_local, q_cols), jnp.bfloat16),
            pltpu.VMEM((per * q_heads, HD), jnp.float32),
            pltpu.SemaphoreType.DMA((4,)),
        ],
        compiler_params=pltpu.CompilerParams(vmem_limit_bytes=24 * 2**20),
        name="merge",
    )(home_slots, home_rows, found[0], *found[2:], found[1])


def solution(mesh):
    return jax.shard_map(
        body,
        mesh=mesh,
        in_specs=(
            P("groups", "pool"),
            P("pool"),
            P("pool", "tensor"),
            P("pool", "tensor"),
            P("pool", "tensor"),
            P(("groups", "pool"), "tensor"),
            P(("groups", "pool"), "tensor"),
            P("groups", None, None),
            P(("groups", "pool"), None, None),
            P("groups"),
        ),
        out_specs=P(("groups", "pool"), "tensor"),
        check_vma=False,
    )
```

```python
import functools

import jax
import jax.numpy as jnp
import numpy as np
from jax import lax
from jax.experimental import pallas as pl
from jax.experimental.pallas import tpu as pltpu
from jax.sharding import PartitionSpec as P

HD = 128
EPS = 1e-05
THETA = 500000.0
LOW = -1e30
DEEP = 512
LEVELS = 16
TILE = 1536


def divides(width, limit):
    while width % limit:
        limit //= 2
    return limit


def tiles(width):
    count = -(-width // TILE)
    each = -(-width // (256 * count)) * 256
    return [(at, min(each, width - at)) for at in range(0, width, each)]


def split3(x):
    a = x.astype(jnp.bfloat16).astype(jnp.float32)
    r = x - a
    b = r.astype(jnp.bfloat16).astype(jnp.float32)
    return a, b, (r - b).astype(jnp.bfloat16).astype(jnp.float32)


def partner(me, k):
    return lax.bitwise_xor(me, k)


def stream(count, pieces, following, ahead):
    def begin():
        for t in range(min(ahead, count)):
            for copy in pieces(t):
                copy.start()
        for copy in following[: max(ahead - count, 0)]:
            copy.start()

    def advance(t):
        @pl.when(t + ahead < count)
        def _():
            for copy in pieces(t + ahead):
                copy.start()

        for j, copy in enumerate(following):
            pl.when(t + ahead == count + j)(copy.start)

    return begin, advance


def add_products(left, block, sums):
    for at, tile in tiles(block.shape[1]):
        sums[:, at : at + tile] += jnp.dot(
            left, block[:, at : at + tile], preferred_element_type=jnp.float32
        )


def spread(chosen, sums, outs, at):
    width = sums.shape[1]
    per = chosen.shape[0] // len(outs)
    rows = jnp.dot(
        chosen, sums.astype(jnp.bfloat16), preferred_element_type=jnp.float32
    ).astype(jnp.bfloat16)
    for k, out in enumerate(outs):
        out[:, at : at + width] = rows[k * per : (k + 1) * per]


def spread_products(chosen, left, block, sums, outs, to):
    for at, tile in tiles(block.shape[1]):
        done = sums[:, at : at + tile] + jnp.dot(
            left, block[:, at : at + tile], preferred_element_type=jnp.float32
        )
        spread(chosen, done, outs, to + at)


def project_kernel(pool, slots, rows_local, me_ref, send, lens, row_len, hidden, gain, *rest):
    w_query, w_key, w_value, *rest = rest
    outs, rest = rest[:pool], rest[pool:]
    lhs, pick, positions, marks, home_rows, home_slots, narrow, *rest = rest
    send_buf, lens_buf, row_len_buf, x_buf, g_buf, *rest = rest
    query_buf, sums, squares, in_sem, sems = rest
    per = pool * slots
    n_rows, depth = x_buf.shape
    count, deep, width = query_buf.shape
    me = me_ref[0]

    def named(home, owner, c):
        if len(send_buf.shape) == 3:
            return send_buf[home, owner, c]
        return send_buf[home * per + owner * slots + c]

    lane = lax.broadcasted_iota(jnp.int32, (1, n_rows), 1)
    place = lax.broadcasted_iota(jnp.int32, (1, HD), 1)
    group = marks.shape[1] // per
    slot_of = lax.broadcasted_iota(jnp.int32, (1, marks.shape[1]), 1) // group

    def choose(i):
        owner = partner(me, i // per)
        s = lax.rem(i, per)
        home = partner(owner, s // slots)
        r = named(home, owner, lax.rem(s, slots))
        row = jnp.where(r >= 0, home * rows_local + r, -1)
        pick[pl.ds(i, 1), :] = (lane == row).astype(jnp.float32)

    def describe(s):
        k, c = s // slots, lax.rem(s, slots)
        home = partner(me, k)
        r = named(home, me, c)
        at = row_len_buf[home * rows_local + jnp.maximum(r, 0)].astype(jnp.float32)
        positions[pl.ds(s, 1), :] = jnp.full((1, HD), at, jnp.float32)
        length = lens_buf[0, home, c] if len(lens_buf.shape) == 3 else lens_buf[home * slots + c]
        earlier = jnp.int32(0)
        for e in range(per):
            same = (named(home, e // slots, e % slots) == r) & (e < me * slots + c)
            earlier = earlier | same.astype(jnp.int32)
        first = jnp.where((earlier == 0) & (r >= 0), 1, 0)
        marks[0:1, :] = jnp.where(slot_of == s, length, marks[0:1, :])
        marks[1:2, :] = jnp.where(slot_of == s, first, marks[1:2, :])
        mine = named(me, home, c)
        home_slots[...] = jnp.where(lax.rem(place, per) == s, mine, home_slots[...])
        home_rows[pl.ds(k, 1), :] = jnp.where(
            lax.rem(place // group, slots) == c, mine, home_rows[pl.ds(k, 1), :]
        )

    chore_steps = 4
    spread_chores = count > chore_steps + 1 and pool * per <= 64 and per % chore_steps == 0

    def each(do, total, t):
        share = -(-total // chore_steps)
        if spread_chores:
            for q in range(share):
                do(t * share + q)
        else:
            assert isinstance(t, int)
            pl.loop(0, total)(do)

    def scale(t):
        at = pl.multiple_of(t * deep, deep)
        x = x_buf[:, pl.ds(at, deep)].astype(jnp.float32)
        gains = g_buf[pl.ds(at, deep)].astype(jnp.float32).reshape(1, deep)
        left = (x * gains).astype(jnp.bfloat16)
        lhs[:, pl.ds(at, deep)] = left
        squared = x * x
        total = squares[...]
        for column in range(0, deep, HD):
            total = total + squared[:, column : column + HD]
        squares[...] = total
        return left

    kv_cols = w_key.shape[1]
    cuts = [0, deep // 4, deep // 2, deep] if count > 1 else [0, deep]

    def pieces(t):
        if isinstance(t, int) and t == 0:
            return [
                pltpu.make_async_copy(
                    w_query.at[a:b, :width], query_buf.at[0, a:b], sems.at[0 if n == 0 else count + n]
                )
                for n, (a, b) in enumerate(zip(cuts[:-1], cuts[1:]))
            ]
        rows = pl.ds(pl.multiple_of(t * deep, deep), deep)
        return [pltpu.make_async_copy(w_query.at[rows, :width], query_buf.at[t], sems.at[t])]

    following = [
        pltpu.make_async_copy(w, target, in_sem.at[5 + n])
        for n, (w, target) in enumerate(
            ((w_key, narrow.at[:, :kv_cols]), (w_value, narrow.at[:, kv_cols:]))
        )
    ]
    begin, advance = stream(count, pieces, following, 3)

    def use(t):
        advance(t)
        left = scale(t)
        for copy in pieces(t):
            copy.wait()
        add_products(left, query_buf.at[t], sums)

    def use_early(t):
        use(t)
        each(choose, pool * per, t - 1)
        each(describe, per, t - 1)

    def use_first():
        advance(0)
        left = scale(0)
        for copy, a, b in zip(pieces(0), cuts[:-1], cuts[1:]):
            copy.wait()
            add_products(left[:, a:b], query_buf.at[0, a:b], sums)

    def use_last(t):
        left = scale(t)
        for copy in pieces(t):
            copy.wait()
        chosen = pick[...].astype(jnp.bfloat16)
        spread_products(chosen, left, query_buf.at[t], sums, outs, 0)
        power = jnp.sum(squares[...], axis=1, keepdims=True)
        at = lax.broadcasted_iota(jnp.int32, (n_rows, HD), 1)
        a, b, c = split3(power)
        parts = jnp.where(at == 0, a, jnp.where(at == 1, b, jnp.where(at == 2, c, 0.0)))
        spread(chosen, parts, outs, sums.shape[1])

    inputs = [
        pltpu.make_async_copy(source, target, in_sem.at[i])
        for i, (source, target) in enumerate(
            (
                (gain, g_buf),
                (hidden, x_buf),
                (send, send_buf),
                (lens, lens_buf),
                (row_len, row_len_buf),
            )
        )
    ]
    for one in inputs:
        one.start()
    begin()
    sums[...] = jnp.zeros(sums.shape, jnp.float32)
    squares[...] = jnp.zeros((n_rows, HD), jnp.float32)
    marks[...] = jnp.zeros(marks.shape, jnp.int32)
    home_rows[...] = jnp.full(home_rows.shape, -1, jnp.int32)
    home_slots[...] = jnp.full(home_slots.shape, -1, jnp.int32)
    for one in inputs:
        one.wait()
    if not spread_chores:
        each(choose, pool * per, 0)
        each(describe, per, 0)
    if count > 1:
        use_first()
    early = 1 + chore_steps if spread_chores else 1
    if spread_chores:
        pl.loop(1, early)(use_early)
    if count > early + 1:
        pl.loop(early, count - 1)(use)
    use_last(count - 1)
    for copy in following:
        copy.wait()


def project_rest_kernel(pool, column, lhs, pick, near, narrow, w_query, *rest):
    outs, (query_buf, sums, sems) = rest[:pool], rest[pool:]
    done = near.shape[1]
    count, deep, _ = query_buf.shape
    chosen = pick[...].astype(jnp.bfloat16)
    targets = [out.at[:, done:] if k == 1 else out for k, out in enumerate(outs)]

    def pieces(t):
        rows = pl.ds(pl.multiple_of(t * deep, deep), deep)
        block = w_query.at[rows, column : column + query_buf.shape[2]]
        return [pltpu.make_async_copy(block, query_buf.at[t], sems.at[t])]

    begin, _ = stream(count, pieces, [], count)
    begin()
    sums[...] = jnp.zeros(sums.shape, jnp.float32)
    outs[1][:, :done] = near[...]
    part = jnp.dot(lhs[...], narrow[...], preferred_element_type=jnp.float32)
    spread(chosen, part, targets, 0)

    @pl.loop(0, count - 1)
    def _(t):
        pieces(t)[0].wait()
        add_products(lhs[:, pl.ds(pl.multiple_of(t * deep, deep), deep)], query_buf.at[t], sums)

    pieces(count - 1)[0].wait()
    left = lhs[:, (count - 1) * deep :]
    spread_products(chosen, left, query_buf.at[count - 1], sums, targets, narrow.shape[1])


def attend_kernel(pool, slots, seg, width_d, q_heads, kv_heads, me_ref, *rest):
    terms, rest = rest[: 2 * pool - 1], rest[2 * pool - 1 :]
    cos, sin, marks, keys, values = rest[:5]
    outs, (q_buf,) = rest[5 : 5 + pool], rest[5 + pool :]
    per = pool * slots
    group = q_heads // kv_heads
    step = HD // group
    scale = HD ** (-0.5)

    own, own_rest, near = terms[0], terms[1], terms[-1]
    far_rest, far = terms[2:pool], terms[pool:-1]
    first_cols, cols = own.shape[1], near.shape[1]

    def total(at):
        if at < first_cols:
            got, others = own[:, at : at + HD], far
        else:
            got, others = own_rest[:, at - first_cols : at - first_cols + HD], far_rest
        got = got.astype(jnp.float32) + near[:, at : at + HD].astype(jnp.float32)
        at = at if at < first_cols else at - first_cols
        for part in others:
            got = got + part[:, at : at + HD].astype(jnp.float32)
        return got

    late = first_cols + 2 * kv_heads * HD
    heads = [*range(0, first_cols - HD, HD), *range(late, cols, HD)]
    power = jnp.sum(total(first_cols - HD), axis=1, keepdims=True)
    factor = lax.rsqrt(power * (1.0 / width_d) + EPS)
    cosines, sines = cos[...], sin[...]

    def rounded(x):
        return x.astype(jnp.bfloat16).astype(jnp.float32)

    def rotated(x):
        return rounded(x * cosines + pltpu.roll(x, HD // 2, axis=1) * sines)

    for i in range(q_heads):
        q_buf[i * per : (i + 1) * per, :] = rotated(total(heads[i]) * factor)
    keys_own = [rotated(total(first_cols + g * HD) * factor) for g in range(kv_heads)]
    values_own = [
        rounded(total(first_cols + (kv_heads + g) * HD) * factor) for g in range(kv_heads)
    ]

    me = me_ref[0]

    def base(j):
        return pl.multiple_of(partner(me, j) * (slots * seg), slots * seg)

    lane = lax.broadcasted_iota(jnp.int32, (1, HD), 1)
    slot_of = lane // group
    at = lax.broadcasted_iota(jnp.int32, (seg, HD), 0)
    at_own = lax.broadcasted_iota(jnp.int32, (step, HD), 0)
    blocks = [(g, s) for s in range(0, per, step) for g in range(kv_heads)]
    columns = []
    for g, s in blocks:
        query = jnp.concatenate(
            [q_buf[pl.ds(g * group * per + s + u, group, stride=per), :] for u in range(step)], 0
        )
        columns.append(query.T.astype(jnp.bfloat16))
    scores = []
    for (g, s), query in zip(blocks, columns):
        score = None
        for u in range(0, step, slots):
            wide = jnp.dot(
                keys[pl.ds(base((s + u) // slots), slots * seg), g * HD : (g + 1) * HD],
                query,
                preferred_element_type=jnp.float32,
            )
            for c in range(slots):
                each = wide[c * seg : (c + 1) * seg]
                score = each if score is None else jnp.where(slot_of == u + c, each, score)
        own = jnp.dot(
            keys_own[g][s : s + step].astype(jnp.bfloat16),
            query,
            preferred_element_type=jnp.float32,
        )
        own = jnp.sum(jnp.where(at_own == slot_of, own, 0.0), axis=0, keepdims=True)
        scores.append((score * scale, own * scale))
    turned, levels = [], {}
    for (g, s), (score, own) in zip(blocks, scores):
        length = marks[0:1, s * group : s * group + HD]
        with_own = marks[1:2, s * group : s * group + HD] > 0
        usable = at < length
        own = jnp.where(with_own, own, LOW)
        top = jnp.maximum(jnp.max(jnp.where(usable, score, LOW), axis=0, keepdims=True), own)
        weight = jnp.where(usable, jnp.exp(score - top), 0.0)
        weight_own = jnp.where(with_own, jnp.exp(own - top), 0.0)
        sums = jnp.sum(weight, axis=0, keepdims=True) + weight_own
        sums = jnp.where(length > 0, sums, 1.0)
        level = top + jnp.log(sums)
        for u in range(0, step, slots):
            at_lane = g * slots * group
            moved = level if at_lane == u * group else pltpu.roll(level, (at_lane - u * group) % HD, axis=1)
            there = (lane >= at_lane) & (lane < at_lane + slots * group)
            home = (s + u) // slots
            levels[home] = jnp.where(there, moved, levels.get(home, 0.0))
        rows = [weight_own, 1.0 / sums, jnp.zeros((HD - seg - 2, HD), jnp.float32)]
        turned.append(jnp.concatenate([weight] + rows, 0).T)
    for (g, s), block in zip(blocks, turned):
        for u in range(step):
            home, c = (s + u) // slots, (s + u) % slots
            rows = block[u * group : (u + 1) * group]
            mixed = jnp.dot(
                rows[:, :seg].astype(jnp.bfloat16),
                values[pl.ds(base(home) + c * seg, seg), g * HD : (g + 1) * HD],
                preferred_element_type=jnp.float32,
            )
            mixed = mixed + rows[:, seg : seg + 1] * values_own[g][s + u : s + u + 1]
            to = c * q_heads + g * group
            outs[home][to : to + group, :] = (mixed * rows[:, seg + 1 : seg + 2]).astype(jnp.bfloat16)
    for home, level in levels.items():
        block = jnp.concatenate([*split3(level), jnp.zeros((LEVELS - 3, HD), jnp.float32)], 0)
        outs[home][slots * q_heads :, :] = block.astype(jnp.bfloat16)


def merge_kernel(pool, slots, rows_local, q_heads, kv_heads, slots_ref, rows_ref, own, *rest):
    found, (out, buf, scaled, sems) = [own, rest[pool - 2], *rest[: pool - 2]], rest[pool - 1 :]
    per = pool * slots
    group = q_heads // kv_heads
    block = slots * q_heads
    span = slots * group
    level = jnp.concatenate(
        [jnp.sum(part[block : block + LEVELS, :].astype(jnp.float32), 0, keepdims=True) for part in found], 0
    )
    named = rows_ref[...]
    lane = lax.broadcasted_iota(jnp.int32, (pool, HD), 1)

    def turns(x):
        for c in range(slots):
            y = x
            if c:
                y = jnp.where(
                    lax.rem(lane, span) < span - c * group,
                    pltpu.roll(x, HD - c * group, axis=1),
                    pltpu.roll(x, span - c * group, axis=1),
                )
            for k in range(pool):
                yield jnp.concatenate([y[k:], y[:k]], 0) if k else y

    same = [other == named for other in turns(named)]
    top = level
    for match, other in zip(same, turns(level)):
        top = jnp.maximum(top, jnp.where(match, other, LOW))
    weight = jnp.exp(level - top)
    total = jnp.zeros_like(weight)
    for match, other in zip(same, turns(weight)):
        total = total + jnp.where(match, other, 0.0)
    share = jnp.where(named >= 0, weight / total, 0.0)
    share = jnp.concatenate([share, jnp.zeros((HD - pool, HD), jnp.float32)], 0).T
    for k in range(pool):
        for c in range(slots):
            for g in range(kv_heads):
                at = c * q_heads + g * group
                each = g * span + c * group
                scaled[k * block + at : k * block + at + group, :] = (
                    found[k][at : at + group, :].astype(jnp.float32)
                    * share[each : each + group, k : k + 1]
                )
    row = lax.broadcasted_iota(jnp.int32, (rows_local, 2 * per), 0)
    match = (slots_ref[:, : 2 * per] == row).astype(jnp.float32).astype(jnp.bfloat16)
    quarter = q_heads // 4
    copies = [
        pltpu.make_async_copy(buf.at[:, columns], out.at[:, columns], sems.at[n])
        for n, columns in enumerate(pl.ds(n * quarter * HD, quarter * HD) for n in range(4))
    ]
    for i in range(q_heads):
        part = scaled[pl.ds(i, per, stride=q_heads), :]
        high = part.astype(jnp.bfloat16)
        low = (part - high.astype(jnp.float32)).astype(jnp.bfloat16)
        buf[:, i * HD : (i + 1) * HD] = jnp.dot(
            match, jnp.concatenate([high, low], 0), preferred_element_type=jnp.float32
        ).astype(jnp.bfloat16)
        if (i + 1) % quarter == 0:
            copies[i // quarter].start()
    for copy in copies:
        copy.wait()


def exchange(parts, order):
    got = list(parts)
    for k in order:
        got[k] = lax.ppermute(parts[k], "pool", [(i, i ^ k) for i in range(len(parts))])
    return got


def in_hbm(x):
    return pltpu.with_memory_space_constraint(x, pltpu.HBM)


SMEM = pl.BlockSpec(memory_space=pltpu.SMEM)
VMEM = pl.BlockSpec(memory_space=pltpu.VMEM)
HBM = pl.BlockSpec(memory_space=pltpu.HBM)


def body(
    hidden_in,
    norm_gain,
    w_query,
    w_key,
    w_value,
    cache_keys,
    cache_values,
    send_row,
    piece_len,
    row_len,
):
    pool = lax.axis_size("pool")
    me = lax.axis_index("pool").astype(jnp.int32)
    n_rows, depth = hidden_in.shape
    width_d = depth * pool
    rows_local = n_rows // pool
    slots = send_row.shape[2]
    per = pool * slots
    seg = cache_keys.shape[0] // per
    q_cols, kv_cols = w_query.shape[1], w_key.shape[1]
    q_heads, kv_heads = q_cols // HD, kv_cols // HD
    group = q_heads // kv_heads
    cols = q_cols + 2 * kv_cols + HD

    if pool <= 8:
        indices = [send_row, piece_len, row_len]
    else:
        indices = [send_row.reshape(-1), piece_len.reshape(-1), row_len]
    deep = divides(depth, DEEP)
    count = depth // deep
    widths = [11 * q_cols // 16, 5 * q_cols // 16]


    def parts(width):
        return [jax.ShapeDtypeStruct((per, width), jnp.bfloat16)] * pool

    operands = [in_hbm(x) for x in (*indices, hidden_in, norm_gain, w_query, w_key, w_value)]
    *first_terms, lhs, pick, positions, marks, home_rows, home_slots, narrow = pl.pallas_call(
        functools.partial(project_kernel, pool, slots, rows_local),
        out_shape=[
            *parts(widths[0] + HD),
            jax.ShapeDtypeStruct((n_rows, depth), jnp.bfloat16),
            jax.ShapeDtypeStruct((pool * per, n_rows), jnp.float32),
            jax.ShapeDtypeStruct((per, HD), jnp.float32),
            jax.ShapeDtypeStruct((2, per * group), jnp.int32),
            jax.ShapeDtypeStruct((pool, HD), jnp.int32),
            jax.ShapeDtypeStruct((1, HD), jnp.int32),
            jax.ShapeDtypeStruct((depth, 2 * kv_cols), jnp.bfloat16),
        ],
        in_specs=[SMEM] + [HBM] * 8,
        out_specs=[VMEM] * (pool + 7),
        scratch_shapes=[
            *(pltpu.SMEM(x.shape, jnp.int32) for x in indices),
            pltpu.VMEM((n_rows, depth), jnp.bfloat16),
            pltpu.VMEM((depth,), jnp.bfloat16),
            pltpu.VMEM((count, deep, widths[0]), jnp.bfloat16),
            pltpu.VMEM((n_rows, widths[0]), jnp.float32),
            pltpu.VMEM((n_rows, HD), jnp.float32),
            pltpu.SemaphoreType.DMA((7,)),
            pltpu.SemaphoreType.DMA((count + 3,)),
        ],
        compiler_params=pltpu.CompilerParams(vmem_limit_bytes=46 * 2**20),
        name="project",
    )(me[None], *operands)
    rest_cols = 2 * kv_cols + widths[1]
    rest_shapes = parts(rest_cols)
    rest_shapes[1] = jax.ShapeDtypeStruct((per, widths[0] + HD + rest_cols), jnp.bfloat16)
    rest_terms = pl.pallas_call(
        functools.partial(project_rest_kernel, pool, widths[0]),
        out_shape=rest_shapes,
        in_specs=[VMEM] * 4 + [HBM],
        out_specs=[VMEM] * pool,
        scratch_shapes=[
            pltpu.VMEM((count, deep, widths[1]), jnp.bfloat16),
            pltpu.VMEM((n_rows, widths[1]), jnp.float32),
            pltpu.SemaphoreType.DMA((count,)),
        ],
        compiler_params=pltpu.CompilerParams(vmem_limit_bytes=40 * 2**20),
        cost_estimate=pl.CostEstimate(
            flops=2 * n_rows * depth * rest_cols,
            bytes_accessed=2 * depth * (rest_cols + n_rows),
            transcendentals=0,
        ),
        name="project_rest",
    )(lhs, pick, first_terms[1], narrow, operands[5])
    first_terms = exchange(first_terms, range(2, pool))
    rest_terms = list(rest_terms)
    early, late = range(2, pool), range(3, pool)
    got, tied = lax.optimization_barrier(
        ([first_terms[k] for k in early], [rest_terms[k] for k in late])
    )
    for k, part in zip(early, got):
        first_terms[k] = part
    for k, part in zip(late, tied):
        rest_terms[k] = part
    rest_terms = exchange(rest_terms, range(1, pool))
    terms = [first_terms[0], rest_terms[0], *rest_terms[2:], *first_terms[2:], rest_terms[1]]

    half = HD // 2
    freq = THETA ** (-(np.arange(half) * 2.0) / HD)
    angles = positions * np.concatenate([freq, freq]).astype(np.float32)[None, :]
    sign = np.concatenate([-np.ones(half), np.ones(half)]).astype(np.float32)[None, :]
    cosines, sines = jnp.cos(angles), jnp.sin(angles) * sign

    found = pl.pallas_call(
        functools.partial(attend_kernel, pool, slots, seg, width_d, q_heads, kv_heads),
        out_shape=[jax.ShapeDtypeStruct((slots * q_heads + LEVELS, HD), jnp.bfloat16)] * pool,
        in_specs=[SMEM] + [VMEM] * (2 * pool + 4),
        out_specs=[VMEM] * pool,
        scratch_shapes=[pltpu.VMEM((q_heads * per, HD), jnp.float32)],
        compiler_params=pltpu.CompilerParams(vmem_limit_bytes=24 * 2**20),
        name="attend",
    )(me[None], *terms, cosines, sines, marks, cache_keys, cache_values)

    found = exchange(found, [*range(2, pool), 1])

    return pl.pallas_call(
        functools.partial(merge_kernel, pool, slots, rows_local, q_heads, kv_heads),
        out_shape=jax.ShapeDtypeStruct((rows_local, q_cols), jnp.bfloat16),
        in_specs=[VMEM] * (2 + pool),
        out_specs=HBM,
        scratch_shapes=[
            pltpu.VMEM((rows_local, q_cols), jnp.bfloat16),
            pltpu.VMEM((per * q_heads, HD), jnp.float32),
            pltpu.SemaphoreType.DMA((4,)),
        ],
        compiler_params=pltpu.CompilerParams(vmem_limit_bytes=24 * 2**20),
        name="merge",
    )(home_slots, home_rows, found[0], *found[2:], found[1])


def solution(mesh):
    return jax.shard_map(
        body,
        mesh=mesh,
        in_specs=(
            P("groups", "pool"),
            P("pool"),
            P("pool", "tensor"),
            P("pool", "tensor"),
            P("pool", "tensor"),
            P(("groups", "pool"), "tensor"),
            P(("groups", "pool"), "tensor"),
            P("groups", None, None),
            P(("groups", "pool"), None, None),
            P("groups"),
        ),
        out_specs=P(("groups", "pool"), "tensor"),
        check_vma=False,
    )
```

```python
import functools

import jax
import jax.numpy as jnp
import numpy as np
from jax import lax
from jax.experimental import pallas as pl
from jax.experimental.pallas import tpu as pltpu
from jax.sharding import PartitionSpec as P

HD = 128
EPS = 1e-05
THETA = 500000.0
LOW = -1e30
DEEP = 1024
LEVELS = 16
TILE = 1536


def divides(width, limit):
    while width % limit:
        limit //= 2
    return limit


def tiles(width):
    count = -(-width // TILE)
    each = -(-width // (256 * count)) * 256
    return [(at, min(each, width - at)) for at in range(0, width, each)]


def split3(x):
    a = x.astype(jnp.bfloat16).astype(jnp.float32)
    r = x - a
    b = r.astype(jnp.bfloat16).astype(jnp.float32)
    return a, b, (r - b).astype(jnp.bfloat16).astype(jnp.float32)


def partner(me, k):
    return lax.bitwise_xor(me, k)


def stream(count, pieces, following, ahead):
    def begin():
        for t in range(min(ahead, count)):
            for copy in pieces(t):
                copy.start()
        for copy in following[: max(ahead - count, 0)]:
            copy.start()

    def advance(t):
        @pl.when(t + ahead < count)
        def _():
            for copy in pieces(t + ahead):
                copy.start()

        for j, copy in enumerate(following):
            pl.when(t + ahead == count + j)(copy.start)

    return begin, advance


def add_products(left, block, sums):
    for at, tile in tiles(block.shape[1]):
        sums[:, at : at + tile] += jnp.dot(
            left, block[:, at : at + tile], preferred_element_type=jnp.float32
        )


def spread(chosen, sums, outs, at):
    width = sums.shape[1]
    per = chosen.shape[0] // len(outs)
    rows = jnp.dot(
        chosen, sums.astype(jnp.bfloat16), preferred_element_type=jnp.float32
    ).astype(jnp.bfloat16)
    for k, out in enumerate(outs):
        out[:, at : at + width] = rows[k * per : (k + 1) * per]


def spread_products(chosen, left, block, sums, outs, to):
    for at, tile in tiles(block.shape[1]):
        done = sums[:, at : at + tile] + jnp.dot(
            left, block[:, at : at + tile], preferred_element_type=jnp.float32
        )
        spread(chosen, done, outs, to + at)


def project_kernel(pool, slots, rows_local, me_ref, send, lens, row_len, hidden, gain, *rest):
    w_query, w_key, w_value, *rest = rest
    outs, rest = rest[:pool], rest[pool:]
    lhs, pick, positions, marks, home_rows, home_slots, narrow, *rest = rest
    send_buf, lens_buf, row_len_buf, x_buf, g_buf, *rest = rest
    query_buf, sums, squares, in_sem, sems = rest
    per = pool * slots
    n_rows, depth = x_buf.shape
    count, deep, width = query_buf.shape
    me = me_ref[0]

    def named(home, owner, c):
        if len(send_buf.shape) == 3:
            return send_buf[home, owner, c]
        return send_buf[home * per + owner * slots + c]

    lane = lax.broadcasted_iota(jnp.int32, (1, n_rows), 1)
    place = lax.broadcasted_iota(jnp.int32, (1, HD), 1)
    group = marks.shape[1] // per
    slot_of = lax.broadcasted_iota(jnp.int32, (1, marks.shape[1]), 1) // group

    def choose(i):
        owner = partner(me, i // per)
        s = lax.rem(i, per)
        home = partner(owner, s // slots)
        r = named(home, owner, lax.rem(s, slots))
        row = jnp.where(r >= 0, home * rows_local + r, -1)
        pick[pl.ds(i, 1), :] = (lane == row).astype(jnp.float32)

    def describe(s):
        k, c = s // slots, lax.rem(s, slots)
        home = partner(me, k)
        r = named(home, me, c)
        at = row_len_buf[home * rows_local + jnp.maximum(r, 0)].astype(jnp.float32)
        positions[pl.ds(s, 1), :] = jnp.full((1, HD), at, jnp.float32)
        length = lens_buf[0, home, c] if len(lens_buf.shape) == 3 else lens_buf[home * slots + c]
        earlier = jnp.int32(0)
        for e in range(per):
            same = (named(home, e // slots, e % slots) == r) & (e < me * slots + c)
            earlier = earlier | same.astype(jnp.int32)
        first = jnp.where((earlier == 0) & (r >= 0), 1, 0)
        marks[0:1, :] = jnp.where(slot_of == s, length, marks[0:1, :])
        marks[1:2, :] = jnp.where(slot_of == s, first, marks[1:2, :])
        mine = named(me, home, c)
        home_slots[...] = jnp.where(lax.rem(place, per) == s, mine, home_slots[...])
        home_rows[pl.ds(k, 1), :] = jnp.where(
            lax.rem(place // group, slots) == c, mine, home_rows[pl.ds(k, 1), :]
        )

    chore_steps = 2
    spread_chores = count > chore_steps + 1 and pool * per <= 64 and per % chore_steps == 0

    def each(do, total, t):
        share = -(-total // chore_steps)
        if spread_chores:
            for q in range(share):
                do(t * share + q)
        else:
            assert isinstance(t, int)
            pl.loop(0, total)(do)

    def scale(t):
        at = pl.multiple_of(t * deep, deep)
        x = x_buf[:, pl.ds(at, deep)].astype(jnp.float32)
        gains = g_buf[pl.ds(at, deep)].astype(jnp.float32).reshape(1, deep)
        left = (x * gains).astype(jnp.bfloat16)
        lhs[:, pl.ds(at, deep)] = left
        squared = x * x
        total = squares[...]
        for column in range(0, deep, HD):
            total = total + squared[:, column : column + HD]
        squares[...] = total
        return left

    kv_cols = w_key.shape[1]
    cuts = [0, deep // 8, deep // 4, deep // 2, deep] if count > 1 else [0, deep]

    def pieces(t):
        if isinstance(t, int) and t == 0:
            return [
                pltpu.make_async_copy(
                    w_query.at[a:b, :width], query_buf.at[0, a:b], sems.at[0 if n == 0 else count + n]
                )
                for n, (a, b) in enumerate(zip(cuts[:-1], cuts[1:]))
            ]
        rows = pl.ds(pl.multiple_of(t * deep, deep), deep)
        return [pltpu.make_async_copy(w_query.at[rows, :width], query_buf.at[t], sems.at[t])]

    following = [
        pltpu.make_async_copy(w, target, in_sem.at[5 + n])
        for n, (w, target) in enumerate(
            ((w_key, narrow.at[:, :kv_cols]), (w_value, narrow.at[:, kv_cols:]))
        )
    ]
    begin, advance = stream(count, pieces, following, 2)

    def use(t):
        advance(t)
        left = scale(t)
        for copy in pieces(t):
            copy.wait()
        add_products(left, query_buf.at[t], sums)

    def use_early(t):
        use(t)
        each(choose, pool * per, t - 1)
        each(describe, per, t - 1)

    def use_first():
        advance(0)
        left = scale(0)
        for copy, a, b in zip(pieces(0), cuts[:-1], cuts[1:]):
            copy.wait()
            add_products(left[:, a:b], query_buf.at[0, a:b], sums)

    def use_last(t):
        advance(t)
        left = scale(t)
        for copy in pieces(t):
            copy.wait()
        chosen = pick[...].astype(jnp.bfloat16)
        spread_products(chosen, left, query_buf.at[t], sums, outs, 0)
        power = jnp.sum(squares[...], axis=1, keepdims=True)
        at = lax.broadcasted_iota(jnp.int32, (n_rows, HD), 1)
        a, b, c = split3(power)
        parts = jnp.where(at == 0, a, jnp.where(at == 1, b, jnp.where(at == 2, c, 0.0)))
        spread(chosen, parts, outs, sums.shape[1])

    inputs = [
        pltpu.make_async_copy(source, target, in_sem.at[i])
        for i, (source, target) in enumerate(
            (
                (gain, g_buf),
                (hidden, x_buf),
                (send, send_buf),
                (lens, lens_buf),
                (row_len, row_len_buf),
            )
        )
    ]
    for one in inputs:
        one.start()
    begin()
    sums[...] = jnp.zeros(sums.shape, jnp.float32)
    squares[...] = jnp.zeros((n_rows, HD), jnp.float32)
    marks[...] = jnp.zeros(marks.shape, jnp.int32)
    home_rows[...] = jnp.full(home_rows.shape, -1, jnp.int32)
    home_slots[...] = jnp.full(home_slots.shape, -1, jnp.int32)
    for one in inputs:
        one.wait()
    if not spread_chores:
        each(choose, pool * per, 0)
        each(describe, per, 0)
    if count > 1:
        use_first()
    early = 1 + chore_steps if spread_chores else 1
    if spread_chores:
        pl.loop(1, early)(use_early)
    if count > early + 1:
        pl.loop(early, count - 1)(use)
    use_last(count - 1)
    for copy in following:
        copy.wait()


def project_rest_kernel(pool, column, lhs, pick, near, narrow, w_query, *rest):
    outs, (query_buf, sums, sems) = rest[:pool], rest[pool:]
    done = near.shape[1]
    count, deep, _ = query_buf.shape
    chosen = pick[...].astype(jnp.bfloat16)
    targets = [out.at[:, done:] if k == 1 else out for k, out in enumerate(outs)]

    def pieces(t):
        rows = pl.ds(pl.multiple_of(t * deep, deep), deep)
        block = w_query.at[rows, column : column + query_buf.shape[2]]
        return [pltpu.make_async_copy(block, query_buf.at[t], sems.at[t])]

    begin, _ = stream(count, pieces, [], count)
    begin()
    sums[...] = jnp.zeros(sums.shape, jnp.float32)
    outs[1][:, :done] = near[...]
    part = jnp.dot(lhs[...], narrow[...], preferred_element_type=jnp.float32)
    spread(chosen, part, targets, 0)

    @pl.loop(0, count - 1)
    def _(t):
        pieces(t)[0].wait()
        add_products(lhs[:, pl.ds(pl.multiple_of(t * deep, deep), deep)], query_buf.at[t], sums)

    pieces(count - 1)[0].wait()
    left = lhs[:, (count - 1) * deep :]
    spread_products(chosen, left, query_buf.at[count - 1], sums, targets, narrow.shape[1])


def attend_kernel(pool, slots, seg, width_d, q_heads, kv_heads, me_ref, *rest):
    terms, rest = rest[: 2 * pool - 1], rest[2 * pool - 1 :]
    cos, sin, marks, keys, values = rest[:5]
    outs, (q_buf,) = rest[5 : 5 + pool], rest[5 + pool :]
    per = pool * slots
    group = q_heads // kv_heads
    step = HD // group
    scale = HD ** (-0.5)

    own, own_rest, near = terms[0], terms[1], terms[-1]
    far_rest, far = terms[2:pool], terms[pool:-1]
    first_cols, cols = own.shape[1], near.shape[1]

    def total(at):
        if at < first_cols:
            got, others = own[:, at : at + HD], far
        else:
            got, others = own_rest[:, at - first_cols : at - first_cols + HD], far_rest
        got = got.astype(jnp.float32) + near[:, at : at + HD].astype(jnp.float32)
        at = at if at < first_cols else at - first_cols
        for part in others:
            got = got + part[:, at : at + HD].astype(jnp.float32)
        return got

    late = first_cols + 2 * kv_heads * HD
    heads = [*range(0, first_cols - HD, HD), *range(late, cols, HD)]
    power = jnp.sum(total(first_cols - HD), axis=1, keepdims=True)
    factor = lax.rsqrt(power * (1.0 / width_d) + EPS)
    cosines, sines = cos[...], sin[...]

    def rounded(x):
        return x.astype(jnp.bfloat16).astype(jnp.float32)

    def rotated(x):
        return rounded(x * cosines + pltpu.roll(x, HD // 2, axis=1) * sines)

    for i in range(q_heads):
        q_buf[i * per : (i + 1) * per, :] = rotated(total(heads[i]) * factor)
    keys_own = [rotated(total(first_cols + g * HD) * factor) for g in range(kv_heads)]
    values_own = [
        rounded(total(first_cols + (kv_heads + g) * HD) * factor) for g in range(kv_heads)
    ]

    me = me_ref[0]

    def base(j):
        return pl.multiple_of(partner(me, j) * (slots * seg), slots * seg)

    lane = lax.broadcasted_iota(jnp.int32, (1, HD), 1)
    slot_of = lane // group
    at = lax.broadcasted_iota(jnp.int32, (seg, HD), 0)
    at_own = lax.broadcasted_iota(jnp.int32, (step, HD), 0)
    blocks = [(g, s) for s in range(0, per, step) for g in range(kv_heads)]
    columns = []
    for g, s in blocks:
        query = jnp.concatenate(
            [q_buf[pl.ds(g * group * per + s + u, group, stride=per), :] for u in range(step)], 0
        )
        columns.append(query.T.astype(jnp.bfloat16))
    scores = []
    for (g, s), query in zip(blocks, columns):
        score = None
        for u in range(0, step, slots):
            wide = jnp.dot(
                keys[pl.ds(base((s + u) // slots), slots * seg), g * HD : (g + 1) * HD],
                query,
                preferred_element_type=jnp.float32,
            )
            for c in range(slots):
                each = wide[c * seg : (c + 1) * seg]
                score = each if score is None else jnp.where(slot_of == u + c, each, score)
        own = jnp.dot(
            keys_own[g][s : s + step].astype(jnp.bfloat16),
            query,
            preferred_element_type=jnp.float32,
        )
        own = jnp.sum(jnp.where(at_own == slot_of, own, 0.0), axis=0, keepdims=True)
        scores.append((score * scale, own * scale))
    turned, levels = [], {}
    for (g, s), (score, own) in zip(blocks, scores):
        length = marks[0:1, s * group : s * group + HD]
        with_own = marks[1:2, s * group : s * group + HD] > 0
        usable = at < length
        own = jnp.where(with_own, own, LOW)
        top = jnp.maximum(jnp.max(jnp.where(usable, score, LOW), axis=0, keepdims=True), own)
        weight = jnp.where(usable, jnp.exp(score - top), 0.0)
        weight_own = jnp.where(with_own, jnp.exp(own - top), 0.0)
        sums = jnp.sum(weight, axis=0, keepdims=True) + weight_own
        sums = jnp.where(length > 0, sums, 1.0)
        level = top + jnp.log(sums)
        for u in range(0, step, slots):
            at_lane = g * slots * group
            moved = level if at_lane == u * group else pltpu.roll(level, (at_lane - u * group) % HD, axis=1)
            there = (lane >= at_lane) & (lane < at_lane + slots * group)
            home = (s + u) // slots
            levels[home] = jnp.where(there, moved, levels.get(home, 0.0))
        rows = [weight_own, 1.0 / sums, jnp.zeros((HD - seg - 2, HD), jnp.float32)]
        turned.append(jnp.concatenate([weight] + rows, 0).T)
    for (g, s), block in zip(blocks, turned):
        for u in range(step):
            home, c = (s + u) // slots, (s + u) % slots
            rows = block[u * group : (u + 1) * group]
            mixed = jnp.dot(
                rows[:, :seg].astype(jnp.bfloat16),
                values[pl.ds(base(home) + c * seg, seg), g * HD : (g + 1) * HD],
                preferred_element_type=jnp.float32,
            )
            mixed = mixed + rows[:, seg : seg + 1] * values_own[g][s + u : s + u + 1]
            to = c * q_heads + g * group
            outs[home][to : to + group, :] = (mixed * rows[:, seg + 1 : seg + 2]).astype(jnp.bfloat16)
    for home, level in levels.items():
        block = jnp.concatenate([*split3(level), jnp.zeros((LEVELS - 3, HD), jnp.float32)], 0)
        outs[home][slots * q_heads :, :] = block.astype(jnp.bfloat16)


def merge_kernel(pool, slots, rows_local, q_heads, kv_heads, slots_ref, rows_ref, own, *rest):
    found, (out, buf, scaled, sems) = [own, rest[pool - 2], *rest[: pool - 2]], rest[pool - 1 :]
    per = pool * slots
    group = q_heads // kv_heads
    block = slots * q_heads
    span = slots * group
    level = jnp.concatenate(
        [jnp.sum(part[block : block + LEVELS, :].astype(jnp.float32), 0, keepdims=True) for part in found], 0
    )
    named = rows_ref[...]
    lane = lax.broadcasted_iota(jnp.int32, (pool, HD), 1)

    def turns(x):
        for c in range(slots):
            y = x
            if c:
                y = jnp.where(
                    lax.rem(lane, span) < span - c * group,
                    pltpu.roll(x, HD - c * group, axis=1),
                    pltpu.roll(x, span - c * group, axis=1),
                )
            for k in range(pool):
                yield jnp.concatenate([y[k:], y[:k]], 0) if k else y

    same = [other == named for other in turns(named)]
    top = level
    for match, other in zip(same, turns(level)):
        top = jnp.maximum(top, jnp.where(match, other, LOW))
    weight = jnp.exp(level - top)
    total = jnp.zeros_like(weight)
    for match, other in zip(same, turns(weight)):
        total = total + jnp.where(match, other, 0.0)
    share = jnp.where(named >= 0, weight / total, 0.0)
    share = jnp.concatenate([share, jnp.zeros((HD - pool, HD), jnp.float32)], 0).T
    for k in range(pool):
        for c in range(slots):
            for g in range(kv_heads):
                at = c * q_heads + g * group
                each = g * span + c * group
                scaled[k * block + at : k * block + at + group, :] = (
                    found[k][at : at + group, :].astype(jnp.float32)
                    * share[each : each + group, k : k + 1]
                )
    row = lax.broadcasted_iota(jnp.int32, (rows_local, 2 * per), 0)
    match = (slots_ref[:, : 2 * per] == row).astype(jnp.float32).astype(jnp.bfloat16)
    quarter = q_heads // 4
    copies = [
        pltpu.make_async_copy(buf.at[:, columns], out.at[:, columns], sems.at[n])
        for n, columns in enumerate(pl.ds(n * quarter * HD, quarter * HD) for n in range(4))
    ]
    for i in range(q_heads):
        part = scaled[pl.ds(i, per, stride=q_heads), :]
        high = part.astype(jnp.bfloat16)
        low = (part - high.astype(jnp.float32)).astype(jnp.bfloat16)
        buf[:, i * HD : (i + 1) * HD] = jnp.dot(
            match, jnp.concatenate([high, low], 0), preferred_element_type=jnp.float32
        ).astype(jnp.bfloat16)
        if (i + 1) % quarter == 0:
            copies[i // quarter].start()
    for copy in copies:
        copy.wait()


def exchange(parts, order):
    got = list(parts)
    for k in order:
        got[k] = lax.ppermute(parts[k], "pool", [(i, i ^ k) for i in range(len(parts))])
    return got


def in_hbm(x):
    return pltpu.with_memory_space_constraint(x, pltpu.HBM)


SMEM = pl.BlockSpec(memory_space=pltpu.SMEM)
VMEM = pl.BlockSpec(memory_space=pltpu.VMEM)
HBM = pl.BlockSpec(memory_space=pltpu.HBM)


def body(
    hidden_in,
    norm_gain,
    w_query,
    w_key,
    w_value,
    cache_keys,
    cache_values,
    send_row,
    piece_len,
    row_len,
):
    pool = lax.axis_size("pool")
    me = lax.axis_index("pool").astype(jnp.int32)
    n_rows, depth = hidden_in.shape
    width_d = depth * pool
    rows_local = n_rows // pool
    slots = send_row.shape[2]
    per = pool * slots
    seg = cache_keys.shape[0] // per
    q_cols, kv_cols = w_query.shape[1], w_key.shape[1]
    q_heads, kv_heads = q_cols // HD, kv_cols // HD
    group = q_heads // kv_heads
    cols = q_cols + 2 * kv_cols + HD

    if pool <= 8:
        indices = [send_row, piece_len, row_len]
    else:
        indices = [send_row.reshape(-1), piece_len.reshape(-1), row_len]
    deep = divides(depth, DEEP)
    count = depth // deep
    widths = [11 * q_cols // 16, 5 * q_cols // 16]


    def parts(width):
        return [jax.ShapeDtypeStruct((per, width), jnp.bfloat16)] * pool

    operands = [in_hbm(x) for x in (*indices, hidden_in, norm_gain, w_query, w_key, w_value)]
    *first_terms, lhs, pick, positions, marks, home_rows, home_slots, narrow = pl.pallas_call(
        functools.partial(project_kernel, pool, slots, rows_local),
        out_shape=[
            *parts(widths[0] + HD),
            jax.ShapeDtypeStruct((n_rows, depth), jnp.bfloat16),
            jax.ShapeDtypeStruct((pool * per, n_rows), jnp.float32),
            jax.ShapeDtypeStruct((per, HD), jnp.float32),
            jax.ShapeDtypeStruct((2, per * group), jnp.int32),
            jax.ShapeDtypeStruct((pool, HD), jnp.int32),
            jax.ShapeDtypeStruct((1, HD), jnp.int32),
            jax.ShapeDtypeStruct((depth, 2 * kv_cols), jnp.bfloat16),
        ],
        in_specs=[SMEM] + [HBM] * 8,
        out_specs=[VMEM] * (pool + 7),
        scratch_shapes=[
            *(pltpu.SMEM(x.shape, jnp.int32) for x in indices),
            pltpu.VMEM((n_rows, depth), jnp.bfloat16),
            pltpu.VMEM((depth,), jnp.bfloat16),
            pltpu.VMEM((count, deep, widths[0]), jnp.bfloat16),
            pltpu.VMEM((n_rows, widths[0]), jnp.float32),
            pltpu.VMEM((n_rows, HD), jnp.float32),
            pltpu.SemaphoreType.DMA((7,)),
            pltpu.SemaphoreType.DMA((count + 4,)),
        ],
        compiler_params=pltpu.CompilerParams(vmem_limit_bytes=46 * 2**20),
        name="project",
    )(me[None], *operands)
    rest_cols = 2 * kv_cols + widths[1]
    rest_shapes = parts(rest_cols)
    rest_shapes[1] = jax.ShapeDtypeStruct((per, widths[0] + HD + rest_cols), jnp.bfloat16)
    rest_terms = pl.pallas_call(
        functools.partial(project_rest_kernel, pool, widths[0]),
        out_shape=rest_shapes,
        in_specs=[VMEM] * 4 + [HBM],
        out_specs=[VMEM] * pool,
        scratch_shapes=[
            pltpu.VMEM((count, deep, widths[1]), jnp.bfloat16),
            pltpu.VMEM((n_rows, widths[1]), jnp.float32),
            pltpu.SemaphoreType.DMA((count,)),
        ],
        compiler_params=pltpu.CompilerParams(vmem_limit_bytes=40 * 2**20),
        cost_estimate=pl.CostEstimate(
            flops=2 * n_rows * depth * rest_cols,
            bytes_accessed=2 * depth * (rest_cols + n_rows),
            transcendentals=0,
        ),
        name="project_rest",
    )(lhs, pick, first_terms[1], narrow, operands[5])
    first_terms = exchange(first_terms, range(2, pool))
    rest_terms = list(rest_terms)
    early, late = range(2, pool), range(3, pool)
    got, tied = lax.optimization_barrier(
        ([first_terms[k] for k in early], [rest_terms[k] for k in late])
    )
    for k, part in zip(early, got):
        first_terms[k] = part
    for k, part in zip(late, tied):
        rest_terms[k] = part
    rest_terms = exchange(rest_terms, range(1, pool))
    terms = [first_terms[0], rest_terms[0], *rest_terms[2:], *first_terms[2:], rest_terms[1]]

    half = HD // 2
    freq = THETA ** (-(np.arange(half) * 2.0) / HD)
    angles = positions * np.concatenate([freq, freq]).astype(np.float32)[None, :]
    sign = np.concatenate([-np.ones(half), np.ones(half)]).astype(np.float32)[None, :]
    cosines, sines = jnp.cos(angles), jnp.sin(angles) * sign

    found = pl.pallas_call(
        functools.partial(attend_kernel, pool, slots, seg, width_d, q_heads, kv_heads),
        out_shape=[jax.ShapeDtypeStruct((slots * q_heads + LEVELS, HD), jnp.bfloat16)] * pool,
        in_specs=[SMEM] + [VMEM] * (2 * pool + 4),
        out_specs=[VMEM] * pool,
        scratch_shapes=[pltpu.VMEM((q_heads * per, HD), jnp.float32)],
        compiler_params=pltpu.CompilerParams(vmem_limit_bytes=24 * 2**20),
        name="attend",
    )(me[None], *terms, cosines, sines, marks, cache_keys, cache_values)

    found = exchange(found, [*range(2, pool), 1])

    return pl.pallas_call(
        functools.partial(merge_kernel, pool, slots, rows_local, q_heads, kv_heads),
        out_shape=jax.ShapeDtypeStruct((rows_local, q_cols), jnp.bfloat16),
        in_specs=[VMEM] * (2 + pool),
        out_specs=HBM,
        scratch_shapes=[
            pltpu.VMEM((rows_local, q_cols), jnp.bfloat16),
            pltpu.VMEM((per * q_heads, HD), jnp.float32),
            pltpu.SemaphoreType.DMA((4,)),
        ],
        compiler_params=pltpu.CompilerParams(vmem_limit_bytes=24 * 2**20),
        name="merge",
    )(home_slots, home_rows, found[0], *found[2:], found[1])


def solution(mesh):
    return jax.shard_map(
        body,
        mesh=mesh,
        in_specs=(
            P("groups", "pool"),
            P("pool"),
            P("pool", "tensor"),
            P("pool", "tensor"),
            P("pool", "tensor"),
            P(("groups", "pool"), "tensor"),
            P(("groups", "pool"), "tensor"),
            P("groups", None, None),
            P(("groups", "pool"), None, None),
            P("groups"),
        ),
        out_specs=P(("groups", "pool"), "tensor"),
        check_vma=False,
    )
```

```python
import functools

import jax
import jax.numpy as jnp
import numpy as np
from jax import lax
from jax.experimental import pallas as pl
from jax.experimental.pallas import tpu as pltpu
from jax.sharding import PartitionSpec as P

HD = 128
EPS = 1e-05
THETA = 500000.0
LOW = -1e30
DEEP = 512
LEVELS = 16
TILE = 3072


def divides(width, limit):
    while width % limit:
        limit //= 2
    return limit


def widest(width, limit):
    return max(tile for tile in range(128, limit + 1, 128) if width % tile == 0)


def split3(x):
    a = x.astype(jnp.bfloat16).astype(jnp.float32)
    r = x - a
    b = r.astype(jnp.bfloat16).astype(jnp.float32)
    return a, b, (r - b).astype(jnp.bfloat16).astype(jnp.float32)


def partner(me, k):
    return lax.bitwise_xor(me, k)


def stream(count, pieces, following, ahead):
    def begin():
        for t in range(min(ahead, count)):
            for copy in pieces(t):
                copy.start()
        for copy in following[: max(ahead - count, 0)]:
            copy.start()

    def advance(t):
        @pl.when(t + ahead < count)
        def _():
            for copy in pieces(t + ahead):
                copy.start()

        for j, copy in enumerate(following):
            pl.when(t + ahead == count + j)(copy.start)

    return begin, advance


def add_products(left, block, sums):
    width = block.shape[1]
    tile = widest(width, TILE)
    for at in range(0, width, tile):
        sums[:, at : at + tile] += jnp.dot(
            left, block[:, at : at + tile], preferred_element_type=jnp.float32
        )


def spread(chosen, sums, outs, at):
    width = sums.shape[1]
    per = chosen.shape[0] // len(outs)
    rows = jnp.dot(
        chosen, sums.astype(jnp.bfloat16), preferred_element_type=jnp.float32
    ).astype(jnp.bfloat16)
    for k, out in enumerate(outs):
        out[:, at : at + width] = rows[k * per : (k + 1) * per]


def spread_products(chosen, left, block, sums, outs, to):
    width = block.shape[1]
    tile = widest(width, TILE)
    for at in range(0, width, tile):
        done = sums[:, at : at + tile] + jnp.dot(
            left, block[:, at : at + tile], preferred_element_type=jnp.float32
        )
        spread(chosen, done, outs, to + at)


def project_kernel(pool, slots, rows_local, me_ref, send, lens, row_len, hidden, gain, *rest):
    w_query, w_key, w_value, *rest = rest
    outs, rest = rest[:pool], rest[pool:]
    lhs, pick, positions, marks, home_rows, home_slots, narrow, *rest = rest
    send_buf, lens_buf, row_len_buf, x_buf, g_buf, *rest = rest
    query_buf, sums, squares, in_sem, sems = rest
    per = pool * slots
    n_rows, depth = x_buf.shape
    count, deep, width = query_buf.shape
    me = me_ref[0]

    def named(home, owner, c):
        if len(send_buf.shape) == 3:
            return send_buf[home, owner, c]
        return send_buf[home * per + owner * slots + c]

    lane = lax.broadcasted_iota(jnp.int32, (1, n_rows), 1)
    place = lax.broadcasted_iota(jnp.int32, (1, HD), 1)
    group = marks.shape[1] // per
    slot_of = lax.broadcasted_iota(jnp.int32, (1, marks.shape[1]), 1) // group

    def choose(i):
        owner = partner(me, i // per)
        s = lax.rem(i, per)
        home = partner(owner, s // slots)
        r = named(home, owner, lax.rem(s, slots))
        row = jnp.where(r >= 0, home * rows_local + r, -1)
        pick[pl.ds(i, 1), :] = (lane == row).astype(jnp.float32)

    def describe(s):
        k, c = s // slots, lax.rem(s, slots)
        home = partner(me, k)
        r = named(home, me, c)
        at = row_len_buf[home * rows_local + jnp.maximum(r, 0)].astype(jnp.float32)
        positions[pl.ds(s, 1), :] = jnp.full((1, HD), at, jnp.float32)
        length = lens_buf[0, home, c] if len(lens_buf.shape) == 3 else lens_buf[home * slots + c]
        earlier = jnp.int32(0)
        for e in range(per):
            same = (named(home, e // slots, e % slots) == r) & (e < me * slots + c)
            earlier = earlier | same.astype(jnp.int32)
        first = jnp.where((earlier == 0) & (r >= 0), 1, 0)
        marks[0:1, :] = jnp.where(slot_of == s, length, marks[0:1, :])
        marks[1:2, :] = jnp.where(slot_of == s, first, marks[1:2, :])
        mine = named(me, home, c)
        home_slots[...] = jnp.where(lax.rem(place, per) == s, mine, home_slots[...])
        home_rows[pl.ds(k, 1), :] = jnp.where(
            lax.rem(place // group, slots) == c, mine, home_rows[pl.ds(k, 1), :]
        )

    chore_steps = 4
    spread_chores = count > chore_steps + 1 and pool * per <= 64 and per % chore_steps == 0

    def each(do, total, t):
        share = -(-total // chore_steps)
        if spread_chores:
            for q in range(share):
                do(t * share + q)
        else:
            assert isinstance(t, int)
            pl.loop(0, total)(do)

    def scale(t):
        at = pl.multiple_of(t * deep, deep)
        x = x_buf[:, pl.ds(at, deep)].astype(jnp.float32)
        gains = g_buf[pl.ds(at, deep)].astype(jnp.float32).reshape(1, deep)
        left = (x * gains).astype(jnp.bfloat16)
        lhs[:, pl.ds(at, deep)] = left
        squared = x * x
        total = squares[...]
        for column in range(0, deep, HD):
            total = total + squared[:, column : column + HD]
        squares[...] = total
        return left

    kv_cols = w_key.shape[1]
    cuts = [0, deep // 4, deep // 2, deep] if count > 1 else [0, deep]

    def pieces(t):
        if isinstance(t, int) and t == 0:
            return [
                pltpu.make_async_copy(
                    w_query.at[a:b, :width], query_buf.at[0, a:b], sems.at[0 if n == 0 else count + n]
                )
                for n, (a, b) in enumerate(zip(cuts[:-1], cuts[1:]))
            ]
        rows = pl.ds(pl.multiple_of(t * deep, deep), deep)
        return [pltpu.make_async_copy(w_query.at[rows, :width], query_buf.at[t], sems.at[t])]

    following = [
        pltpu.make_async_copy(w, target, in_sem.at[5 + n])
        for n, (w, target) in enumerate(
            ((w_key, narrow.at[:, :kv_cols]), (w_value, narrow.at[:, kv_cols:]))
        )
    ]
    begin, advance = stream(count, pieces, following, 3)

    def use(t):
        advance(t)
        left = scale(t)
        for copy in pieces(t):
            copy.wait()
        add_products(left, query_buf.at[t], sums)

    def use_early(t):
        use(t)
        each(choose, pool * per, t - 1)
        each(describe, per, t - 1)

    def use_first():
        advance(0)
        left = scale(0)
        for copy, a, b in zip(pieces(0), cuts[:-1], cuts[1:]):
            copy.wait()
            add_products(left[:, a:b], query_buf.at[0, a:b], sums)

    def use_last(t):
        left = scale(t)
        for copy in pieces(t):
            copy.wait()
        chosen = pick[...].astype(jnp.bfloat16)
        spread_products(chosen, left, query_buf.at[t], sums, outs, 0)
        power = jnp.sum(squares[...], axis=1, keepdims=True)
        at = lax.broadcasted_iota(jnp.int32, (n_rows, HD), 1)
        a, b, c = split3(power)
        parts = jnp.where(at == 0, a, jnp.where(at == 1, b, jnp.where(at == 2, c, 0.0)))
        spread(chosen, parts, outs, sums.shape[1])

    inputs = [
        pltpu.make_async_copy(source, target, in_sem.at[i])
        for i, (source, target) in enumerate(
            (
                (gain, g_buf),
                (hidden, x_buf),
                (send, send_buf),
                (lens, lens_buf),
                (row_len, row_len_buf),
            )
        )
    ]
    for one in inputs:
        one.start()
    begin()
    sums[...] = jnp.zeros(sums.shape, jnp.float32)
    squares[...] = jnp.zeros((n_rows, HD), jnp.float32)
    marks[...] = jnp.zeros(marks.shape, jnp.int32)
    home_rows[...] = jnp.full(home_rows.shape, -1, jnp.int32)
    home_slots[...] = jnp.full(home_slots.shape, -1, jnp.int32)
    for one in inputs:
        one.wait()
    if not spread_chores:
        each(choose, pool * per, 0)
        each(describe, per, 0)
    if count > 1:
        use_first()
    early = 1 + chore_steps if spread_chores else 1
    if spread_chores:
        pl.loop(1, early)(use_early)
    if count > early + 1:
        pl.loop(early, count - 1)(use)
    use_last(count - 1)
    for copy in following:
        copy.wait()


def project_rest_kernel(pool, column, lhs, pick, near, narrow, w_query, *rest):
    outs, (query_buf, sums, sems) = rest[:pool], rest[pool:]
    done = near.shape[1]
    count, deep, _ = query_buf.shape
    chosen = pick[...].astype(jnp.bfloat16)
    targets = [out.at[:, done:] if k == 1 else out for k, out in enumerate(outs)]

    def pieces(t):
        rows = pl.ds(pl.multiple_of(t * deep, deep), deep)
        block = w_query.at[rows, column : column + query_buf.shape[2]]
        return [pltpu.make_async_copy(block, query_buf.at[t], sems.at[t])]

    begin, _ = stream(count, pieces, [], count)
    begin()
    sums[...] = jnp.zeros(sums.shape, jnp.float32)
    outs[1][:, :done] = near[...]
    part = jnp.dot(lhs[...], narrow[...], preferred_element_type=jnp.float32)
    spread(chosen, part, targets, 0)

    @pl.loop(0, count - 1)
    def _(t):
        pieces(t)[0].wait()
        add_products(lhs[:, pl.ds(pl.multiple_of(t * deep, deep), deep)], query_buf.at[t], sums)

    pieces(count - 1)[0].wait()
    left = lhs[:, (count - 1) * deep :]
    spread_products(chosen, left, query_buf.at[count - 1], sums, targets, narrow.shape[1])


def attend_kernel(pool, slots, seg, width_d, q_heads, kv_heads, me_ref, *rest):
    terms, rest = rest[: 2 * pool - 1], rest[2 * pool - 1 :]
    cos, sin, marks, keys, values = rest[:5]
    outs, (q_buf,) = rest[5 : 5 + pool], rest[5 + pool :]
    per = pool * slots
    group = q_heads // kv_heads
    step = HD // group
    scale = HD ** (-0.5)

    own, own_rest, near = terms[0], terms[1], terms[-1]
    far_rest, far = terms[2:pool], terms[pool:-1]
    first_cols, cols = own.shape[1], near.shape[1]

    def total(at):
        if at < first_cols:
            got, others = own[:, at : at + HD], far
        else:
            got, others = own_rest[:, at - first_cols : at - first_cols + HD], far_rest
        got = got.astype(jnp.float32) + near[:, at : at + HD].astype(jnp.float32)
        at = at if at < first_cols else at - first_cols
        for part in others:
            got = got + part[:, at : at + HD].astype(jnp.float32)
        return got

    late = first_cols + 2 * kv_heads * HD
    heads = [*range(0, first_cols - HD, HD), *range(late, cols, HD)]
    power = jnp.sum(total(first_cols - HD), axis=1, keepdims=True)
    factor = lax.rsqrt(power * (1.0 / width_d) + EPS)
    cosines, sines = cos[...], sin[...]

    def rounded(x):
        return x.astype(jnp.bfloat16).astype(jnp.float32)

    def rotated(x):
        return rounded(x * cosines + pltpu.roll(x, HD // 2, axis=1) * sines)

    for i in range(q_heads):
        q_buf[i * per : (i + 1) * per, :] = rotated(total(heads[i]) * factor)
    keys_own = [rotated(total(first_cols + g * HD) * factor) for g in range(kv_heads)]
    values_own = [
        rounded(total(first_cols + (kv_heads + g) * HD) * factor) for g in range(kv_heads)
    ]

    me = me_ref[0]

    def base(j):
        return pl.multiple_of(partner(me, j) * (slots * seg), slots * seg)

    lane = lax.broadcasted_iota(jnp.int32, (1, HD), 1)
    slot_of = lane // group
    at = lax.broadcasted_iota(jnp.int32, (seg, HD), 0)
    at_own = lax.broadcasted_iota(jnp.int32, (step, HD), 0)
    blocks = [(g, s) for s in range(0, per, step) for g in range(kv_heads)]
    columns = []
    for g, s in blocks:
        query = jnp.concatenate(
            [q_buf[pl.ds(g * group * per + s + u, group, stride=per), :] for u in range(step)], 0
        )
        columns.append(query.T.astype(jnp.bfloat16))
    scores = []
    for (g, s), query in zip(blocks, columns):
        score = None
        for u in range(0, step, slots):
            wide = jnp.dot(
                keys[pl.ds(base((s + u) // slots), slots * seg), g * HD : (g + 1) * HD],
                query,
                preferred_element_type=jnp.float32,
            )
            for c in range(slots):
                each = wide[c * seg : (c + 1) * seg]
                score = each if score is None else jnp.where(slot_of == u + c, each, score)
        own = jnp.dot(
            keys_own[g][s : s + step].astype(jnp.bfloat16),
            query,
            preferred_element_type=jnp.float32,
        )
        own = jnp.sum(jnp.where(at_own == slot_of, own, 0.0), axis=0, keepdims=True)
        scores.append((score * scale, own * scale))
    turned, levels = [], {}
    for (g, s), (score, own) in zip(blocks, scores):
        length = marks[0:1, s * group : s * group + HD]
        with_own = marks[1:2, s * group : s * group + HD] > 0
        usable = at < length
        own = jnp.where(with_own, own, LOW)
        top = jnp.maximum(jnp.max(jnp.where(usable, score, LOW), axis=0, keepdims=True), own)
        weight = jnp.where(usable, jnp.exp(score - top), 0.0)
        weight_own = jnp.where(with_own, jnp.exp(own - top), 0.0)
        sums = jnp.sum(weight, axis=0, keepdims=True) + weight_own
        sums = jnp.where(length > 0, sums, 1.0)
        level = top + jnp.log(sums)
        for u in range(0, step, slots):
            at_lane = g * slots * group
            moved = level if at_lane == u * group else pltpu.roll(level, (at_lane - u * group) % HD, axis=1)
            there = (lane >= at_lane) & (lane < at_lane + slots * group)
            home = (s + u) // slots
            levels[home] = jnp.where(there, moved, levels.get(home, 0.0))
        rows = [weight_own, 1.0 / sums, jnp.zeros((HD - seg - 2, HD), jnp.float32)]
        turned.append(jnp.concatenate([weight] + rows, 0).T)
    for (g, s), block in zip(blocks, turned):
        for u in range(step):
            home, c = (s + u) // slots, (s + u) % slots
            rows = block[u * group : (u + 1) * group]
            mixed = jnp.dot(
                rows[:, :seg].astype(jnp.bfloat16),
                values[pl.ds(base(home) + c * seg, seg), g * HD : (g + 1) * HD],
                preferred_element_type=jnp.float32,
            )
            mixed = mixed + rows[:, seg : seg + 1] * values_own[g][s + u : s + u + 1]
            to = c * q_heads + g * group
            outs[home][to : to + group, :] = (mixed * rows[:, seg + 1 : seg + 2]).astype(jnp.bfloat16)
    for home, level in levels.items():
        block = jnp.concatenate([*split3(level), jnp.zeros((LEVELS - 3, HD), jnp.float32)], 0)
        outs[home][slots * q_heads :, :] = block.astype(jnp.bfloat16)


def merge_kernel(pool, slots, rows_local, q_heads, kv_heads, slots_ref, rows_ref, own, *rest):
    found, (out, buf, scaled, sems) = [own, rest[pool - 2], *rest[: pool - 2]], rest[pool - 1 :]
    per = pool * slots
    group = q_heads // kv_heads
    block = slots * q_heads
    span = slots * group
    level = jnp.concatenate(
        [jnp.sum(part[block : block + LEVELS, :].astype(jnp.float32), 0, keepdims=True) for part in found], 0
    )
    named = rows_ref[...]
    lane = lax.broadcasted_iota(jnp.int32, (pool, HD), 1)

    def turns(x):
        for c in range(slots):
            y = x
            if c:
                y = jnp.where(
                    lax.rem(lane, span) < span - c * group,
                    pltpu.roll(x, HD - c * group, axis=1),
                    pltpu.roll(x, span - c * group, axis=1),
                )
            for k in range(pool):
                yield jnp.concatenate([y[k:], y[:k]], 0) if k else y

    same = [other == named for other in turns(named)]
    top = level
    for match, other in zip(same, turns(level)):
        top = jnp.maximum(top, jnp.where(match, other, LOW))
    weight = jnp.exp(level - top)
    total = jnp.zeros_like(weight)
    for match, other in zip(same, turns(weight)):
        total = total + jnp.where(match, other, 0.0)
    share = jnp.where(named >= 0, weight / total, 0.0)
    share = jnp.concatenate([share, jnp.zeros((HD - pool, HD), jnp.float32)], 0).T
    for k in range(pool):
        for c in range(slots):
            for g in range(kv_heads):
                at = c * q_heads + g * group
                each = g * span + c * group
                scaled[k * block + at : k * block + at + group, :] = (
                    found[k][at : at + group, :].astype(jnp.float32)
                    * share[each : each + group, k : k + 1]
                )
    row = lax.broadcasted_iota(jnp.int32, (rows_local, 2 * per), 0)
    match = (slots_ref[:, : 2 * per] == row).astype(jnp.float32).astype(jnp.bfloat16)
    quarter = q_heads // 4
    copies = [
        pltpu.make_async_copy(buf.at[:, columns], out.at[:, columns], sems.at[n])
        for n, columns in enumerate(pl.ds(n * quarter * HD, quarter * HD) for n in range(4))
    ]
    for i in range(q_heads):
        part = scaled[pl.ds(i, per, stride=q_heads), :]
        high = part.astype(jnp.bfloat16)
        low = (part - high.astype(jnp.float32)).astype(jnp.bfloat16)
        buf[:, i * HD : (i + 1) * HD] = jnp.dot(
            match, jnp.concatenate([high, low], 0), preferred_element_type=jnp.float32
        ).astype(jnp.bfloat16)
        if (i + 1) % quarter == 0:
            copies[i // quarter].start()
    for copy in copies:
        copy.wait()


def exchange(parts, order):
    got = list(parts)
    for k in order:
        got[k] = lax.ppermute(parts[k], "pool", [(i, i ^ k) for i in range(len(parts))])
    return got


def in_hbm(x):
    return pltpu.with_memory_space_constraint(x, pltpu.HBM)


SMEM = pl.BlockSpec(memory_space=pltpu.SMEM)
VMEM = pl.BlockSpec(memory_space=pltpu.VMEM)
HBM = pl.BlockSpec(memory_space=pltpu.HBM)


def body(
    hidden_in,
    norm_gain,
    w_query,
    w_key,
    w_value,
    cache_keys,
    cache_values,
    send_row,
    piece_len,
    row_len,
):
    pool = lax.axis_size("pool")
    me = lax.axis_index("pool").astype(jnp.int32)
    n_rows, depth = hidden_in.shape
    width_d = depth * pool
    rows_local = n_rows // pool
    slots = send_row.shape[2]
    per = pool * slots
    seg = cache_keys.shape[0] // per
    q_cols, kv_cols = w_query.shape[1], w_key.shape[1]
    q_heads, kv_heads = q_cols // HD, kv_cols // HD
    group = q_heads // kv_heads
    cols = q_cols + 2 * kv_cols + HD

    if pool <= 8:
        indices = [send_row, piece_len, row_len]
    else:
        indices = [send_row.reshape(-1), piece_len.reshape(-1), row_len]
    deep = divides(depth, DEEP)
    count = depth // deep
    widths = [11 * q_cols // 16, 5 * q_cols // 16]


    def parts(width):
        return [jax.ShapeDtypeStruct((per, width), jnp.bfloat16)] * pool

    operands = [in_hbm(x) for x in (*indices, hidden_in, norm_gain, w_query, w_key, w_value)]
    *first_terms, lhs, pick, positions, marks, home_rows, home_slots, narrow = pl.pallas_call(
        functools.partial(project_kernel, pool, slots, rows_local),
        out_shape=[
            *parts(widths[0] + HD),
            jax.ShapeDtypeStruct((n_rows, depth), jnp.bfloat16),
            jax.ShapeDtypeStruct((pool * per, n_rows), jnp.float32),
            jax.ShapeDtypeStruct((per, HD), jnp.float32),
            jax.ShapeDtypeStruct((2, per * group), jnp.int32),
            jax.ShapeDtypeStruct((pool, HD), jnp.int32),
            jax.ShapeDtypeStruct((1, HD), jnp.int32),
            jax.ShapeDtypeStruct((depth, 2 * kv_cols), jnp.bfloat16),
        ],
        in_specs=[SMEM] + [HBM] * 8,
        out_specs=[VMEM] * (pool + 7),
        scratch_shapes=[
            *(pltpu.SMEM(x.shape, jnp.int32) for x in indices),
            pltpu.VMEM((n_rows, depth), jnp.bfloat16),
            pltpu.VMEM((depth,), jnp.bfloat16),
            pltpu.VMEM((count, deep, widths[0]), jnp.bfloat16),
            pltpu.VMEM((n_rows, widths[0]), jnp.float32),
            pltpu.VMEM((n_rows, HD), jnp.float32),
            pltpu.SemaphoreType.DMA((7,)),
            pltpu.SemaphoreType.DMA((count + 3,)),
        ],
        compiler_params=pltpu.CompilerParams(vmem_limit_bytes=46 * 2**20),
        name="project",
    )(me[None], *operands)
    rest_cols = 2 * kv_cols + widths[1]
    rest_shapes = parts(rest_cols)
    rest_shapes[1] = jax.ShapeDtypeStruct((per, widths[0] + HD + rest_cols), jnp.bfloat16)
    rest_terms = pl.pallas_call(
        functools.partial(project_rest_kernel, pool, widths[0]),
        out_shape=rest_shapes,
        in_specs=[VMEM] * 4 + [HBM],
        out_specs=[VMEM] * pool,
        scratch_shapes=[
            pltpu.VMEM((count, deep, widths[1]), jnp.bfloat16),
            pltpu.VMEM((n_rows, widths[1]), jnp.float32),
            pltpu.SemaphoreType.DMA((count,)),
        ],
        compiler_params=pltpu.CompilerParams(vmem_limit_bytes=40 * 2**20),
        cost_estimate=pl.CostEstimate(
            flops=2 * n_rows * depth * rest_cols,
            bytes_accessed=2 * depth * (rest_cols + n_rows),
            transcendentals=0,
        ),
        name="project_rest",
    )(lhs, pick, first_terms[1], narrow, operands[5])
    first_terms = exchange(first_terms, range(2, pool))
    rest_terms = list(rest_terms)
    early, late = range(2, pool), range(3, pool)
    got, tied = lax.optimization_barrier(
        ([first_terms[k] for k in early], [rest_terms[k] for k in late])
    )
    for k, part in zip(early, got):
        first_terms[k] = part
    for k, part in zip(late, tied):
        rest_terms[k] = part
    rest_terms = exchange(rest_terms, range(1, pool))
    terms = [first_terms[0], rest_terms[0], *rest_terms[2:], *first_terms[2:], rest_terms[1]]

    half = HD // 2
    freq = THETA ** (-(np.arange(half) * 2.0) / HD)
    angles = positions * np.concatenate([freq, freq]).astype(np.float32)[None, :]
    sign = np.concatenate([-np.ones(half), np.ones(half)]).astype(np.float32)[None, :]
    cosines, sines = jnp.cos(angles), jnp.sin(angles) * sign

    found = pl.pallas_call(
        functools.partial(attend_kernel, pool, slots, seg, width_d, q_heads, kv_heads),
        out_shape=[jax.ShapeDtypeStruct((slots * q_heads + LEVELS, HD), jnp.bfloat16)] * pool,
        in_specs=[SMEM] + [VMEM] * (2 * pool + 4),
        out_specs=[VMEM] * pool,
        scratch_shapes=[pltpu.VMEM((q_heads * per, HD), jnp.float32)],
        compiler_params=pltpu.CompilerParams(vmem_limit_bytes=24 * 2**20),
        name="attend",
    )(me[None], *terms, cosines, sines, marks, cache_keys, cache_values)

    found = exchange(found, [*range(2, pool), 1])

    return pl.pallas_call(
        functools.partial(merge_kernel, pool, slots, rows_local, q_heads, kv_heads),
        out_shape=jax.ShapeDtypeStruct((rows_local, q_cols), jnp.bfloat16),
        in_specs=[VMEM] * (2 + pool),
        out_specs=HBM,
        scratch_shapes=[
            pltpu.VMEM((rows_local, q_cols), jnp.bfloat16),
            pltpu.VMEM((per * q_heads, HD), jnp.float32),
            pltpu.SemaphoreType.DMA((4,)),
        ],
        compiler_params=pltpu.CompilerParams(vmem_limit_bytes=24 * 2**20),
        name="merge",
    )(home_slots, home_rows, found[0], *found[2:], found[1])


def solution(mesh):
    return jax.shard_map(
        body,
        mesh=mesh,
        in_specs=(
            P("groups", "pool"),
            P("pool"),
            P("pool", "tensor"),
            P("pool", "tensor"),
            P("pool", "tensor"),
            P(("groups", "pool"), "tensor"),
            P(("groups", "pool"), "tensor"),
            P("groups", None, None),
            P(("groups", "pool"), None, None),
            P("groups"),
        ),
        out_specs=P(("groups", "pool"), "tensor"),
        check_vma=False,
    )
```
